256 devices in a mesh: dp: 64 (over z, x_lo, y), mp: 4 (over x_hi, core).
Axes of the slice: x: 4 (x_hi: 2, x_lo: 2; x = x_hi * 2 + x_lo), y: 4, z: 8, core: 2. Of those that a mesh axis runs over, the one named last changes fastest.
Arguments:
- image_feats: bfloat16 [14336, 1152], P('dp'), may hold values from -6 to 6
- text_feats: bfloat16 [14336, 1152], P('dp'), may hold values from -6 to 6
- image_proj: bfloat16 [1152, 1152], P(None, 'mp'), may hold values from -0.1875 to 0.1875
- text_proj: bfloat16 [1152, 1152], P(None, 'mp'), may hold values from -0.1875 to 0.1875
- log_temp: float32 [1], replicated, may hold values from 1 to 2.3
- bias: float32 [1], replicated, may hold values from -4 to -1
Outputs:
- image_proj_grad: float32 [1152, 1152], P('dp', 'mp')
- text_proj_grad: float32 [1152, 1152], P('dp', 'mp')
The draws below stay inside these ranges and needn't reach their ends.
All inputs are finite; a program needn't handle non-finite values.
Results may differ from the reference program's by a relative error of at most 0.004.
Values may be sent and summed in bfloat16 or wider, within the bound.
A program may use at most 64 MiB of HBM per device.

```python
import jax
import jax.numpy as jnp
from jax import lax

DI = 1152
DT = 1152
E = 1152
B_DEV = 224
B = 14336


def block_scale(own_key, dims, pieces, smallest, top_value):
    level, own = 1.0, jax.random.fold_in(own_key, 6)
    for position, blocks in pieces:
        steps = jnp.exp(jax.random.uniform(jax.random.fold_in(own, position), (blocks,), jnp.float32, smallest / len(pieces), top_value / len(pieces)))
        level = level * jnp.repeat(steps, dims[position] // blocks).reshape([-1 if axis == position else 1 for axis in range(len(dims))])
    return level


def scatter_about(own_key, dims, spread, bound, split=(), dtype=jnp.bfloat16):
    result = spread * jax.random.normal(own_key, dims, jnp.float32)
    if split:
        result = result * block_scale(own_key, dims, split, -0.22, 0.18)
    return jnp.clip(result, -bound, bound).astype(dtype)


def setup_inputs(seed: int = 0) -> dict:
    splits = jax.random.split(jax.random.key(seed), 7)
    return {
        "image_feats": scatter_about(splits[0], (B, DI), 1.0, 6.0, ((0, 64),)),
        "text_feats": scatter_about(splits[1], (B, DT), 1.0, 6.0, ((0, 64),)),
        "image_proj": scatter_about(splits[2], (DI, E), DI ** -0.5, 0.1875, ((1, 4),)),
        "text_proj": scatter_about(splits[3], (DT, E), DT ** -0.5, 0.1875, ((1, 4),)),
        "log_temp": jnp.clip(jax.random.uniform(splits[4], (1,), jnp.float32, 1.0, 2.3), 1.0, 2.3),
        "bias": jnp.clip(jax.random.uniform(splits[5], (1,), jnp.float32, -4.0, -1.0), -4.0, -1.0),
    }


def unit_rows(emb):
    wide = emb.astype(jnp.float32)
    scale = lax.rsqrt(lax.optimization_barrier(jnp.sum(wide * wide, axis=1, keepdims=True)) + 1e-06)
    return (wide * scale, scale)

def unit_back(unit, scale, upstream):
    inner = lax.optimization_barrier(jnp.sum(unit * upstream, axis=1, keepdims=True))
    return (scale * (upstream - unit * inner)).astype(jnp.bfloat16)

def reference(image_feats, text_feats, image_proj, text_proj, log_temp, bias):
    image_emb = jnp.dot(image_feats, image_proj, preferred_element_type=jnp.float32).astype(jnp.bfloat16)
    text_emb = jnp.dot(text_feats, text_proj, preferred_element_type=jnp.float32).astype(jnp.bfloat16)
    image_unit, image_scale = unit_rows(image_emb)
    text_unit, text_scale = unit_rows(text_emb)
    image_x = image_unit.astype(jnp.bfloat16)
    text_x = text_unit.astype(jnp.bfloat16)
    total = image_x.shape[0]
    width = image_x.shape[1]
    temp = jnp.exp(log_temp[0])
    shift = bias[0]
    blocks = total // B_DEV
    columns = jnp.arange(total).astype(jnp.int32)

    def step(text_dx, block):
        start = (block * B_DEV).astype(jnp.int32)
        rows_x = lax.dynamic_slice_in_dim(image_x, start, B_DEV, 0)
        dots = jnp.dot(rows_x, text_x.T, preferred_element_type=jnp.float32)
        logits = temp * dots + shift
        row_ids = start + jnp.arange(B_DEV).astype(jnp.int32)
        sign = jnp.where(row_ids[:, None] == columns[None, :], jnp.float32(1.0), jnp.float32(-1.0))
        grad = -sign * jax.nn.sigmoid(-sign * logits) / total
        scaled = (temp * grad).astype(jnp.bfloat16)
        image_dx = jnp.dot(scaled, text_x, preferred_element_type=jnp.float32)
        text_dx = text_dx + jnp.dot(scaled.T, rows_x, preferred_element_type=jnp.float32)
        return (text_dx, image_dx)
    init = jnp.zeros((total, width), jnp.float32)
    text_dx, image_dx = lax.scan(step, init, jnp.arange(blocks).astype(jnp.int32))
    image_dx = image_dx.reshape(total, width)
    image_dz = unit_back(image_unit, image_scale, image_dx)
    text_dz = unit_back(text_unit, text_scale, text_dx)
    image_proj_grad = jnp.dot(image_feats.T, image_dz, preferred_element_type=jnp.float32)
    text_proj_grad = jnp.dot(text_feats.T, text_dz, preferred_element_type=jnp.float32)
    return (image_proj_grad, text_proj_grad)
```

```python
import functools

import jax
import jax.numpy as jnp
from jax import lax
from jax.experimental import pallas as pl
from jax.experimental.pallas import tpu as pltpu
from jax.sharding import PartitionSpec as P

MESH = pl.DeviceIdType.MESH
F32, BF = jnp.float32, jnp.bfloat16
PIECE = 64
POS = {4: 0, 0: 1, 3: 2, 5: 3, 2: 4, 6: 5, 1: 6, 7: 7}


def dot(a, b):
    return jnp.dot(a, b, preferred_element_type=F32)


def dot_nt(a, b):
    return lax.dot_general(a, b, (((1,), (1,)), ((), ())), preferred_element_type=F32)


def dot_tn(a, b):
    return lax.dot_general(a, b, (((0,), (0,)), ((), ())), preferred_element_type=F32)


def kernel(total, fi_hbm, ft_hbm, wi_hbm, wt_hbm, lt_ref, bs_ref, oi_ref, ot_ref,
           feats, wts, featst, es, er, unit, scal, img, txt, dacc, prob, gi, gt,
           gib, r4a, r3a, r2a, r1a, r4b, r3b, r2b, r1b, sa, sb,
           sibr, gtb, tp4, tpr, tmr, zs, zr, fin, fst, fr, fx, ys, yr,
           lsem, ssem, rsem):
    dp, mp = lax.axis_index("dp"), lax.axis_index("mp")
    z, xl, y = dp // 8, (dp // 4) % 2, dp % 4
    c = mp % 2
    x = (mp // 2) * 2 + xl

    def dev(xx, yy, zz, cc):
        return (zz * 8 + (xx % 2) * 4 + yy, (xx // 2) * 2 + cc)

    xp, xm = dev((x + 1) % 4, y, z, c), dev((x + 3) % 4, y, z, c)
    yp, ym = dev(x, (y + 1) % 4, z, c), dev(x, (y + 3) % 4, z, c)
    zp, zm = dev(x, y, (z + 1) % 8, c), dev(x, y, (z + 7) % 8, c)
    y2 = dev(x, (y + 2) % 4, z, c)
    xo = (z * 8 + (1 - xl) * 4 + y, mp)
    sib = (dp, (mp // 2) * 2 + (1 - c))
    mps = [(dp, (mp + k) % 4) for k in (1, 2, 3)]

    barrier = pltpu.get_barrier_semaphore()
    greeted = mps + [xp, xm, yp, ym, zp, zm, y2]
    for d in greeted:
        pl.semaphore_signal(barrier, inc=1, device_id=d, device_id_type=MESH)

    loads = []
    for k, (s, t) in enumerate(((fi_hbm, feats.at[0, 0:224]), (wi_hbm, wts.at[0]),
                                (ft_hbm, feats.at[1, 0:224]), (wt_hbm, wts.at[1]))):
        cp = pltpu.make_async_copy(s, t, lsem.at[k])
        cp.start()
        loads.append(cp)
    feats[:, 224:256, :] = jnp.zeros((2, 32, 1152), BF)

    started = []

    def send(src, dst, to):
        k = len(started)
        cp = pltpu.make_async_remote_copy(src_ref=src, dst_ref=dst, send_sem=ssem.at[k],
                                          recv_sem=rsem.at[k], device_id=to, device_id_type=MESH)
        cp.start()
        started.append(cp)
        return cp

    place = (lax.broadcasted_iota(jnp.int32, (32, 128), 1)
             == lax.broadcasted_iota(jnp.int32, (32, 128), 0) + 32 * mp).astype(F32).astype(BF)
    emb_in = [[], []]
    for m in (0, 1):
        loads[2 * m].wait()
        loads[2 * m + 1].wait()
        main = dot(feats[m], wts[m, :, 0:256]).astype(BF)
        rest = dot(feats[m], wts[m, :, 256:288]).astype(BF)
        rest = dot(rest, place).astype(BF)
        for q in range(4):
            es[m, q, :, 0:256] = main[64 * q:64 * q + 64]
            es[m, q, :, 256:384] = rest[64 * q:64 * q + 64]
        if m == 0:
            pl.semaphore_wait(barrier, len(greeted))
        for k in (1, 2, 3):
            emb_in[m].append(send(es.at[m, (mp + k) % 4], er.at[m, mp], mps[k - 1]))
        er[m, mp] = es[m, mp]

    def normalize(m):
        for cp in emb_in[m]:
            cp.wait_recv()
        rest = sum(er[m, q, :, 256:384].astype(F32) for q in range(4))
        wide = jnp.concatenate([er[m, q, :, 0:256].astype(F32) for q in range(4)] + [rest], axis=1)
        scale = lax.rsqrt(jnp.sum(wide * wide, axis=1, keepdims=True) + 1e-06)
        unit[m] = wide * scale
        scal[m] = jnp.broadcast_to(scale, (64, 128))
        return (wide * scale).astype(BF)

    A, B = pl.ds(0, 32), pl.ds(32, 32)
    A0, A1, B0, B1 = pl.ds(0, 16), pl.ds(16, 16), pl.ds(32, 16), pl.ds(48, 16)
    got = {}
    img[0, 0] = normalize(0)
    got["A03"] = send(img.at[0, 0, A], img.at[0, 3, A], xp)
    got["A01"] = send(img.at[0, 0, A], img.at[0, 1, A], xm)
    got["B30"] = send(img.at[0, 0, B], img.at[3, 0, B], yp)
    got["B10"] = send(img.at[0, 0, B], img.at[1, 0, B], ym)
    got["A30"] = send(img.at[0, 0, A], img.at[3, 0, A], yp)
    got["A10"] = send(img.at[0, 0, A], img.at[1, 0, A], ym)
    got["B03"] = send(img.at[0, 0, B], img.at[0, 3, B], xp)
    got["B01"] = send(img.at[0, 0, B], img.at[0, 1, B], xm)

    txt[POS[0], 0] = normalize(1)
    tgot = {}
    sgot = []
    tgot[7] = send(txt.at[POS[0], 0], txt.at[POS[7], 0], zp)
    tgot[1] = send(txt.at[POS[0], 0], txt.at[POS[1], 0], zm)
    sgot.append(send(txt.at[POS[0], 0], txt.at[POS[0], 1], sib))

    def text_hop(k):
        for src, nxt, to, half in ((8 - k, 7 - k, zp, A), (k, k + 1, zm, B)):
            tgot[src].wait_recv()
            if k < 3:
                tgot[nxt] = send(txt.at[POS[src], 0], txt.at[POS[nxt], 0], to)
            else:
                tgot[(4, src)] = send(txt.at[POS[src], 0, half], txt.at[POS[4], 0, half], to)
            sgot.append(send(txt.at[POS[src], 0], txt.at[POS[src], 1], sib))

    got["A03"].wait_recv()
    got["A02+"] = send(img.at[0, 3, A0], img.at[0, 2, A0], xp)
    got["A01"].wait_recv()
    got["A02-"] = send(img.at[0, 1, A1], img.at[0, 2, A1], xm)
    got["B30"].wait_recv()
    got["B20+"] = send(img.at[3, 0, B0], img.at[2, 0, B0], yp)
    got["B10"].wait_recv()
    got["B20-"] = send(img.at[1, 0, B1], img.at[2, 0, B1], ym)

    def second(d):
        got["A3%d" % d] = send(img.at[0, d, A], img.at[3, d, A], yp)
        got["A1%d" % d] = send(img.at[0, d, A], img.at[1, d, A], ym)
        got["B%d3" % d] = send(img.at[d, 0, B], img.at[d, 3, B], xp)
        got["B%d1" % d] = send(img.at[d, 0, B], img.at[d, 1, B], xm)

    def third(d):
        got["A3%d" % d].wait_recv()
        got["A2%d+" % d] = send(img.at[3, d, A0], img.at[2, d, A0], yp)
        got["A1%d" % d].wait_recv()
        got["A2%d-" % d] = send(img.at[1, d, A1], img.at[2, d, A1], ym)
        got["B%d3" % d].wait_recv()
        got["B%d2+" % d] = send(img.at[d, 3, B0], img.at[d, 2, B0], xp)
        got["B%d1" % d].wait_recv()
        got["B%d2-" % d] = send(img.at[d, 1, B1], img.at[d, 2, B1], xm)

    second(1)
    second(3)
    text_hop(1)
    for k in ("A02+", "A02-", "B20+", "B20-"):
        got[k].wait_recv()
    second(2)
    third(0)
    text_hop(2)
    third(1)
    text_hop(3)
    third(3)
    tgot[(4, 5)].wait_recv()
    tgot[(4, 3)].wait_recv()
    sgot.append(send(txt.at[POS[4], 0], txt.at[POS[4], 1], sib))
    third(2)
    for m in (0, 1):
        for k in range(8):
            featst[m, k] = jnp.transpose(feats[m])[144 * k:144 * k + 144]
    for cp in sgot:
        cp.wait_recv()
    for d in range(4):
        for s in ("A2%d+", "A2%d-", "B%d2+", "B%d2-"):
            got[s % d].wait_recv()

    temp = jnp.exp(jnp.full((1, 1), lt_ref[0], F32))
    shift = jnp.full((1, 1), bs_ref[0], F32)
    gain = temp * (1.0 / total)
    text_all = txt[...].reshape(1024, 1152)

    def pairs(dy):
        dacc[...] = dot_nt(img[dy].reshape(256, 1152), text_all)

        def rows(i, _):
            at = pl.ds(pl.multiple_of(i * 16, 16), 16)
            logits = temp * dacc[at, :] + shift
            prob[pl.ds(pl.multiple_of(dy * 256 + i * 16, 16), 16), :] = (
                gain / (1.0 + jnp.exp(-logits))).astype(BF)
            return 0
        lax.fori_loop(0, 16, rows, 0, unroll=2)
        if dy == 0:
            logits = temp * dacc[0:64, 128:256] + shift
            same = (lax.broadcasted_iota(jnp.int32, (64, 128), 0)
                    == lax.broadcasted_iota(jnp.int32, (64, 128), 1))
            prob[0:64, 128:256] = jnp.where(
                same, -gain / (1.0 + jnp.exp(logits)), gain / (1.0 + jnp.exp(-logits))).astype(BF)
        gi[dy] = dot(prob[dy * 256:dy * 256 + 256, :], text_all).reshape(4, 64, 1152)

    pairs(2)
    gib[2, :, A] = gi[2, :, A].astype(BF)
    q4a = [send(gib.at[2, :, A0], r4a.at[:, A0], yp), send(gib.at[2, :, A1], r4a.at[:, A1], ym)]
    pairs(1)
    pairs(3)
    pairs(0)
    gib[:, 2, B] = gi[:, 2, B].astype(BF)
    q4b = [send(gib.at[:, 2, B0], r4b.at[:, A0], xp), send(gib.at[:, 2, B1], r4b.at[:, A1], xm)]

    def text_block(n):
        gt[2 * n:2 * n + 2] = dot_tn(prob[:, 256 * n:256 * n + 256],
                                     img[...].reshape(1024, 1152)).reshape(2, 2, 64, 1152)
        return send(gt.at[2 * n:2 * n + 2, 1], sibr.at[2 * n:2 * n + 2], sib)

    q0 = text_block(0)

    for cp in q4a:
        cp.wait_recv()
    for d in range(4):
        gib[1, d, A0] = (gi[1, d, A0] + r4a[d, A0].astype(F32)).astype(BF)
        gib[1, d, A1] = gi[1, d, A1].astype(BF)
        gib[3, d, A0] = gi[3, d, A0].astype(BF)
        gib[3, d, A1] = (gi[3, d, A1] + r4a[d, A1].astype(F32)).astype(BF)
    q3a = [send(gib.at[1, :, A], r3a.at[0], yp), send(gib.at[3, :, A], r3a.at[1], ym)]
    for cp in q4b:
        cp.wait_recv()
    for d in range(4):
        gib[d, 1, B0] = (gi[d, 1, B0] + r4b[d, A0].astype(F32)).astype(BF)
        gib[d, 1, B1] = gi[d, 1, B1].astype(BF)
        gib[d, 3, B0] = gi[d, 3, B0].astype(BF)
        gib[d, 3, B1] = (gi[d, 3, B1] + r4b[d, A1].astype(F32)).astype(BF)
    q3b = [send(gib.at[:, 1, B], r3b.at[0], xp), send(gib.at[:, 3, B], r3b.at[1], xm)]

    q0.wait_recv()
    gtb[POS[4]] = (gt[POS[4], 0] + sibr[POS[4]]).astype(BF)
    plus = send(gtb.at[POS[4], A], tp4.at[A], zp)
    minus = send(gtb.at[POS[4], B], tp4.at[B], zm)
    q1 = text_block(1)
    q2 = text_block(2)
    q3 = text_block(3)
    q1.wait_recv()
    plus.wait_recv()
    s3 = gt[POS[3], 0] + sibr[POS[3]]
    gtb[POS[3], A] = (s3[0:32] + tp4[A].astype(F32)).astype(BF)
    gtb[POS[3], B] = s3[32:64].astype(BF)
    plus = send(gtb.at[POS[3]], tpr.at[0], zp)
    minus.wait_recv()
    s3 = gt[POS[5], 0] + sibr[POS[5]]
    gtb[POS[5], A] = s3[0:32].astype(BF)
    gtb[POS[5], B] = (s3[32:64] + tp4[B].astype(F32)).astype(BF)
    minus = send(gtb.at[POS[5]], tmr.at[0], zm)
    for n, (a, b, q) in enumerate(((2, 6, q2), (1, 7, q3))):
        q.wait_recv()
        plus.wait_recv()
        gtb[POS[a]] = (gt[POS[a], 0] + sibr[POS[a]] + tpr[n].astype(F32)).astype(BF)
        plus = send(gtb.at[POS[a]], tpr.at[n + 1], zp)
        minus.wait_recv()
        gtb[POS[b]] = (gt[POS[b], 0] + sibr[POS[b]] + tmr[n].astype(F32)).astype(BF)
        minus = send(gtb.at[POS[b]], tmr.at[n + 1], zm)

    for cp in q3a:
        cp.wait_recv()
    for d in (2, 1, 3, 0):
        sa[d] = gi[0, d, A] + r3a[0, d].astype(F32) + r3a[1, d].astype(F32)
        if d == 2:
            q2a = [send(sa.at[2, A0], r2a.at[A0], xp), send(sa.at[2, A1], r2a.at[A1], xm)]
    for cp in q3b:
        cp.wait_recv()
    for d in (2, 1, 3, 0):
        sb[d] = gi[d, 0, B] + r3b[0, d].astype(F32) + r3b[1, d].astype(F32)
        if d == 2:
            q2b = [send(sb.at[2, A0], r2b.at[A0], yp), send(sb.at[2, A1], r2b.at[A1], ym)]
    last = []
    for q, s, r2, r1, fwd, back in ((q2a, sa, r2a, r1a, xp, xm), (q2b, sb, r2b, r1b, yp, ym)):
        for cp in q:
            cp.wait_recv()
        s[1, A0] += r2[A0]
        s[3, A1] += r2[A1]
        last.append(send(s.at[1], r1.at[0], fwd))
        last.append(send(s.at[3], r1.at[1], back))

    def back(m, dx):
        inner = jnp.sum(unit[m] * dx, axis=1, keepdims=True)
        dz = (scal[m][:, 0:1] * (dx - unit[m] * inner)).astype(BF)
        for q in range(4):
            zs[q, m, :, 0:256] = dz[:, 256 * q:256 * q + 256]
            zs[q, m, :, 256:384] = dz[:, 1024:1152]
        zr[mp, m] = zs[mp, m]
        return [send(zs.at[(mp + k) % 4, m], zr.at[mp, m], mps[k - 1]) for k in (1, 2, 3)]

    plus.wait_recv()
    minus.wait_recv()
    zin = back(1, gt[POS[0], 0] + sibr[POS[0]] + tpr[2].astype(F32) + tmr[2].astype(F32))
    for cp in last:
        cp.wait_recv()
    zin += back(0, jnp.concatenate([sa[0] + r1a[0] + r1a[1], sb[0] + r1b[0] + r1b[1]], axis=0))
    for cp in zin:
        cp.wait_recv()

    def gathered(m, cols):
        return jnp.concatenate([zr[q, m, :, cols] for q in range(4)], axis=0)

    i0 = lax.broadcasted_iota(jnp.int32, (128, 128), 0)
    i1 = lax.broadcasted_iota(jnp.int32, (128, 128), 1)
    pick_i = ((i0 == i1 + 32 * mp) & (i1 < 32)).astype(F32).astype(BF)
    pick_t = ((i0 == i1 - 32 + 32 * mp) & (i1 >= 32) & (i1 < 64)).astype(F32).astype(BF)
    zi, zt = gathered(0, slice(0, 256)), gathered(1, slice(0, 256))
    ri = dot(gathered(0, slice(256, 384)), pick_i).astype(BF)
    rt = dot(gathered(1, slice(256, 384)), pick_t).astype(BF)

    def chunk(dz):
        a, b = featst[0, (z + dz) % 8], featst[1, (z + dz) % 8]
        return jnp.concatenate([dot(a, zi), dot(b, zt), dot(a, ri) + dot(b, rt)], axis=1)

    H0, H1 = pl.ds(0, 80), pl.ds(80, 64)
    fst[4] = chunk(4).astype(BF)
    plus = send(fst.at[4, H0], fr.at[4, H0], zp)
    minus = send(fst.at[4, H1], fr.at[4, H1], zm)
    for a in (3, 2, 1):
        b = 8 - a
        fin[0] = chunk(a)
        fin[1] = chunk(b)
        plus.wait_recv()
        if a == 3:
            fin[0, H0] += fr[4, H0].astype(F32)
        else:
            fin[0] += fr[a + 1].astype(F32)
        fst[a] = fin[0].astype(BF)
        plus = send(fst.at[a], fr.at[a], zp)
        minus.wait_recv()
        if a == 3:
            fin[1, H1] += fr[4, H1].astype(F32)
        else:
            fin[1] += fr[b - 1].astype(F32)
        fst[b] = fin[1].astype(BF)
        minus = send(fst.at[b], fr.at[b], zm)
    fin[0] = chunk(0)
    plus.wait_recv()
    minus.wait_recv()
    summed = fin[0] + fr[1].astype(F32) + fr[7].astype(F32)
    fx[0] = summed[0:72]
    fx[1] = summed[72:144]
    cp = send(fx.at[1 - xl], fx.at[2], xo)
    cp.wait_recv()
    summed = fx[xl] + fx[2]
    for k in range(4):
        ys[k, 0:18] = summed[18 * k:18 * k + 18]
        ys[k, 18:24] = jnp.zeros((6, 640), F32)
    q = [send(ys.at[(y + 2) % 4], yr.at[1], y2), send(ys.at[(y + 1) % 4], yr.at[0], yp),
         send(ys.at[(y + 3) % 4], yr.at[2], ym)]
    for cp in q:
        cp.wait_recv()
    out = ys[y] + yr[0] + yr[1] + yr[2]
    oi_ref[:, 0:256] = out[0:18, 0:256]
    oi_ref[:, 256:288] = out[0:18, 512:544]
    ot_ref[:, 0:256] = out[0:18, 256:512]
    ot_ref[:, 256:288] = pltpu.roll(out[:, 512:640], 96, 1)[0:18, 0:32]
    for cp in started:
        cp.wait_send()


COPIES = 200


def local(image_feats, text_feats, image_proj, text_proj, log_temp, bias):
    total = image_feats.shape[0] * lax.axis_size("dp")
    vm = pltpu.VMEM
    out = jax.ShapeDtypeStruct((18, 288), F32)
    return pl.pallas_call(
        functools.partial(kernel, total),
        out_shape=(out, out),
        in_specs=[pl.BlockSpec(memory_space=pl.ANY)] * 4
        + [pl.BlockSpec(memory_space=pltpu.SMEM)] * 2,
        out_specs=(pl.BlockSpec(memory_space=vm), pl.BlockSpec(memory_space=vm)),
        scratch_shapes=[
            vm((2, 256, 1152), BF),
            vm((2, 1152, 288), BF),
            vm((2, 8, 144, 256), BF),
            vm((2, 4, 64, 384), BF),
            vm((2, 4, 64, 384), BF),
            vm((2, 64, 1152), F32),
            vm((2, 64, 128), F32),
            vm((4, 4, 64, 1152), BF),
            vm((8, 2, 64, 1152), BF),
            vm((256, 1024), F32),
            vm((1024, 1024), BF),
            vm((4, 4, 64, 1152), F32),
            vm((8, 2, 64, 1152), F32),
            vm((4, 4, 64, 1152), BF),
            vm((4, 32, 1152), BF),
            vm((2, 4, 32, 1152), BF),
            vm((32, 1152), F32),
            vm((2, 32, 1152), F32),
            vm((4, 32, 1152), BF),
            vm((2, 4, 32, 1152), BF),
            vm((32, 1152), F32),
            vm((2, 32, 1152), F32),
            vm((4, 32, 1152), F32),
            vm((4, 32, 1152), F32),
            vm((8, 64, 1152), F32),
            vm((8, 64, 1152), BF),
            vm((64, 1152), BF),
            vm((3, 64, 1152), BF),
            vm((3, 64, 1152), BF),
            vm((4, 2, 64, 384), BF),
            vm((4, 2, 64, 384), BF),
            vm((2, 144, 640), F32),
            vm((8, 144, 640), BF),
            vm((8, 144, 640), BF),
            vm((3, 72, 640), F32),
            vm((4, 24, 640), F32),
            vm((3, 24, 640), F32),
            pltpu.SemaphoreType.DMA((4,)),
            pltpu.SemaphoreType.DMA((COPIES,)),
            pltpu.SemaphoreType.DMA((COPIES,)),
        ],
        name="contrastive",
        compiler_params=pltpu.CompilerParams(
            collective_id=0, has_side_effects=True, vmem_limit_bytes=60 * 2**20
        ),
    )(image_feats, text_feats, image_proj, text_proj, log_temp, bias)


def solution(mesh):
    placed = (P("dp", None), P("dp", None), P(None, "mp"), P(None, "mp"), P(), P())
    return jax.shard_map(
        local, mesh=mesh, in_specs=placed, out_specs=(P("dp", "mp"), P("dp", "mp")), check_vma=False
    )
```

```python
import functools

import jax
import jax.numpy as jnp
from jax import lax
from jax.experimental import pallas as pl
from jax.experimental.pallas import tpu as pltpu
from jax.sharding import PartitionSpec as P

MESH = pl.DeviceIdType.MESH
F32, BF = jnp.float32, jnp.bfloat16
PIECE = 64
POS = {4: 0, 0: 1, 3: 2, 5: 3, 2: 4, 6: 5, 1: 6, 7: 7}


def dot(a, b):
    return jnp.dot(a, b, preferred_element_type=F32)


def dot_nt(a, b):
    return lax.dot_general(a, b, (((1,), (1,)), ((), ())), preferred_element_type=F32)


def dot_tn(a, b):
    return lax.dot_general(a, b, (((0,), (0,)), ((), ())), preferred_element_type=F32)


def kernel(total, fi_hbm, ft_hbm, wi_hbm, wt_hbm, lt_ref, bs_ref, oi_ref, ot_ref,
           feats, wts, featst, es, er, unit, scal, img, txt, prob, gi, gt,
           gib, ra, rb, ra2, rb2, sa, sb, sab, sbb,
           sibr, gtb, tp4, tpr, tmr, zs, zr, fst, fr, ys, yr,
           lsem, ssem, rsem):
    dp, mp = lax.axis_index("dp"), lax.axis_index("mp")
    z, xl, y = dp // 8, (dp // 4) % 2, dp % 4
    c = mp % 2
    x = (mp // 2) * 2 + xl

    def dev(xx, yy, zz, cc):
        return (zz * 8 + (xx % 2) * 4 + yy, (xx // 2) * 2 + cc)

    xp, x2, xm = (dev((x + k) % 4, y, z, c) for k in (1, 2, 3))
    yp, y2, ym = (dev(x, (y + k) % 4, z, c) for k in (1, 2, 3))
    zs_at = [dev(x, y, (z + k) % 8, c) for k in range(8)]
    zp, zm = zs_at[1], zs_at[7]
    ws_at = [(z * 8 + ((xl + k // 4) % 2) * 4 + (y + k) % 4, mp) for k in range(8)]
    sib = (dp, (mp // 2) * 2 + (1 - c))
    mps = [(dp, (mp + k) % 4) for k in (1, 2, 3)]

    barrier = pltpu.get_barrier_semaphore()
    greeted = mps + [xp, xm] + zs_at[1:] + ws_at[1:4] + ws_at[5:]
    for d in greeted:
        pl.semaphore_signal(barrier, inc=1, device_id=d, device_id_type=MESH)

    loads = []
    for k, (s, t) in enumerate(((fi_hbm, feats.at[0, 0:224]), (wi_hbm, wts.at[0]),
                                (ft_hbm, feats.at[1, 0:224]), (wt_hbm, wts.at[1]))):
        cp = pltpu.make_async_copy(s, t, lsem.at[k])
        cp.start()
        loads.append(cp)
    feats[:, 224:256, :] = jnp.zeros((2, 32, 1152), BF)

    started = []

    def send(src, dst, to):
        k = len(started)
        cp = pltpu.make_async_remote_copy(src_ref=src, dst_ref=dst, send_sem=ssem.at[k],
                                          recv_sem=rsem.at[k], device_id=to, device_id_type=MESH)
        cp.start()
        started.append(cp)
        return cp

    place = (lax.broadcasted_iota(jnp.int32, (32, 128), 1)
             == lax.broadcasted_iota(jnp.int32, (32, 128), 0) + 32 * mp).astype(F32).astype(BF)
    emb_in = [[], []]
    for m in (0, 1):
        loads[2 * m].wait()
        loads[2 * m + 1].wait()
        main = dot_nt(feats[m], wts[m, 0:256, :]).astype(BF)
        rest = dot_nt(feats[m], wts[m, 256:288, :]).astype(BF)
        rest = dot(rest, place).astype(BF)
        for q in range(4):
            es[m, q, :, 0:256] = main[64 * q:64 * q + 64]
            es[m, q, :, 256:384] = rest[64 * q:64 * q + 64]
        if m == 0:
            pl.semaphore_wait(barrier, len(greeted))
        for k in (1, 2, 3):
            emb_in[m].append(send(es.at[m, (mp + k) % 4], er.at[m, mp], mps[k - 1]))
        er[m, mp] = es[m, mp]

    def normalize(m):
        for cp in emb_in[m]:
            cp.wait_recv()
        rest = sum(er[m, q, :, 256:384].astype(F32) for q in range(4))
        wide = jnp.concatenate([er[m, q, :, 0:256].astype(F32) for q in range(4)] + [rest], axis=1)
        scale = lax.rsqrt(jnp.sum(wide * wide, axis=1, keepdims=True) + 1e-06)
        unit[m] = wide * scale
        scal[m] = jnp.broadcast_to(scale, (64, 128))
        return (wide * scale).astype(BF)

    A, B = pl.ds(0, 32), pl.ds(32, 32)
    A0, A1, B0, B1 = pl.ds(0, 16), pl.ds(16, 16), pl.ds(32, 16), pl.ds(48, 16)
    got = {}
    img[0, 0] = normalize(0)
    got["A03"] = send(img.at[0, 0, A], img.at[0, 3, A], xp)
    got["A01"] = send(img.at[0, 0, A], img.at[0, 1, A], xm)
    got["B30"] = send(img.at[0, 0, B], img.at[3, 0, B], yp)
    got["B10"] = send(img.at[0, 0, B], img.at[1, 0, B], ym)
    got["A02"] = send(img.at[0, 0, A], img.at[0, 2, A], x2)
    got["B20"] = send(img.at[0, 0, B], img.at[2, 0, B], y2)
    got["A30"] = send(img.at[0, 0, A], img.at[3, 0, A], yp)
    got["A10"] = send(img.at[0, 0, A], img.at[1, 0, A], ym)
    got["B03"] = send(img.at[0, 0, B], img.at[0, 3, B], xp)
    got["B01"] = send(img.at[0, 0, B], img.at[0, 1, B], xm)

    txt[POS[0], 0] = normalize(1)
    tgot = {}
    sgot = []
    tgot[7] = send(txt.at[POS[0], 0], txt.at[POS[7], 0], zp)
    tgot[1] = send(txt.at[POS[0], 0], txt.at[POS[1], 0], zm)
    sgot.append(send(txt.at[POS[0], 0], txt.at[POS[0], 1], sib))

    def text_hop(k):
        for src, nxt, to, half in ((8 - k, 7 - k, zp, A), (k, k + 1, zm, B)):
            tgot[src].wait_recv()
            if k < 3:
                tgot[nxt] = send(txt.at[POS[src], 0], txt.at[POS[nxt], 0], to)
            else:
                tgot[(4, src)] = send(txt.at[POS[src], 0, half], txt.at[POS[4], 0, half], to)
            sgot.append(send(txt.at[POS[src], 0], txt.at[POS[src], 1], sib))

    wide_t = jnp.transpose(feats[0])
    for k in range(8):
        featst[0, k] = wide_t[144 * k:144 * k + 144]
    p0 = lax.broadcasted_iota(jnp.int32, (144, 1152), 0)
    at_z = p0 + 126 * ((p0 * 3641) >> 16)
    p1 = lax.broadcasted_iota(jnp.int32, (144, 1152), 1)

    def turn(w, _):
        featst[1, w] = dot_nt((p1 == at_z + 18 * w).astype(F32).astype(BF), feats[1]).astype(BF)
        return 0
    lax.fori_loop(0, 8, turn, 0)

    def second(d):
        got["A3%d" % d] = send(img.at[0, d, A], img.at[3, d, A], yp)
        got["A1%d" % d] = send(img.at[0, d, A], img.at[1, d, A], ym)
        got["B%d3" % d] = send(img.at[d, 0, B], img.at[d, 3, B], xp)
        got["B%d1" % d] = send(img.at[d, 0, B], img.at[d, 1, B], xm)

    def third(d):
        got["A3%d" % d].wait_recv()
        got["A2%d+" % d] = send(img.at[3, d, A0], img.at[2, d, A0], yp)
        got["A1%d" % d].wait_recv()
        got["A2%d-" % d] = send(img.at[1, d, A1], img.at[2, d, A1], ym)
        got["B%d3" % d].wait_recv()
        got["B%d2+" % d] = send(img.at[d, 3, B0], img.at[d, 2, B0], xp)
        got["B%d1" % d].wait_recv()
        got["B%d2-" % d] = send(img.at[d, 1, B1], img.at[d, 2, B1], xm)

    for k in ("A03", "A01", "B30", "B10"):
        got[k].wait_recv()
    second(1)
    second(3)
    text_hop(1)
    for k in ("A02", "B20"):
        got[k].wait_recv()
    second(2)
    third(0)
    text_hop(2)
    third(1)
    third(3)
    text_hop(3)
    third(2)

    temp = jnp.exp(jnp.full((1, 1), lt_ref[0], F32))
    shift = jnp.full((1, 1), bs_ref[0], F32)
    gain = temp * (1.0 / total)

    def scores(dy, n):
        at = pl.ds(2 * n, 2)
        logits = temp * dot_nt(img[dy].reshape(256, 1152), txt[at].reshape(256, 1152)) + shift
        cols = pl.ds(pl.multiple_of(256 * n, 256), 256)
        prob[256 * dy:256 * dy + 256, cols] = (gain / (1.0 + jnp.exp(-logits))).astype(BF)
        return logits

    def early(dy):
        for d in range(4) if dy == 2 else ():
            got["A2%d+" % d].wait_recv()
            got["A2%d-" % d].wait_recv()
        got["B%d2+" % dy].wait_recv()
        got["B%d2-" % dy].wait_recv()

        def some(i, _):
            scores(dy, 3 - i)
            return 0
        lax.fori_loop(0, 3, some, 0)

    def late(dy):
        logits = scores(dy, 0)
        if dy == 0:
            logits = logits[0:64, 128:256]
            same = (lax.broadcasted_iota(jnp.int32, (64, 128), 0)
                    == lax.broadcasted_iota(jnp.int32, (64, 128), 1))
            prob[0:64, 128:256] = jnp.where(
                same, -gain / (1.0 + jnp.exp(logits)), gain / (1.0 + jnp.exp(-logits))).astype(BF)
        gi[dy] = dot(prob[256 * dy:256 * dy + 256, :],
                     txt[...].reshape(1024, 1152)).reshape(4, 64, 1152)
        gib[dy] = gi[dy].astype(BF)
        if dy:
            qa.append(send(gib.at[dy, :, A], ra.at[dy - 1], (yp, y2, ym)[dy - 1]))
        for d in (2, 1, 3):
            qb.append(send(gib.at[dy, d, B], rb.at[d - 1, dy], (xp, x2, xm)[d - 1]))

    qa, qb = [], []
    for cp in sgot:
        cp.wait_recv()
    early(0)
    tgot[(4, 5)].wait_recv()
    tgot[(4, 3)].wait_recv()
    last_sib = send(txt.at[POS[4], 0], txt.at[POS[4], 1], sib)
    early(1)
    early(3)
    last_sib.wait_recv()
    late(1)
    late(3)
    late(0)
    early(2)
    late(2)

    def text_block(n):
        gt[2 * n:2 * n + 2] = dot_tn(prob[:, 256 * n:256 * n + 256],
                                     img[...].reshape(1024, 1152)).reshape(2, 2, 64, 1152)
        return send(gt.at[2 * n:2 * n + 2, 1], sibr.at[2 * n:2 * n + 2], sib)

    q0 = text_block(0)
    q1 = text_block(1)
    q0.wait_recv()
    gtb[POS[4]] = (gt[POS[4], 0] + sibr[POS[4]]).astype(BF)
    plus = send(gtb.at[POS[4], A], tp4.at[A], zp)
    minus = send(gtb.at[POS[4], B], tp4.at[B], zm)
    q2 = text_block(2)
    q3 = text_block(3)
    q1.wait_recv()
    plus.wait_recv()
    s3 = gt[POS[3], 0] + sibr[POS[3]]
    gtb[POS[3], A] = (s3[0:32] + tp4[A].astype(F32)).astype(BF)
    gtb[POS[3], B] = s3[32:64].astype(BF)
    plus = send(gtb.at[POS[3]], tpr.at[0], zp)
    minus.wait_recv()
    s3 = gt[POS[5], 0] + sibr[POS[5]]
    gtb[POS[5], A] = s3[0:32].astype(BF)
    gtb[POS[5], B] = (s3[32:64] + tp4[B].astype(F32)).astype(BF)
    minus = send(gtb.at[POS[5]], tmr.at[0], zm)
    for n, (a, b, q) in enumerate(((2, 6, q2), (1, 7, q3))):
        q.wait_recv()
        plus.wait_recv()
        gtb[POS[a]] = (gt[POS[a], 0] + sibr[POS[a]] + tpr[n].astype(F32)).astype(BF)
        plus = send(gtb.at[POS[a]], tpr.at[n + 1], zp)
        minus.wait_recv()
        gtb[POS[b]] = (gt[POS[b], 0] + sibr[POS[b]] + tmr[n].astype(F32)).astype(BF)
        minus = send(gtb.at[POS[b]], tmr.at[n + 1], zm)

    for cp in qa:
        cp.wait_recv()
    qa2, qb2 = [], []
    for d in (2, 1, 3, 0):
        sa[d] = gi[0, d, A] + ra[0, d].astype(F32) + ra[1, d].astype(F32) + ra[2, d].astype(F32)
        if d:
            sab[d - 1] = sa[d].astype(BF)
            qa2.append(send(sab.at[d - 1], ra2.at[d - 1], (xp, x2, xm)[d - 1]))
    for cp in qb:
        cp.wait_recv()
    for d in (2, 1, 3, 0):
        sb[d] = gi[d, 0, B] + rb[0, d].astype(F32) + rb[1, d].astype(F32) + rb[2, d].astype(F32)
        if d:
            sbb[d - 1] = sb[d].astype(BF)
            qb2.append(send(sbb.at[d - 1], rb2.at[d - 1], (yp, y2, ym)[d - 1]))

    def back(m, dx):
        inner = jnp.sum(unit[m] * dx, axis=1, keepdims=True)
        dz = (scal[m][:, 0:1] * (dx - unit[m] * inner)).astype(BF)
        for q in range(4):
            zs[m, q, :, 0:256] = dz[:, 256 * q:256 * q + 256]
            zs[m, q, :, 256:384] = dz[:, 1024:1152]
        zr[m, mp] = zs[m, mp]
        return [send(zs.at[m, (mp + k) % 4], zr.at[m, mp], mps[k - 1]) for k in (1, 2, 3)]

    plus.wait_recv()
    minus.wait_recv()
    zt_in = back(1, gt[POS[0], 0] + sibr[POS[0]] + tpr[2].astype(F32) + tmr[2].astype(F32))
    for cp in qa2 + qb2:
        cp.wait_recv()
    sums = [s[0] + r[0].astype(F32) + r[1].astype(F32) + r[2].astype(F32)
            for s, r in ((sa, ra2), (sb, rb2))]
    zi_in = back(0, jnp.concatenate(sums, axis=0))

    pick = (lax.broadcasted_iota(jnp.int32, (128, 128), 0)
            == lax.broadcasted_iota(jnp.int32, (128, 128), 1) + 32 * mp)
    pick = (pick & (lax.broadcasted_iota(jnp.int32, (128, 128), 1) < 32)).astype(F32).astype(BF)
    far_z, far_w = (4, 3, 5, 2, 6, 1, 7), (6, 2, 5, 7, 1, 3, 4)

    def first(m, arrived, far, base, at):
        for cp in arrived:
            cp.wait_recv()
        rest = jnp.concatenate([zr[m, q, :, 256:384] for q in range(4)], axis=0)
        grads = jnp.concatenate(
            [jnp.concatenate([zr[m, q, :, 0:256] for q in range(4)], axis=0),
             dot(rest, pick).astype(BF)], axis=1)
        q = []
        for k in far:
            fst[m, k] = dot(featst[m, base(k)], grads).astype(BF)
            q.append(send(fst.at[m, k], fr.at[m, k], at[k]))
        return q, dot(featst[m, base(0)], grads)

    def second_sum(m, q, own, far, base, at):
        for cp in q:
            cp.wait_recv()
        summed = own
        for k in far:
            summed = summed + fr[m, k].astype(F32)
        for k in range(8):
            ys[m, k, 0:18] = summed[18 * k:18 * k + 18]
            ys[m, k, 18:24] = jnp.zeros((6, 384), F32)
        return [send(ys.at[m, base(k)], yr.at[m, k], at[k]) for k in far]

    def by_z(k):
        return (z + k) % 8

    def by_w(k):
        return ((xl + k // 4) % 2) * 4 + (y + k) % 4

    qt, own_t = first(1, zt_in, far_w, by_w, ws_at)
    qi, own_i = first(0, zi_in, far_z, by_z, zs_at)
    qt2 = second_sum(1, qt, own_t, far_z, by_z, zs_at)
    qi2 = second_sum(0, qi, own_i, far_w, by_w, ws_at)
    for m, q, base, ref in ((1, qt2, by_z, ot_ref), (0, qi2, by_w, oi_ref)):
        for cp in q:
            cp.wait_recv()
        out = ys[m, base(0)]
        for k in range(1, 8):
            out = out + yr[m, k]
        ref[...] = out[0:18, 0:288]
    for cp in started:
        cp.wait_send()


COPIES = 256


def local(image_feats, text_feats, image_proj, text_proj, log_temp, bias):
    total = image_feats.shape[0] * lax.axis_size("dp")
    vm = pltpu.VMEM
    out = jax.ShapeDtypeStruct((18, 288), F32)
    return pl.pallas_call(
        functools.partial(kernel, total),
        out_shape=(out, out),
        in_specs=[pl.BlockSpec(memory_space=pl.ANY)] * 4
        + [pl.BlockSpec(memory_space=pltpu.SMEM)] * 2,
        out_specs=(pl.BlockSpec(memory_space=vm), pl.BlockSpec(memory_space=vm)),
        scratch_shapes=[
            vm((2, 256, 1152), BF),
            vm((2, 288, 1152), BF),
            vm((2, 8, 144, 256), BF),
            vm((2, 4, 64, 384), BF),
            vm((2, 4, 64, 384), BF),
            vm((2, 64, 1152), F32),
            vm((2, 64, 128), F32),
            vm((4, 4, 64, 1152), BF),
            vm((8, 2, 64, 1152), BF),
            vm((1024, 1024), BF),
            vm((4, 4, 64, 1152), F32),
            vm((8, 2, 64, 1152), F32),
            vm((4, 4, 64, 1152), BF),
            vm((3, 4, 32, 1152), BF),
            vm((3, 4, 32, 1152), BF),
            vm((3, 32, 1152), BF),
            vm((3, 32, 1152), BF),
            vm((4, 32, 1152), F32),
            vm((4, 32, 1152), F32),
            vm((3, 32, 1152), BF),
            vm((3, 32, 1152), BF),
            vm((8, 64, 1152), F32),
            vm((8, 64, 1152), BF),
            vm((64, 1152), BF),
            vm((3, 64, 1152), BF),
            vm((3, 64, 1152), BF),
            vm((2, 4, 64, 384), BF),
            vm((2, 4, 64, 384), BF),
            vm((2, 8, 144, 384), BF),
            vm((2, 8, 144, 384), BF),
            vm((2, 8, 24, 384), F32),
            vm((2, 8, 24, 384), F32),
            pltpu.SemaphoreType.DMA((4,)),
            pltpu.SemaphoreType.DMA((COPIES,)),
            pltpu.SemaphoreType.DMA((COPIES,)),
        ],
        name="contrastive",
        compiler_params=pltpu.CompilerParams(
            collective_id=0, has_side_effects=True, vmem_limit_bytes=60 * 2**20
        ),
    )(image_feats, text_feats, image_proj.T, text_proj.T, log_temp, bias)


def solution(mesh):
    placed = (P("dp", None), P("dp", None), P(None, "mp"), P(None, "mp"), P(), P())
    return jax.shard_map(
        local, mesh=mesh, in_specs=placed, out_specs=(P("dp", "mp"), P("dp", "mp")), check_vma=False
    )
```

```python
import functools

import jax
import jax.numpy as jnp
from jax import lax
from jax.experimental import pallas as pl
from jax.experimental.pallas import tpu as pltpu
from jax.sharding import PartitionSpec as P

MESH = pl.DeviceIdType.MESH
F32, BF = jnp.float32, jnp.bfloat16
PIECE = 64
POS = {4: 0, 0: 1, 3: 2, 5: 3, 2: 4, 6: 5, 1: 6, 7: 7}


def dot(a, b):
    return jnp.dot(a, b, preferred_element_type=F32)


def dot_nt(a, b):
    return lax.dot_general(a, b, (((1,), (1,)), ((), ())), preferred_element_type=F32)


def dot_tn(a, b):
    return lax.dot_general(a, b, (((0,), (0,)), ((), ())), preferred_element_type=F32)


def kernel(total, fi_hbm, ft_hbm, wi_hbm, wt_hbm, lt_ref, bs_ref, oi_ref, ot_ref,
           feats, wts, featst, es, er, unit, scal, img, txt, prob, gi, gt,
           gib, ra, ra2, sa, sab, sibr, gtb, tp4, tpr, tmr, zs, zr,
           fsi, fri, fst, frt, ysi, yri, yst, yrt,
           lsem, ssem, rsem):
    dp, mp = lax.axis_index("dp"), lax.axis_index("mp")
    z, xl, y = dp // 8, (dp // 4) % 2, dp % 4
    c = mp % 2
    x = (mp // 2) * 2 + xl

    def dev(xx, yy, zz, cc):
        return (zz * 8 + (xx % 2) * 4 + yy, (xx // 2) * 2 + cc)

    xp, x2, xm = (dev((x + k) % 4, y, z, c) for k in (1, 2, 3))
    yp, y2, ym = (dev(x, (y + k) % 4, z, c) for k in (1, 2, 3))
    zs_at = [dev(x, y, (z + k) % 8, c) for k in range(8)]
    zp, zm = zs_at[1], zs_at[7]
    ws_at = [(z * 8 + ((xl + k // 4) % 2) * 4 + (y + k) % 4, mp) for k in range(8)]
    sib = (dp, (mp // 2) * 2 + (1 - c))
    mps = [(dp, (mp + k) % 4) for k in (1, 2, 3)]

    barrier = pltpu.get_barrier_semaphore()
    greeted = mps + [xp, xm] + zs_at[1:] + ws_at[1:4] + ws_at[5:]
    for d in greeted:
        pl.semaphore_signal(barrier, inc=1, device_id=d, device_id_type=MESH)

    loads = []
    for k, (s, t) in enumerate(((fi_hbm, feats.at[0, 0:224]), (wi_hbm, wts.at[0]),
                                (ft_hbm, feats.at[1, 0:224]), (wt_hbm, wts.at[1]))):
        cp = pltpu.make_async_copy(s, t, lsem.at[k])
        cp.start()
        loads.append(cp)
    feats[:, 224:256, :] = jnp.zeros((2, 32, 1152), BF)

    started = []

    def send(src, dst, to):
        k = len(started)
        cp = pltpu.make_async_remote_copy(src_ref=src, dst_ref=dst, send_sem=ssem.at[k],
                                          recv_sem=rsem.at[k], device_id=to, device_id_type=MESH)
        cp.start()
        started.append(cp)
        return cp

    place = (lax.broadcasted_iota(jnp.int32, (32, 128), 1)
             == lax.broadcasted_iota(jnp.int32, (32, 128), 0) + 32 * mp).astype(F32).astype(BF)
    emb_in = [[], []]
    for m in (0, 1):
        loads[2 * m].wait()
        loads[2 * m + 1].wait()
        main = dot_nt(feats[m], wts[m, 0:256, :]).astype(BF)
        rest = dot_nt(feats[m], wts[m, 256:288, :]).astype(BF)
        rest = dot(rest, place).astype(BF)
        for q in range(4):
            es[m, q, :, 0:256] = main[64 * q:64 * q + 64]
            es[m, q, :, 256:384] = rest[64 * q:64 * q + 64]
        if m == 0:
            pl.semaphore_wait(barrier, len(greeted))
        for k in (1, 2, 3):
            emb_in[m].append(send(es.at[m, (mp + k) % 4], er.at[m, mp], mps[k - 1]))
        er[m, mp] = es[m, mp]

    def normalize(m):
        for cp in emb_in[m]:
            cp.wait_recv()
        rest = sum(er[m, q, :, 256:384].astype(F32) for q in range(4))
        wide = jnp.concatenate([er[m, q, :, 0:256].astype(F32) for q in range(4)] + [rest], axis=1)
        scale = lax.rsqrt(jnp.sum(wide * wide, axis=1, keepdims=True) + 1e-06)
        unit[m] = wide * scale
        scal[m] = jnp.broadcast_to(scale, (64, 128))
        return (wide * scale).astype(BF)

    A, B, A0, A1 = pl.ds(0, 32), pl.ds(32, 32), pl.ds(0, 16), pl.ds(16, 16)
    axis1 = ((xp, x2, xm), (yp, y2, ym))
    axis2 = ((yp, y2, ym), (xp, x2, xm))
    got = {}
    piece = normalize(0)
    img[0, 0, 0] = piece[0:32]
    img[0, 1, 0] = piece[32:64]
    for j in (1, 3, 2):
        for h in (0, 1):
            got[0, h, 4 - j] = send(img.at[0, h, 0], img.at[0, h, 4 - j], axis1[h][j - 1])

    def second(j):
        for h in (0, 1):
            got[3, h, j] = send(img.at[0, h, j], img.at[3, h, j], axis2[h][0])
            got[1, h, j] = send(img.at[0, h, j], img.at[1, h, j], axis2[h][2])

    def third(j):
        for h in (0, 1):
            got[3, h, j].wait_recv()
            got[4, h, j] = send(img.at[3, h, j, A0], img.at[2, h, j, A0], axis2[h][0])
            got[1, h, j].wait_recv()
            got[5, h, j] = send(img.at[1, h, j, A1], img.at[2, h, j, A1], axis2[h][2])

    second(0)
    txt[POS[0], 0] = normalize(1)
    tgot = {}
    sgot = []
    tgot[7] = send(txt.at[POS[0], 0], txt.at[POS[7], 0], zp)
    tgot[1] = send(txt.at[POS[0], 0], txt.at[POS[1], 0], zm)
    sgot.append(send(txt.at[POS[0], 0], txt.at[POS[0], 1], sib))

    def text_hop(k):
        for src, nxt, to, half in ((8 - k, 7 - k, zp, A), (k, k + 1, zm, B)):
            tgot[src].wait_recv()
            if k < 3:
                tgot[nxt] = send(txt.at[POS[src], 0], txt.at[POS[nxt], 0], to)
            else:
                tgot[(4, src)] = send(txt.at[POS[src], 0, half], txt.at[POS[4], 0, half], to)
            sgot.append(send(txt.at[POS[src], 0], txt.at[POS[src], 1], sib))

    temp = jnp.exp(jnp.full((1, 1), lt_ref[0], F32))
    shift = jnp.full((1, 1), bs_ref[0], F32)
    gain = temp * (1.0 / total)

    def scores(k, n):
        at = pl.ds(2 * n, 2)
        logits = temp * dot_nt(img[k].reshape(256, 1152), txt[at].reshape(256, 1152)) + shift
        cols = pl.ds(pl.multiple_of(256 * n, 256), 256)
        prob[256 * k:256 * k + 256, cols] = (gain / (1.0 + jnp.exp(-logits))).astype(BF)
        return logits

    def some_scores(k, count):
        def one(i, _):
            scores(k, 3 - i)
            return 0
        lax.fori_loop(0, count, one, 0)

    for j in (1, 3):
        got[0, 0, j].wait_recv()
        got[0, 1, j].wait_recv()
        second(j)
    text_hop(1)
    got[0, 0, 2].wait_recv()
    got[0, 1, 2].wait_recv()
    second(2)
    third(0)
    text_hop(2)
    sgot[1].wait_recv()
    sgot[2].wait_recv()
    scores(0, 3)
    third(1)
    third(3)
    text_hop(3)
    sgot[3].wait_recv()
    sgot[4].wait_recv()
    scores(0, 2)
    third(2)

    for n in (5, 6, 0):
        sgot[n].wait_recv()
    scores(0, 1)
    some_scores(1, 3)
    tgot[(4, 5)].wait_recv()
    tgot[(4, 3)].wait_recv()
    last_sib = send(txt.at[POS[4], 0], txt.at[POS[4], 1], sib)
    some_scores(3, 3)
    last_sib.wait_recv()
    scores(1, 0)
    scores(3, 0)
    logits = scores(0, 0)
    r0 = lax.broadcasted_iota(jnp.int32, (32, 128), 0)
    r1 = lax.broadcasted_iota(jnp.int32, (32, 128), 1)
    for h in (0, 1):
        own = logits[128 * h:128 * h + 32, 128:256]
        prob[128 * h:128 * h + 32, 128:256] = jnp.where(
            r1 == r0 + 32 * h, -gain / (1.0 + jnp.exp(own)), gain / (1.0 + jnp.exp(-own))).astype(BF)

    qa = [[], []]

    def image_block(k):
        gi[k] = dot(prob[256 * k:256 * k + 256, :],
                    txt[...].reshape(1024, 1152)).reshape(2, 4, 32, 1152)
        if k:
            gib[k - 1] = gi[k].astype(BF)
            for h in (0, 1):
                qa[h].append(send(gib.at[k - 1, h], ra.at[k - 1, h], axis2[h][k - 1]))

    def text_block(n):
        gt[2 * n:2 * n + 2] = dot_tn(prob[:, 256 * n:256 * n + 256],
                                     img[...].reshape(1024, 1152)).reshape(2, 2, 64, 1152)
        return send(gt.at[2 * n:2 * n + 2, 1], sibr.at[2 * n:2 * n + 2], sib)

    image_block(1)
    image_block(3)
    for j in range(4):
        for h in (0, 1):
            got[4, h, j].wait_recv()
            got[5, h, j].wait_recv()
    some_scores(2, 4)
    image_block(2)
    q0 = text_block(0)
    q1 = text_block(1)
    q0.wait_recv()
    gtb[POS[4]] = (gt[POS[4], 0] + sibr[POS[4]]).astype(BF)
    plus = send(gtb.at[POS[4], A], tp4.at[A], zp)
    minus = send(gtb.at[POS[4], B], tp4.at[B], zm)
    q2 = text_block(2)
    q3 = text_block(3)
    image_block(0)

    wide_t = jnp.transpose(feats[0])
    for k in range(8):
        featst[0, k] = wide_t[144 * k:144 * k + 144]
    p0 = lax.broadcasted_iota(jnp.int32, (144, 1152), 0)
    at_z = p0 + 126 * ((p0 * 3641) >> 16)
    p1 = lax.broadcasted_iota(jnp.int32, (144, 1152), 1)

    def turn(w, _):
        turned = (p1 == at_z + 18 * w).astype(F32).astype(BF)
        featst[1, w] = dot_nt(turned, feats[1]).astype(BF)
        featst[2, w] = dot_nt(turned, feats[0]).astype(BF)
        return 0
    lax.fori_loop(0, 8, turn, 0)

    q1.wait_recv()
    plus.wait_recv()
    s3 = gt[POS[3], 0] + sibr[POS[3]]
    gtb[POS[3], A] = (s3[0:32] + tp4[A].astype(F32)).astype(BF)
    gtb[POS[3], B] = s3[32:64].astype(BF)
    plus = send(gtb.at[POS[3]], tpr.at[0], zp)
    minus.wait_recv()
    s3 = gt[POS[5], 0] + sibr[POS[5]]
    gtb[POS[5], A] = s3[0:32].astype(BF)
    gtb[POS[5], B] = (s3[32:64] + tp4[B].astype(F32)).astype(BF)
    minus = send(gtb.at[POS[5]], tmr.at[0], zm)

    def text_sum(n, a, b, q, plus, minus):
        q.wait_recv()
        plus.wait_recv()
        gtb[POS[a]] = (gt[POS[a], 0] + sibr[POS[a]] + tpr[n].astype(F32)).astype(BF)
        plus = send(gtb.at[POS[a]], tpr.at[n + 1], zp)
        minus.wait_recv()
        gtb[POS[b]] = (gt[POS[b], 0] + sibr[POS[b]] + tmr[n].astype(F32)).astype(BF)
        return plus, send(gtb.at[POS[b]], tmr.at[n + 1], zm)

    plus, minus = text_sum(0, 2, 6, q2, plus, minus)
    qa2 = []
    for h in (0, 1):
        for cp in qa[h]:
            cp.wait_recv()
        for j in (2, 1, 3, 0):
            part = gi[0, h, j]
            for k in range(3):
                part = part + ra[k, h, j].astype(F32)
            if j:
                sab[h, j - 1] = part.astype(BF)
                qa2.append(send(sab.at[h, j - 1], ra2.at[h, j - 1], axis1[h][j - 1]))
            else:
                sa[h] = part
    plus, minus = text_sum(1, 1, 7, q3, plus, minus)

    def back(m, dx):
        inner = jnp.sum(unit[m] * dx, axis=1, keepdims=True)
        dz = (scal[m][:, 0:1] * (dx - unit[m] * inner)).astype(BF)
        for q in range(4):
            zs[m, q, :, 0:256] = dz[:, 256 * q:256 * q + 256]
            zs[m, q, :, 256:384] = dz[:, 1024:1152]
        zr[m, mp] = zs[m, mp]
        return [send(zs.at[m, (mp + k) % 4], zr.at[m, mp], mps[k - 1]) for k in (1, 2, 3)]

    for cp in qa2:
        cp.wait_recv()
    zi_in = back(0, jnp.concatenate(
        [sa[h] + ra2[h, 0].astype(F32) + ra2[h, 1].astype(F32) + ra2[h, 2].astype(F32)
         for h in (0, 1)], axis=0))
    plus.wait_recv()
    minus.wait_recv()
    zt_in = back(1, gt[POS[0], 0] + sibr[POS[0]] + tpr[2].astype(F32) + tmr[2].astype(F32))

    far_z, far_w = (4, 3, 5, 2, 6, 1, 7), (6, 2, 5, 7, 1, 3, 4)
    l0 = lax.broadcasted_iota(jnp.int32, (128, 128), 0)
    l1 = lax.broadcasted_iota(jnp.int32, (128, 128), 1)

    def by_z(k):
        return (z + k) % 8

    def by_w(k):
        return ((xl + k // 4) % 2) * 4 + (y + k) % 4

    def columns(m, arrived):
        for cp in arrived:
            cp.wait_recv()
        pick = ((l0 + 32 * m == l1 + 32 * mp) & (l1 >= 32 * m) & (l1 < 32 * m + 32)).astype(F32).astype(BF)
        rest = jnp.concatenate([zr[m, q, :, 256:384] for q in range(4)], axis=0)
        return (jnp.concatenate([zr[m, q, :, 0:256] for q in range(4)], axis=0),
                dot(rest, pick).astype(BF))

    def spread(st, rc, far, make, at):
        q = []
        for k in far:
            st[k] = make(k).astype(BF)
            q.append(send(st.at[k], rc.at[k], at[k]))
        return q

    def regroup(q, own, rc, far, ys, yr, base, at):
        for cp in q:
            cp.wait_recv()
        for k in far:
            own = own + rc[k].astype(F32)
        for k in range(8):
            ys[k, 0:18] = own[18 * k:18 * k + 18]
        return [send(ys.at[base(k)], yr.at[k], at[k]) for k in far]

    def last_sum(q, ys, yr, base):
        for cp in q:
            cp.wait_recv()
        out = ys[base(0)]
        for k in range(1, 8):
            out = out + yr[k]
        return out

    main_i, rest_i = columns(0, zi_in)

    def make_i(k):
        return dot(featst[0, by_z(k)], main_i)

    qi = spread(fsi, fri, far_z, make_i, zs_at)
    own_i = make_i(0)
    main_t, rest_t = columns(1, zt_in)

    def make_t(k):
        a, b = featst[1, by_w(k)], featst[2, by_w(k)]
        return jnp.concatenate([dot(a, main_t), dot(a, rest_t) + dot(b, rest_i)], axis=1)

    qt = spread(fst, frt, far_w, make_t, ws_at)
    own_t = make_t(0)
    qi = regroup(qi, own_i, fri, far_z, ysi, yri, by_w, ws_at)
    qt = regroup(qt, own_t, frt, far_w, yst, yrt, by_z, zs_at)
    oi_ref[:, 0:256] = last_sum(qi, ysi, yri, by_w)[0:18]
    out = last_sum(qt, yst, yrt, by_z)
    ot_ref[:, 0:256] = out[0:18, 0:256]
    oi_ref[:, 256:288] = out[0:18, 256:288]
    ot_ref[:, 256:288] = pltpu.roll(out[:, 256:384], 96, 1)[0:18, 0:32]
    for cp in started:
        cp.wait_send()


COPIES = 256


def local(image_feats, text_feats, image_proj, text_proj, log_temp, bias):
    total = image_feats.shape[0] * lax.axis_size("dp")
    vm = pltpu.VMEM
    out = jax.ShapeDtypeStruct((18, 288), F32)
    return pl.pallas_call(
        functools.partial(kernel, total),
        out_shape=(out, out),
        in_specs=[pl.BlockSpec(memory_space=pl.ANY)] * 4
        + [pl.BlockSpec(memory_space=pltpu.SMEM)] * 2,
        out_specs=(pl.BlockSpec(memory_space=vm), pl.BlockSpec(memory_space=vm)),
        scratch_shapes=[
            vm((2, 256, 1152), BF),
            vm((2, 288, 1152), BF),
            vm((3, 8, 144, 256), BF),
            vm((2, 4, 64, 384), BF),
            vm((2, 4, 64, 384), BF),
            vm((2, 64, 1152), F32),
            vm((2, 64, 128), F32),
            vm((4, 2, 4, 32, 1152), BF),
            vm((8, 2, 64, 1152), BF),
            vm((1024, 1024), BF),
            vm((4, 2, 4, 32, 1152), F32),
            vm((8, 2, 64, 1152), F32),
            vm((3, 2, 4, 32, 1152), BF),
            vm((3, 2, 4, 32, 1152), BF),
            vm((2, 3, 32, 1152), BF),
            vm((2, 32, 1152), F32),
            vm((2, 3, 32, 1152), BF),
            vm((8, 64, 1152), F32),
            vm((8, 64, 1152), BF),
            vm((64, 1152), BF),
            vm((3, 64, 1152), BF),
            vm((3, 64, 1152), BF),
            vm((2, 4, 64, 384), BF),
            vm((2, 4, 64, 384), BF),
            vm((8, 144, 256), BF),
            vm((8, 144, 256), BF),
            vm((8, 144, 384), BF),
            vm((8, 144, 384), BF),
            vm((8, 24, 256), F32),
            vm((8, 24, 256), F32),
            vm((8, 24, 384), F32),
            vm((8, 24, 384), F32),
            pltpu.SemaphoreType.DMA((4,)),
            pltpu.SemaphoreType.DMA((COPIES,)),
            pltpu.SemaphoreType.DMA((COPIES,)),
        ],
        name="contrastive",
        compiler_params=pltpu.CompilerParams(
            collective_id=0, has_side_effects=True, vmem_limit_bytes=60 * 2**20
        ),
    )(image_feats, text_feats, image_proj.T, text_proj.T, log_temp, bias)


def solution(mesh):
    placed = (P("dp", None), P("dp", None), P(None, "mp"), P(None, "mp"), P(), P())
    return jax.shard_map(
        local, mesh=mesh, in_specs=placed, out_specs=(P("dp", "mp"), P("dp", "mp")), check_vma=False
    )
```

```python
import functools

import jax
import jax.numpy as jnp
from jax import lax
from jax.experimental import pallas as pl
from jax.experimental.pallas import tpu as pltpu
from jax.sharding import PartitionSpec as P

MESH = pl.DeviceIdType.MESH
F32, BF = jnp.float32, jnp.bfloat16
PIECE = 64
POS = {4: 0, 0: 1, 3: 2, 5: 3, 2: 4, 6: 5, 1: 6, 7: 7}


def dot(a, b):
    return jnp.dot(a, b, preferred_element_type=F32)


def dot_nt(a, b):
    return lax.dot_general(a, b, (((1,), (1,)), ((), ())), preferred_element_type=F32)


def dot_tn(a, b):
    return lax.dot_general(a, b, (((0,), (0,)), ((), ())), preferred_element_type=F32)


def kernel(total, fi_hbm, ft_hbm, wi_hbm, wt_hbm, lt_ref, bs_ref, oi_ref, ot_ref,
           feats, wts, featst, es, er, unit, scal, img, txt, prob, gi, gt,
           gib, ra, ra2, r4, sa, sab, gts, sibr, gtb, tr, zs, zr,
           fsi, fri, fst, frt, ysi, yri, yst, yrt,
           lsem, ssem, rsem):
    dp, mp = lax.axis_index("dp"), lax.axis_index("mp")
    z, xl, y = dp // 8, (dp // 4) % 2, dp % 4
    c = mp % 2
    x = (mp // 2) * 2 + xl

    def dev(xx, yy, zz, cc):
        return (zz * 8 + (xx % 2) * 4 + yy, (xx // 2) * 2 + cc)

    xp, x2, xm = (dev((x + k) % 4, y, z, c) for k in (1, 2, 3))
    yp, y2, ym = (dev(x, (y + k) % 4, z, c) for k in (1, 2, 3))
    zs_at = [dev(x, y, (z + k) % 8, c) for k in range(8)]
    zp, zm = zs_at[1], zs_at[7]
    ws_at = [(z * 8 + ((xl + k // 4) % 2) * 4 + (y + k) % 4, mp) for k in range(8)]
    sib = (dp, (mp // 2) * 2 + (1 - c))
    mps = [(dp, (mp + k) % 4) for k in (1, 2, 3)]

    barrier = pltpu.get_barrier_semaphore()
    greeted = mps + [xp, xm] + zs_at[1:] + ws_at[1:4] + ws_at[5:]
    for d in greeted:
        pl.semaphore_signal(barrier, inc=1, device_id=d, device_id_type=MESH)

    loads = []
    for k, (s, t) in enumerate(((fi_hbm, feats.at[0, 0:224]), (wi_hbm, wts.at[0]),
                                (ft_hbm, feats.at[1, 0:224]), (wt_hbm, wts.at[1]))):
        cp = pltpu.make_async_copy(s, t, lsem.at[k])
        cp.start()
        loads.append(cp)
    feats[:, 224:256, :] = jnp.zeros((2, 32, 1152), BF)

    started = []

    def send(src, dst, to):
        k = len(started)
        cp = pltpu.make_async_remote_copy(src_ref=src, dst_ref=dst, send_sem=ssem.at[k],
                                          recv_sem=rsem.at[k], device_id=to, device_id_type=MESH)
        cp.start()
        started.append(cp)
        return cp

    place = (lax.broadcasted_iota(jnp.int32, (32, 128), 1)
             == lax.broadcasted_iota(jnp.int32, (32, 128), 0) + 32 * mp).astype(F32).astype(BF)
    emb_in = [[], []]
    for m in (0, 1):
        loads[2 * m].wait()
        loads[2 * m + 1].wait()
        main = dot_nt(feats[m], wts[m, 0:256, :]).astype(BF)
        rest = dot_nt(feats[m], wts[m, 256:288, :]).astype(BF)
        rest = dot(rest, place).astype(BF)
        for q in range(4):
            es[m, q, :, 0:256] = main[64 * q:64 * q + 64]
            es[m, q, :, 256:384] = rest[64 * q:64 * q + 64]
        if m == 0:
            pl.semaphore_wait(barrier, len(greeted))
        for k in (1, 2, 3):
            emb_in[m].append(send(es.at[m, (mp + k) % 4], er.at[m, mp], mps[k - 1]))
        er[m, mp] = es[m, mp]

    def normalize(m):
        for cp in emb_in[m]:
            cp.wait_recv()
        rest = sum(er[m, q, :, 256:384].astype(F32) for q in range(4))
        wide = jnp.concatenate([er[m, q, :, 0:256].astype(F32) for q in range(4)] + [rest], axis=1)
        scale = lax.rsqrt(jnp.sum(wide * wide, axis=1, keepdims=True) + 1e-06)
        unit[m] = wide * scale
        scal[m] = jnp.broadcast_to(scale, (64, 128))
        return (wide * scale).astype(BF)

    A, B, A0, A1 = pl.ds(0, 32), pl.ds(32, 32), pl.ds(0, 16), pl.ds(16, 16)
    axis1 = ((xp, x2, xm), (yp, y2, ym))
    axis2 = ((yp, y2, ym), (xp, x2, xm))
    got = {}
    piece = normalize(0)
    img[0, 0, 0] = piece[0:32]
    img[0, 1, 0] = piece[32:64]
    for j in (1, 3, 2):
        for h in (0, 1):
            got[0, h, 4 - j] = send(img.at[0, h, 0], img.at[0, h, 4 - j], axis1[h][j - 1])

    def second(j):
        for h in (0, 1):
            got[3, h, j] = send(img.at[0, h, j], img.at[3, h, j], axis2[h][0])
            got[1, h, j] = send(img.at[0, h, j], img.at[1, h, j], axis2[h][2])

    def third(j):
        for h in (0, 1):
            got[3, h, j].wait_recv()
            got[4, h, j] = send(img.at[3, h, j, A0], img.at[2, h, j, A0], axis2[h][0])
            got[1, h, j].wait_recv()
            got[5, h, j] = send(img.at[1, h, j, A1], img.at[2, h, j, A1], axis2[h][2])

    second(0)
    txt[POS[0], 0] = normalize(1)
    tgot, sgot = {}, {}
    halves = (A, B)

    def text_send(src, dst, half, to):
        tgot[dst, half] = send(txt.at[POS[src], 0, halves[half]], txt.at[POS[dst], 0, halves[half]], to)

    def text_share(*slots):
        for k in slots:
            sgot[k] = send(txt.at[POS[k], 0], txt.at[POS[k], 1], sib)

    def text_shared(*slots):
        for k in slots:
            sgot[k].wait_recv()

    def text_hop(k):
        for turn in (0, 1):
            for src, nxt, to, lead in ((8 - k, 7 - k, zp, 0), (k, k + 1, zm, 1)):
                half = (lead + turn) % 2
                tgot[src, half].wait_recv()
                if k < 3 or turn == 0:
                    text_send(src, nxt, half, to)
        text_share(8 - k, k)

    text_send(0, 7, 0, zp)
    text_send(0, 1, 1, zm)
    text_send(0, 7, 1, zp)
    text_send(0, 1, 0, zm)
    text_share(0)
    temp = jnp.exp(jnp.full((1, 1), lt_ref[0], F32))
    shift = jnp.full((1, 1), bs_ref[0], F32)
    gain = temp * (1.0 / total)

    def scores(k, n):
        at = pl.ds(2 * n, 2)
        logits = temp * dot_nt(img[k].reshape(256, 1152), txt[at].reshape(256, 1152)) + shift
        cols = pl.ds(pl.multiple_of(256 * n, 256), 256)
        prob[256 * k:256 * k + 256, cols] = (gain / (1.0 + jnp.exp(-logits))).astype(BF)
        return logits

    def some_scores(k, count):
        def one(i, _):
            scores(k, 3 - i)
            return 0
        lax.fori_loop(0, count, one, 0)

    sent = {}

    def image_block(k):
        gi[k] = dot(prob[256 * k:256 * k + 256, :],
                    txt[...].reshape(1024, 1152)).reshape(2, 4, 32, 1152)

    def text_block(n):
        gt[2 * n:2 * n + 2] = dot_tn(prob[:, 256 * n:256 * n + 256],
                                     img[...].reshape(1024, 1152)).reshape(2, 2, 64, 1152)
        gts[n] = gt[2 * n:2 * n + 2, 1].astype(BF)
        return send(gts.at[n], sibr.at[n], sib)

    def text_own(k):
        return gt[POS[k], 0] + sibr[POS[k] // 2, POS[k] % 2].astype(F32)

    def text_on(k, half):
        at = halves[half]
        part = gt[POS[k], 0, at] + sibr[POS[k] // 2, POS[k] % 2, at].astype(F32)
        back_k = k + 1 if k < 4 else k - 1
        if k != 4 and (back_k != 4 or half == (0 if k == 3 else 1)):
            sent[back_k, half].wait_recv()
            part = part + tr[back_k, at].astype(F32)
        gtb[k, at] = part.astype(BF)
        to = zp if k < 4 or (k == 4 and half == 0) else zm
        sent[k, half] = send(gtb.at[k, at], tr.at[k, at], to)

    for j in (1, 3):
        got[0, 0, j].wait_recv()
        got[0, 1, j].wait_recv()
        second(j)
    text_hop(1)
    got[0, 0, 2].wait_recv()
    got[0, 1, 2].wait_recv()
    second(2)
    third(0)
    text_hop(2)
    text_shared(1, 7)
    scores(0, 3)
    third(1)
    third(3)
    text_hop(3)
    text_shared(2, 6)
    scores(0, 2)
    third(2)

    def two_scores(k):
        def one(i, _):
            scores(k, 3 - i)
            return 0
        lax.fori_loop(0, 2, one, 0)

    two_scores(1)
    tgot[4, 0].wait_recv()
    tgot[4, 1].wait_recv()
    text_share(4)
    two_scores(3)
    text_shared(3, 5, 0)
    for k in (1, 3, 0):
        scores(k, 1)
    text_shared(4)
    scores(1, 0)
    scores(3, 0)
    logits = scores(0, 0)
    r0 = lax.broadcasted_iota(jnp.int32, (32, 128), 0)
    r1 = lax.broadcasted_iota(jnp.int32, (32, 128), 1)
    for h in (0, 1):
        own = logits[128 * h:128 * h + 32, 128:256]
        prob[128 * h:128 * h + 32, 128:256] = jnp.where(
            r1 == r0 + 32 * h, -gain / (1.0 + jnp.exp(own)), gain / (1.0 + jnp.exp(-own))).astype(BF)

    for j in range(4):
        for h in (0, 1):
            got[4, h, j].wait_recv()
            got[5, h, j].wait_recv()
    some_scores(2, 4)
    image_block(2)
    gib[1] = gi[2].astype(BF)
    q4 = [[send(gib.at[1, h, :, A0], r4.at[h, :, A0], axis2[h][0]),
           send(gib.at[1, h, :, A1], r4.at[h, :, A1], axis2[h][2])] for h in (0, 1)]
    q0 = text_block(0)
    image_block(1)
    image_block(3)
    for h in (0, 1):
        gib[0, h, :, A1] = gi[1, h, :, A1].astype(BF)
        gib[2, h, :, A0] = gi[3, h, :, A0].astype(BF)
    q1 = text_block(1)
    q0.wait_recv()
    text_on(4, 0)
    text_on(4, 1)
    q1.wait_recv()
    text_on(3, 1)
    text_on(5, 0)
    qa = [[], []]
    for h in (0, 1):
        for cp in q4[h]:
            cp.wait_recv()
        gib[0, h, :, A0] = (gi[1, h, :, A0] + r4[h, :, A0].astype(F32)).astype(BF)
        gib[2, h, :, A1] = (gi[3, h, :, A1] + r4[h, :, A1].astype(F32)).astype(BF)
        for i in (0, 1):
            qa[h].append(send(gib.at[2 * i, h], ra.at[i, h], axis2[h][2 * i]))
    q2 = text_block(2)
    q3 = text_block(3)
    text_on(3, 0)
    text_on(5, 1)
    image_block(0)
    q2.wait_recv()
    text_on(2, 1)
    text_on(6, 0)
    text_on(2, 0)
    text_on(6, 1)
    q3.wait_recv()
    text_on(1, 1)
    text_on(7, 0)
    qa2 = []
    for h in (0, 1):
        for cp in qa[h]:
            cp.wait_recv()
        for j in (2, 1, 3, 0):
            part = gi[0, h, j] + ra[0, h, j].astype(F32) + ra[1, h, j].astype(F32)
            if j:
                sab[h, j - 1] = part.astype(BF)
                qa2.append(send(sab.at[h, j - 1], ra2.at[h, j - 1], axis1[h][j - 1]))
            else:
                sa[h] = part
    text_on(1, 0)
    text_on(7, 1)

    def back(m, dx):
        inner = jnp.sum(unit[m] * dx, axis=1, keepdims=True)
        dz = (scal[m][:, 0:1] * (dx - unit[m] * inner)).astype(BF)
        for q in range(4):
            zs[m, q, :, 0:256] = dz[:, 256 * q:256 * q + 256]
            zs[m, q, :, 256:384] = dz[:, 1024:1152]
        zr[m, mp] = zs[m, mp]
        return [send(zs.at[m, (mp + k) % 4], zr.at[m, mp], mps[k - 1]) for k in (1, 2, 3)]

    for k in (1, 7):
        for half in (0, 1):
            sent[k, half].wait_recv()
    zt_in = back(1, text_own(0) + tr[1].astype(F32) + tr[7].astype(F32))
    for cp in qa2:
        cp.wait_recv()
    zi_in = back(0, jnp.concatenate(
        [sa[h] + ra2[h, 0].astype(F32) + ra2[h, 1].astype(F32) + ra2[h, 2].astype(F32)
         for h in (0, 1)], axis=0))

    wide_t = jnp.transpose(feats[0])
    for k in range(8):
        featst[0, k] = wide_t[144 * k:144 * k + 144]
    p0 = lax.broadcasted_iota(jnp.int32, (144, 1152), 0)
    at_z = p0 + 126 * ((p0 * 3641) >> 16)
    p1 = lax.broadcasted_iota(jnp.int32, (144, 1152), 1)

    def turn(w, _):
        turned = (p1 == at_z + 18 * w).astype(F32).astype(BF)
        featst[1, w] = dot_nt(turned, feats[1]).astype(BF)
        featst[2, w] = dot_nt(turned, feats[0]).astype(BF)
        return 0
    lax.fori_loop(0, 8, turn, 0)


    far_z, far_w = (4, 3, 5, 2, 6, 1, 7), (6, 2, 5, 7, 1, 3, 4)
    l0 = lax.broadcasted_iota(jnp.int32, (128, 128), 0)
    l1 = lax.broadcasted_iota(jnp.int32, (128, 128), 1)

    def by_z(k):
        return (z + k) % 8

    def by_w(k):
        return ((xl + k // 4) % 2) * 4 + (y + k) % 4

    def columns(m, arrived):
        for cp in arrived:
            cp.wait_recv()
        pick = ((l0 + 32 * m == l1 + 32 * mp) & (l1 >= 32 * m) & (l1 < 32 * m + 32)).astype(F32).astype(BF)
        rest = jnp.concatenate([zr[m, q, :, 256:384] for q in range(4)], axis=0)
        return (jnp.concatenate([zr[m, q, :, 0:256] for q in range(4)], axis=0),
                dot(rest, pick).astype(BF))

    def spread(st, rc, far, make, at):
        q = []
        for k in far:
            st[k] = make(k).astype(BF)
            q.append(send(st.at[k], rc.at[k], at[k]))
        return q

    def regroup(q, own, rc, far, ys, yr, base, at):
        for cp in q:
            cp.wait_recv()
        for k in far:
            own = own + rc[k].astype(F32)
        for k in range(8):
            ys[k, 0:18] = own[18 * k:18 * k + 18].astype(BF)
        return [send(ys.at[base(k)], yr.at[k], at[k]) for k in far]

    def last_sum(q, ys, yr, base):
        for cp in q:
            cp.wait_recv()
        out = ys[base(0)].astype(F32)
        for k in range(1, 8):
            out = out + yr[k].astype(F32)
        return out

    main_i, rest_i = columns(0, zi_in)

    def make_i(k):
        return dot(featst[0, by_z(k)], main_i)

    qi = spread(fsi, fri, far_z, make_i, zs_at)
    own_i = make_i(0)
    main_t, rest_t = columns(1, zt_in)

    def make_t(k):
        a, b = featst[1, by_w(k)], featst[2, by_w(k)]
        return jnp.concatenate([dot(a, main_t), dot(a, rest_t) + dot(b, rest_i)], axis=1)

    qt = spread(fst, frt, far_w, make_t, ws_at)
    own_t = make_t(0)
    qi = regroup(qi, own_i, fri, far_z, ysi, yri, by_w, ws_at)
    qt = regroup(qt, own_t, frt, far_w, yst, yrt, by_z, zs_at)
    oi_ref[:, 0:256] = last_sum(qi, ysi, yri, by_w)[0:18]
    out = last_sum(qt, yst, yrt, by_z)
    ot_ref[:, 0:256] = out[0:18, 0:256]
    oi_ref[:, 256:288] = out[0:18, 256:288]
    ot_ref[:, 256:288] = pltpu.roll(out[:, 256:384], 96, 1)[0:18, 0:32]
    for cp in started:
        cp.wait_send()


COPIES = 256


def local(image_feats, text_feats, image_proj, text_proj, log_temp, bias):
    total = image_feats.shape[0] * lax.axis_size("dp")
    vm = pltpu.VMEM
    out = jax.ShapeDtypeStruct((18, 288), F32)
    return pl.pallas_call(
        functools.partial(kernel, total),
        out_shape=(out, out),
        in_specs=[pl.BlockSpec(memory_space=pl.ANY)] * 4
        + [pl.BlockSpec(memory_space=pltpu.SMEM)] * 2,
        out_specs=(pl.BlockSpec(memory_space=vm), pl.BlockSpec(memory_space=vm)),
        scratch_shapes=[
            vm((2, 256, 1152), BF),
            vm((2, 288, 1152), BF),
            vm((3, 8, 144, 256), BF),
            vm((2, 4, 64, 384), BF),
            vm((2, 4, 64, 384), BF),
            vm((2, 64, 1152), F32),
            vm((2, 64, 128), F32),
            vm((4, 2, 4, 32, 1152), BF),
            vm((8, 2, 64, 1152), BF),
            vm((1024, 1024), BF),
            vm((4, 2, 4, 32, 1152), F32),
            vm((8, 2, 64, 1152), F32),
            vm((3, 2, 4, 32, 1152), BF),
            vm((2, 2, 4, 32, 1152), BF),
            vm((2, 3, 32, 1152), BF),
            vm((2, 4, 32, 1152), BF),
            vm((2, 32, 1152), F32),
            vm((2, 3, 32, 1152), BF),
            vm((4, 2, 64, 1152), BF),
            vm((4, 2, 64, 1152), BF),
            vm((8, 64, 1152), BF),
            vm((8, 64, 1152), BF),
            vm((2, 4, 64, 384), BF),
            vm((2, 4, 64, 384), BF),
            vm((8, 144, 256), BF),
            vm((8, 144, 256), BF),
            vm((8, 144, 384), BF),
            vm((8, 144, 384), BF),
            vm((8, 32, 256), BF),
            vm((8, 32, 256), BF),
            vm((8, 32, 384), BF),
            vm((8, 32, 384), BF),
            pltpu.SemaphoreType.DMA((4,)),
            pltpu.SemaphoreType.DMA((COPIES,)),
            pltpu.SemaphoreType.DMA((COPIES,)),
        ],
        name="contrastive",
        compiler_params=pltpu.CompilerParams(
            collective_id=0, has_side_effects=True, vmem_limit_bytes=60 * 2**20
        ),
    )(image_feats, text_feats, image_proj.T, text_proj.T, log_temp, bias)


def solution(mesh):
    placed = (P("dp", None), P("dp", None), P(None, "mp"), P(None, "mp"), P(), P())
    return jax.shard_map(
        local, mesh=mesh, in_specs=placed, out_specs=(P("dp", "mp"), P("dp", "mp")), check_vma=False
    )
```

```python
import functools

import jax
import jax.numpy as jnp
from jax import lax
from jax.experimental import pallas as pl
from jax.experimental.pallas import tpu as pltpu
from jax.sharding import PartitionSpec as P

MESH = pl.DeviceIdType.MESH
F32, BF = jnp.float32, jnp.bfloat16
PIECE = 64
POS = {4: 0, 0: 1, 3: 2, 5: 3, 2: 4, 6: 5, 1: 6, 7: 7}


def dot(a, b):
    return jnp.dot(a, b, preferred_element_type=F32)


def dot_nt(a, b):
    return lax.dot_general(a, b, (((1,), (1,)), ((), ())), preferred_element_type=F32)


def dot_tn(a, b):
    return lax.dot_general(a, b, (((0,), (0,)), ((), ())), preferred_element_type=F32)


def kernel(total, fi_hbm, ft_hbm, wi_hbm, wt_hbm, lt_ref, bs_ref, oi_ref, ot_ref,
           feats, wts, featst, es, er, unit, scal, img, txt, prob, gi, gt,
           gib, ra, ra2, r4, sa, sab, gts, sibr, gtb, tr, zs, zr,
           fsi, fri, fst, frt, fsr, frr, ysi, yri, yst, yrt,
           lsem, ssem, rsem):
    dp, mp = lax.axis_index("dp"), lax.axis_index("mp")
    z, xl, y = dp // 8, (dp // 4) % 2, dp % 4
    c = mp % 2
    x = (mp // 2) * 2 + xl

    def dev(xx, yy, zz, cc):
        return (zz * 8 + (xx % 2) * 4 + yy, (xx // 2) * 2 + cc)

    xp, x2, xm = (dev((x + k) % 4, y, z, c) for k in (1, 2, 3))
    yp, y2, ym = (dev(x, (y + k) % 4, z, c) for k in (1, 2, 3))
    zs_at = [dev(x, y, (z + k) % 8, c) for k in range(8)]
    zp, zm = zs_at[1], zs_at[7]
    ws_at = [(z * 8 + ((xl + k // 4) % 2) * 4 + (y + k) % 4, mp) for k in range(8)]
    sib = (dp, (mp // 2) * 2 + (1 - c))
    mps = [(dp, (mp + k) % 4) for k in (1, 2, 3)]

    barrier = pltpu.get_barrier_semaphore()
    greeted = mps + [xp, xm] + zs_at[1:] + ws_at[1:4] + ws_at[5:]
    for d in greeted:
        pl.semaphore_signal(barrier, inc=1, device_id=d, device_id_type=MESH)

    loads = []
    for k, (s, t) in enumerate(((fi_hbm, feats.at[0, 0:224]), (wi_hbm, wts.at[0]),
                                (ft_hbm, feats.at[1, 0:224]), (wt_hbm, wts.at[1]))):
        cp = pltpu.make_async_copy(s, t, lsem.at[k])
        cp.start()
        loads.append(cp)
    feats[:, 224:256, :] = jnp.zeros((2, 32, 1152), BF)

    started = []

    def send(src, dst, to):
        k = len(started)
        cp = pltpu.make_async_remote_copy(src_ref=src, dst_ref=dst, send_sem=ssem.at[k],
                                          recv_sem=rsem.at[k], device_id=to, device_id_type=MESH)
        cp.start()
        started.append(cp)
        return cp

    place = (lax.broadcasted_iota(jnp.int32, (32, 128), 1)
             == lax.broadcasted_iota(jnp.int32, (32, 128), 0) + 32 * mp).astype(F32).astype(BF)
    emb_in = [[], []]
    for m in (0, 1):
        loads[2 * m].wait()
        loads[2 * m + 1].wait()
        main = dot_nt(feats[m], wts[m, 0:256, :]).astype(BF)
        rest = dot_nt(feats[m], wts[m, 256:288, :]).astype(BF)
        rest = dot(rest, place).astype(BF)
        for q in range(4):
            es[m, q, :, 0:256] = main[64 * q:64 * q + 64]
            es[m, q, :, 256:384] = rest[64 * q:64 * q + 64]
        if m == 0:
            pl.semaphore_wait(barrier, len(greeted))
        for k in (1, 2, 3):
            emb_in[m].append(send(es.at[m, (mp + k) % 4], er.at[m, mp], mps[k - 1]))
        er[m, mp] = es[m, mp]

    def normalize(m):
        for cp in emb_in[m]:
            cp.wait_recv()
        rest = sum(er[m, q, :, 256:384].astype(F32) for q in range(4))
        wide = jnp.concatenate([er[m, q, :, 0:256].astype(F32) for q in range(4)] + [rest], axis=1)
        scale = lax.rsqrt(jnp.sum(wide * wide, axis=1, keepdims=True) + 1e-06)
        unit[m] = wide * scale
        scal[m] = jnp.broadcast_to(scale, (64, 128))
        return (wide * scale).astype(BF)

    A, B, A0, A1 = pl.ds(0, 32), pl.ds(32, 32), pl.ds(0, 16), pl.ds(16, 16)
    axis1 = ((xp, x2, xm), (yp, y2, ym))
    axis2 = ((yp, y2, ym), (xp, x2, xm))
    got = {}
    piece = normalize(0)
    img[0, 0, 0] = piece[0:32]
    img[0, 1, 0] = piece[32:64]
    for j in (1, 3, 2):
        for h in (0, 1):
            got[0, h, 4 - j] = send(img.at[0, h, 0], img.at[0, h, 4 - j], axis1[h][j - 1])

    def second(j):
        for h in (0, 1):
            got[3, h, j] = send(img.at[0, h, j], img.at[3, h, j], axis2[h][0])
            got[1, h, j] = send(img.at[0, h, j], img.at[1, h, j], axis2[h][2])

    def third(j):
        for h in (0, 1):
            got[3, h, j].wait_recv()
            got[4, h, j] = send(img.at[3, h, j, A0], img.at[2, h, j, A0], axis2[h][0])
            got[1, h, j].wait_recv()
            got[5, h, j] = send(img.at[1, h, j, A1], img.at[2, h, j, A1], axis2[h][2])

    second(0)
    txt[POS[0], 0] = normalize(1)
    tgot, sgot = {}, {}
    halves = (A, B)

    def text_send(src, dst, half, to):
        tgot[dst, half] = send(txt.at[POS[src], 0, halves[half]], txt.at[POS[dst], 0, halves[half]], to)

    def text_share(*slots):
        for k in slots:
            sgot[k] = send(txt.at[POS[k], 0], txt.at[POS[k], 1], sib)

    def text_shared(*slots):
        for k in slots:
            sgot[k].wait_recv()

    def text_hop(k, turns=(0, 1)):
        for turn in turns:
            for src, nxt, to, lead in ((8 - k, 7 - k, zp, 0), (k, k + 1, zm, 1)):
                half = (lead + turn) % 2
                tgot[src, half].wait_recv()
                if k < 3 or turn == 0:
                    text_send(src, nxt, half, to)
        if turns[-1]:
            text_share(8 - k, k)

    text_send(0, 7, 0, zp)
    text_send(0, 1, 1, zm)
    text_send(0, 7, 1, zp)
    text_send(0, 1, 0, zm)
    text_share(0)
    temp = jnp.exp(jnp.full((1, 1), lt_ref[0], F32))
    shift = jnp.full((1, 1), bs_ref[0], F32)
    gain = temp * (1.0 / total)

    def scores(k, n):
        at = pl.ds(2 * n, 2)
        logits = temp * dot_nt(img[k].reshape(256, 1152), txt[at].reshape(256, 1152)) + shift
        cols = pl.ds(pl.multiple_of(256 * n, 256), 256)
        prob[256 * k:256 * k + 256, cols] = (gain / (1.0 + jnp.exp(-logits))).astype(BF)
        return logits

    def some_scores(k, count):
        def one(i, _):
            scores(k, 3 - i)
            return 0
        lax.fori_loop(0, count, one, 0)

    sent = {}

    def image_block(k):
        gi[k] = dot(prob[256 * k:256 * k + 256, :],
                    txt[...].reshape(1024, 1152)).reshape(2, 4, 32, 1152)

    def text_block(n):
        gt[2 * n:2 * n + 2] = dot_tn(prob[:, 256 * n:256 * n + 256],
                                     img[...].reshape(1024, 1152)).reshape(2, 2, 64, 1152)
        gts[n] = gt[2 * n:2 * n + 2, 1].astype(BF)
        return send(gts.at[n], sibr.at[n], sib)

    def text_own(k):
        return gt[POS[k], 0] + sibr[POS[k] // 2, POS[k] % 2].astype(F32)

    def text_on(k, half):
        at = halves[half]
        part = gt[POS[k], 0, at] + sibr[POS[k] // 2, POS[k] % 2, at].astype(F32)
        back_k = k + 1 if k < 4 else k - 1
        if k != 4 and (back_k != 4 or half == (0 if k == 3 else 1)):
            sent[back_k, half].wait_recv()
            part = part + tr[back_k, at].astype(F32)
        gtb[k, at] = part.astype(BF)
        to = zp if k < 4 or (k == 4 and half == 0) else zm
        sent[k, half] = send(gtb.at[k, at], tr.at[k, at], to)

    for j in (1, 3):
        got[0, 0, j].wait_recv()
        got[0, 1, j].wait_recv()
        second(j)
    text_hop(1)
    got[0, 0, 2].wait_recv()
    got[0, 1, 2].wait_recv()
    second(2)
    third(0)
    text_hop(2)
    text_shared(1, 7)
    scores(0, 3)
    third(1)
    third(3)
    text_shared(2, 6)
    scores(0, 2)
    third(2)
    text_hop(3, (0,))

    def two_scores(k):
        def one(i, _):
            scores(k, 3 - i)
            return 0
        lax.fori_loop(0, 2, one, 0)

    two_scores(1)
    text_hop(3, (1,))
    two_scores(3)
    tgot[4, 0].wait_recv()
    tgot[4, 1].wait_recv()
    text_share(4)
    text_shared(3, 5, 0)
    for k in (1, 3, 0):
        scores(k, 1)
    text_shared(4)
    scores(1, 0)
    scores(3, 0)
    logits = scores(0, 0)
    r0 = lax.broadcasted_iota(jnp.int32, (32, 128), 0)
    r1 = lax.broadcasted_iota(jnp.int32, (32, 128), 1)
    for h in (0, 1):
        own = logits[128 * h:128 * h + 32, 128:256]
        prob[128 * h:128 * h + 32, 128:256] = jnp.where(
            r1 == r0 + 32 * h, -gain / (1.0 + jnp.exp(own)), gain / (1.0 + jnp.exp(-own))).astype(BF)

    for j in range(4):
        for h in (0, 1):
            got[4, h, j].wait_recv()
            got[5, h, j].wait_recv()
    some_scores(2, 4)
    q0 = text_block(0)
    image_block(2)
    gib[1] = gi[2].astype(BF)
    pairs = (pl.ds(2, 2), pl.ds(0, 2))
    q4 = [[[send(gib.at[1, h, p, A0], r4.at[h, p, A0], axis2[h][0]),
            send(gib.at[1, h, p, A1], r4.at[h, p, A1], axis2[h][2])] for h in (0, 1)] for p in pairs]
    q1 = text_block(1)
    q0.wait_recv()
    text_on(4, 0)
    text_on(4, 1)
    image_block(1)
    for h in (0, 1):
        gib[0, h, :, A1] = gi[1, h, :, A1].astype(BF)
    q1.wait_recv()
    text_on(3, 1)
    text_on(5, 0)
    image_block(3)
    for h in (0, 1):
        gib[2, h, :, A0] = gi[3, h, :, A0].astype(BF)
    qa = [[], []]

    def image_on(n):
        p = pairs[n]
        for h in (0, 1):
            for cp in q4[n][h]:
                cp.wait_recv()
            gib[0, h, p, A0] = (gi[1, h, p, A0] + r4[h, p, A0].astype(F32)).astype(BF)
            gib[2, h, p, A1] = (gi[3, h, p, A1] + r4[h, p, A1].astype(F32)).astype(BF)
            for i in (0, 1):
                qa[n].append(send(gib.at[2 * i, h, p], ra.at[i, h, p], axis2[h][2 * i]))

    qa2 = []

    def image_first(n):
        for cp in qa[n]:
            cp.wait_recv()
        for j in (2, 3) if n == 0 else (1, 0):
            for h in (0, 1):
                part = gi[0, h, j] + ra[0, h, j].astype(F32) + ra[1, h, j].astype(F32)
                if j:
                    sab[h, j - 1] = part.astype(BF)
                    qa2.append(send(sab.at[h, j - 1], ra2.at[h, j - 1], axis1[h][j - 1]))
                else:
                    sa[h] = part

    image_on(0)
    q2 = text_block(2)
    text_on(3, 0)
    text_on(5, 1)
    image_on(1)
    q3 = text_block(3)
    image_block(0)
    q2.wait_recv()
    text_on(2, 1)
    text_on(6, 0)
    text_on(2, 0)
    text_on(6, 1)
    image_first(0)
    q3.wait_recv()
    text_on(1, 1)
    text_on(7, 0)
    image_first(1)
    text_on(1, 0)
    text_on(7, 1)

    def back(m, dx):
        inner = jnp.sum(unit[m] * dx, axis=1, keepdims=True)
        dz = (scal[m][:, 0:1] * (dx - unit[m] * inner)).astype(BF)
        for q in range(4):
            zs[m, q, :, 0:256] = dz[:, 256 * q:256 * q + 256]
            zs[m, q, :, 256:384] = dz[:, 1024:1152]
        zr[m, mp] = zs[m, mp]
        return [send(zs.at[m, (mp + k) % 4], zr.at[m, mp], mps[k - 1]) for k in (1, 2, 3)]

    for k in (1, 7):
        for half in (0, 1):
            sent[k, half].wait_recv()
    zt_in = back(1, text_own(0) + tr[1].astype(F32) + tr[7].astype(F32))
    for cp in qa2:
        cp.wait_recv()
    zi_in = back(0, jnp.concatenate(
        [sa[h] + ra2[h, 0].astype(F32) + ra2[h, 1].astype(F32) + ra2[h, 2].astype(F32)
         for h in (0, 1)], axis=0))

    wide_t = jnp.transpose(feats[0])
    for k in range(8):
        featst[0, k] = wide_t[144 * k:144 * k + 144]
    p0 = lax.broadcasted_iota(jnp.int32, (144, 1152), 0)
    at_z = p0 + 126 * ((p0 * 3641) >> 16)
    p1 = lax.broadcasted_iota(jnp.int32, (144, 1152), 1)

    def turn(w, _):
        turned = (p1 == at_z + 18 * w).astype(F32).astype(BF)
        featst[1, w] = dot_nt(turned, feats[1]).astype(BF)
        featst[2, w] = dot_nt(turned, feats[0]).astype(BF)
        return 0
    lax.fori_loop(0, 8, turn, 0)


    far_z, far_w = (4, 3, 5, 2, 6, 1, 7), (6, 2, 5, 7, 1, 3, 4)
    l0 = lax.broadcasted_iota(jnp.int32, (128, 128), 0)
    l1 = lax.broadcasted_iota(jnp.int32, (128, 128), 1)

    def by_z(k):
        return (z + k) % 8

    def by_w(k):
        return ((xl + k // 4) % 2) * 4 + (y + k) % 4

    def columns(m, arrived):
        for cp in arrived:
            cp.wait_recv()
        pick = ((l0 + 32 * m == l1 + 32 * mp) & (l1 >= 32 * m) & (l1 < 32 * m + 32)).astype(F32).astype(BF)
        rest = jnp.concatenate([zr[m, q, :, 256:384] for q in range(4)], axis=0)
        return (jnp.concatenate([zr[m, q, :, 0:256] for q in range(4)], axis=0),
                dot(rest, pick).astype(BF))

    def regroup(q, own, rc, near, far, ys, yr, base, at):
        for cp in q:
            cp.wait_recv()
        for k in near:
            own = own + rc[k].astype(F32)
        cols = own.shape[1]
        for k in range(8):
            ys[k, :, 0:cols] = own[18 * k:18 * k + 16].astype(BF)
            tail = [own[18 * k + r:18 * k + r + 1, i:i + 128] for r in (16, 17) for i in range(0, cols, 128)]
            tail.append(jnp.zeros((16 - len(tail), 128), F32))
            ys[k, :, cols:cols + 128] = jnp.concatenate(tail, axis=0).astype(BF)
        return [send(ys.at[base(k)], yr.at[k], at[k]) for k in far]

    def last_sum(q, ys, yr, base):
        for cp in q:
            cp.wait_recv()
        out = ys[base(0)].astype(F32)
        for k in range(1, 8):
            out = out + yr[k].astype(F32)
        cols = out.shape[1] - 128
        n = cols // 128
        tail = [jnp.concatenate([out[r * n + i:r * n + i + 1, cols:] for i in range(n)], axis=1) for r in (0, 1)]
        return jnp.concatenate([out[:, 0:cols]] + tail, axis=0)

    main_i, rest_i = columns(0, zi_in)
    main_t, rest_t = columns(1, zt_in)

    def make_t(k):
        a, b = featst[1, by_w(k)], featst[2, by_w(k)]
        rest = dot(a, rest_t) + dot(b, rest_i)
        return dot(a, main_t), rest[0:72] + pltpu.roll(rest[72:144], 64, 1)

    qt = []
    for k in far_w:
        part, rest = make_t(k)
        fst[k] = part.astype(BF)
        fsr[k, 0:72] = rest.astype(BF)
        qt.append(send(fst.at[k], frt.at[k], ws_at[k]))
        qt.append(send(fsr.at[k], frr.at[k], ws_at[k]))
    own_t, own_r = make_t(0)


    def make_i(k):
        return dot(featst[0, by_z(k)], main_i)

    H0, H1 = pl.ds(0, 80), pl.ds(80, 64)
    fsi[4] = make_i(4).astype(BF)
    qi4 = [send(fsi.at[4, H0], fri.at[4, H0], zs_at[2]), send(fsi.at[4, H1], fri.at[4, H1], zs_at[6])]
    qi3, qi = [], []
    for k, q in ((3, qi3), (5, qi3), (1, qi), (7, qi)):
        fsi[k] = make_i(k).astype(BF)
        q.append(send(fsi.at[k], fri.at[k], zp if k < 4 else zm))
    own_2, own_6 = make_i(2), make_i(6)
    own_i = make_i(0)
    for k, part, via, half in ((2, own_2, 3, 0), (6, own_6, 5, 1)):
        qi3[half].wait_recv()
        part = part + fri[via].astype(F32)
        qi4[half].wait_recv()
        if half == 0:
            fsi[k, H0] = (part[0:80] + fri[4, H0].astype(F32)).astype(BF)
            fsi[k, H1] = part[80:144].astype(BF)
        else:
            fsi[k, H0] = part[0:80].astype(BF)
            fsi[k, H1] = (part[80:144] + fri[4, H1].astype(F32)).astype(BF)
        qi.append(send(fsi.at[k], fri.at[k], zs_at[k]))
    for cp in qt:
        cp.wait_recv()
    for k in far_w:
        own_r = own_r + frr[k, 0:72].astype(F32)
        own_t = own_t + frt[k].astype(F32)
    own_t = jnp.concatenate([own_t, jnp.concatenate([own_r, pltpu.roll(own_r, 64, 1)], axis=0)], axis=1)
    qt = regroup([], own_t, frt, (), far_z, yst, yrt, by_z, zs_at)
    qi = regroup(qi, own_i, fri, (1, 7, 2, 6), far_w, ysi, yri, by_w, ws_at)
    oi_ref[:, 0:256] = last_sum(qi, ysi, yri, by_w)
    out = last_sum(qt, yst, yrt, by_z)
    ot_ref[:, 0:256] = out[:, 0:256]
    oi_ref[:, 256:288] = out[:, 256:288]
    ot_ref[:, 256:288] = pltpu.roll(out[:, 256:384], 96, 1)[:, 0:32]
    for cp in started:
        cp.wait_send()


COPIES = 256


def local(image_feats, text_feats, image_proj, text_proj, log_temp, bias):
    total = image_feats.shape[0] * lax.axis_size("dp")
    vm = pltpu.VMEM
    out = jax.ShapeDtypeStruct((18, 288), F32)
    return pl.pallas_call(
        functools.partial(kernel, total),
        out_shape=(out, out),
        in_specs=[pl.BlockSpec(memory_space=pl.ANY)] * 4
        + [pl.BlockSpec(memory_space=pltpu.SMEM)] * 2,
        out_specs=(pl.BlockSpec(memory_space=vm), pl.BlockSpec(memory_space=vm)),
        scratch_shapes=[
            vm((2, 256, 1152), BF),
            vm((2, 288, 1152), BF),
            vm((3, 8, 144, 256), BF),
            vm((2, 4, 64, 384), BF),
            vm((2, 4, 64, 384), BF),
            vm((2, 64, 1152), F32),
            vm((2, 64, 128), F32),
            vm((4, 2, 4, 32, 1152), BF),
            vm((8, 2, 64, 1152), BF),
            vm((1024, 1024), BF),
            vm((4, 2, 4, 32, 1152), F32),
            vm((8, 2, 64, 1152), F32),
            vm((3, 2, 4, 32, 1152), BF),
            vm((2, 2, 4, 32, 1152), BF),
            vm((2, 3, 32, 1152), BF),
            vm((2, 4, 32, 1152), BF),
            vm((2, 32, 1152), F32),
            vm((2, 3, 32, 1152), BF),
            vm((4, 2, 64, 1152), BF),
            vm((4, 2, 64, 1152), BF),
            vm((8, 64, 1152), BF),
            vm((8, 64, 1152), BF),
            vm((2, 4, 64, 384), BF),
            vm((2, 4, 64, 384), BF),
            vm((8, 144, 256), BF),
            vm((8, 144, 256), BF),
            vm((8, 144, 256), BF),
            vm((8, 144, 256), BF),
            vm((8, 80, 128), BF),
            vm((8, 80, 128), BF),
            vm((8, 16, 384), BF),
            vm((8, 16, 384), BF),
            vm((8, 16, 512), BF),
            vm((8, 16, 512), BF),
            pltpu.SemaphoreType.DMA((4,)),
            pltpu.SemaphoreType.DMA((COPIES,)),
            pltpu.SemaphoreType.DMA((COPIES,)),
        ],
        name="contrastive",
        compiler_params=pltpu.CompilerParams(
            collective_id=0, has_side_effects=True, vmem_limit_bytes=60 * 2**20
        ),
    )(image_feats, text_feats, image_proj.T, text_proj.T, log_temp, bias)


def solution(mesh):
    placed = (P("dp", None), P("dp", None), P(None, "mp"), P(None, "mp"), P(), P())
    return jax.shard_map(
        local, mesh=mesh, in_specs=placed, out_specs=(P("dp", "mp"), P("dp", "mp")), check_vma=False
    )
```

```python
import functools

import jax
import jax.numpy as jnp
from jax import lax
from jax.experimental import pallas as pl
from jax.experimental.pallas import tpu as pltpu
from jax.sharding import PartitionSpec as P

MESH = pl.DeviceIdType.MESH
F32, BF = jnp.float32, jnp.bfloat16
PIECE = 64
POS = {4: 0, 0: 1, 3: 2, 5: 3, 2: 4, 6: 5, 1: 6, 7: 7}


def dot(a, b):
    return jnp.dot(a, b, preferred_element_type=F32)


def dot_nt(a, b):
    return lax.dot_general(a, b, (((1,), (1,)), ((), ())), preferred_element_type=F32)


def dot_tn(a, b):
    return lax.dot_general(a, b, (((0,), (0,)), ((), ())), preferred_element_type=F32)


def kernel(total, fi_hbm, ft_hbm, wi_hbm, wt_hbm, lt_ref, bs_ref, o_ref,
           feats, wts, featst, es, er, esr, err, unit, scal, img, txt, prob, gi, gt,
           gib, ra, ra2, r2, r4, sa, sab, gts, sibr, gtb, tr, zs, zr, zsr, zrr,
           fsi, fri, fst, frt, fsr, frr, ysi, yri, yst, yrt,
           lsem, ssem, rsem):
    oi_ref, ot_ref = o_ref.at[0], o_ref.at[1]
    dp, mp = lax.axis_index("dp"), lax.axis_index("mp")
    z, xl, y = dp // 8, (dp // 4) % 2, dp % 4
    c = mp % 2
    x = (mp // 2) * 2 + xl

    def dev(xx, yy, zz, cc):
        return (zz * 8 + (xx % 2) * 4 + yy, (xx // 2) * 2 + cc)

    xp, x2, xm = (dev((x + k) % 4, y, z, c) for k in (1, 2, 3))
    yp, y2, ym = (dev(x, (y + k) % 4, z, c) for k in (1, 2, 3))
    zs_at = [dev(x, y, (z + k) % 8, c) for k in range(8)]
    zp, zm = zs_at[1], zs_at[7]
    ws_at = [(z * 8 + ((xl + k // 4) % 2) * 4 + (y + k) % 4, mp) for k in range(8)]
    sib = (dp, (mp // 2) * 2 + (1 - c))
    mps = [(dp, (mp + k) % 4) for k in (1, 2, 3)]

    barrier = pltpu.get_barrier_semaphore()
    greeted = mps + [xp, xm] + zs_at[1:] + ws_at[1:4] + ws_at[5:]
    for d in greeted:
        pl.semaphore_signal(barrier, inc=1, device_id=d, device_id_type=MESH)

    loads = []
    for k, (s, t) in enumerate(((fi_hbm, feats.at[0, 0:224]), (wi_hbm, wts.at[0]),
                                (ft_hbm, feats.at[1, 0:224]), (wt_hbm, wts.at[1]))):
        cp = pltpu.make_async_copy(s, t, lsem.at[k])
        cp.start()
        loads.append(cp)
    feats[:, 224:256, :] = jnp.zeros((2, 32, 1152), BF)

    started = []

    def send(src, dst, to):
        k = len(started)
        cp = pltpu.make_async_remote_copy(src_ref=src, dst_ref=dst, send_sem=ssem.at[k],
                                          recv_sem=rsem.at[k], device_id=to, device_id_type=MESH)
        cp.start()
        started.append(cp)
        return cp

    l0 = lax.broadcasted_iota(jnp.int32, (32, 128), 0)
    l1 = lax.broadcasted_iota(jnp.int32, (32, 128), 1)
    emb_in = []
    rests = []
    for m in (0, 1):
        loads[2 * m].wait()
        loads[2 * m + 1].wait()
        main = dot_nt(feats[m], wts[m, 0:256, :]).astype(BF)
        rest = dot_nt(feats[m], wts[m, 256:288, :]).astype(BF)
        place = (l1 == l0 + 32 * ((mp + 2 * m) % 4)).astype(F32).astype(BF)
        rests.append(dot(rest, place))
        for q in range(4):
            es[m, q] = main[64 * q:64 * q + 64]
        if m == 0:
            pl.semaphore_wait(barrier, len(greeted))
        else:
            rest = (rests[0] + rests[1]).astype(BF)
            for q in range(4):
                esr[q] = rest[64 * q:64 * q + 64]
            emb_in += [send(esr.at[(mp + k) % 4], err.at[mp], mps[k - 1]) for k in (1, 2, 3)]
            err[mp] = esr[mp]
        emb_in += [send(es.at[m, (mp + k) % 4], er.at[m, mp], mps[k - 1]) for k in (1, 2, 3)]
        er[m, mp] = es[m, mp]

    lane = lax.broadcasted_iota(jnp.int32, (64, 128), 1) // 32

    def normalize(m):
        rest = sum(jnp.where(lane == (q + 2 * m) % 4, err[q].astype(F32), 0.0) for q in range(4))
        if m:
            rest = pltpu.roll(rest, 64, 1)
        wide = jnp.concatenate([er[m, q].astype(F32) for q in range(4)] + [rest], axis=1)
        scale = lax.rsqrt(jnp.sum(wide * wide, axis=1, keepdims=True) + 1e-06)
        unit[m] = wide * scale
        scal[m] = jnp.broadcast_to(scale, (64, 128))
        return (wide * scale).astype(BF)

    for cp in emb_in:
        cp.wait_recv()
    A, B, A0, A1 = pl.ds(0, 32), pl.ds(32, 32), pl.ds(0, 16), pl.ds(16, 16)
    axis1 = ((xp, x2, xm), (yp, y2, ym))
    axis2 = ((yp, y2, ym), (xp, x2, xm))
    got = {}
    piece = normalize(0)
    img[0, 0, 0] = piece[0:32]
    img[0, 1, 0] = piece[32:64]
    for j in (1, 3, 2):
        for h in (0, 1):
            got[0, h, 4 - j] = send(img.at[0, h, 0], img.at[0, h, 4 - j], axis1[h][j - 1])

    def second(j):
        for h in (0, 1):
            got[3, h, j] = send(img.at[0, h, j], img.at[3, h, j], axis2[h][0])
            got[1, h, j] = send(img.at[0, h, j], img.at[1, h, j], axis2[h][2])

    def third(j):
        for h in (0, 1):
            got[3, h, j].wait_recv()
            got[4, h, j] = send(img.at[3, h, j, A0], img.at[2, h, j, A0], axis2[h][0])
            got[1, h, j].wait_recv()
            got[5, h, j] = send(img.at[1, h, j, A1], img.at[2, h, j, A1], axis2[h][2])

    second(0)
    txt[POS[0], 0] = normalize(1)
    tgot, sgot = {}, {}
    halves = (A, B)

    def text_send(src, dst, half, to):
        tgot[dst, half] = send(txt.at[POS[src], 0, halves[half]], txt.at[POS[dst], 0, halves[half]], to)

    def text_share(*slots):
        for k in slots:
            sgot[k] = send(txt.at[POS[k], 0], txt.at[POS[k], 1], sib)

    def text_shared(*slots):
        for k in slots:
            sgot[k].wait_recv()

    def text_hop(k, turns=(0, 1)):
        for turn in turns:
            for src, nxt, to, lead in ((8 - k, 7 - k, zp, 0), (k, k + 1, zm, 1)):
                half = (lead + turn) % 2
                tgot[src, half].wait_recv()
                if k < 3 or turn == 0:
                    text_send(src, nxt, half, to)
        if turns[-1]:
            text_share(8 - k, k)

    text_send(0, 7, 0, zp)
    text_send(0, 1, 1, zm)
    text_send(0, 7, 1, zp)
    text_send(0, 1, 0, zm)
    text_share(0)
    temp = jnp.exp(jnp.full((1, 1), lt_ref[0], F32))
    shift = jnp.full((1, 1), bs_ref[0], F32)
    gain = temp * (1.0 / total)

    def scores(k, n):
        at = pl.ds(2 * n, 2)
        logits = temp * dot_nt(img[k].reshape(256, 1152), txt[at].reshape(256, 1152)) + shift
        cols = pl.ds(pl.multiple_of(256 * n, 256), 256)
        prob[256 * k:256 * k + 256, cols] = (gain / (1.0 + jnp.exp(-logits))).astype(BF)
        return logits

    def some_scores(k, count):
        for i in range(count):
            scores(k, 3 - i)

    sent = {}

    def image_block(k):
        gi[k] = dot(prob[256 * k:256 * k + 256, :],
                    txt[...].reshape(1024, 1152)).reshape(2, 4, 32, 1152)

    def text_block(n):
        gt[2 * n:2 * n + 2] = dot_tn(prob[:, 256 * n:256 * n + 256],
                                     img[...].reshape(1024, 1152)).reshape(2, 2, 64, 1152)
        gts[n] = gt[2 * n:2 * n + 2, 1].astype(BF)
        return send(gts.at[n], sibr.at[n], sib)

    def text_own(k):
        return gt[POS[k], 0] + sibr[POS[k] // 2, POS[k] % 2].astype(F32)

    def text_on(k, half):
        at = halves[half]
        part = gt[POS[k], 0, at] + sibr[POS[k] // 2, POS[k] % 2, at].astype(F32)
        back_k = k + 1 if k < 4 else k - 1
        if k != 4 and (back_k != 4 or half == (0 if k == 3 else 1)):
            sent[back_k, half].wait_recv()
            part = part + tr[back_k, at].astype(F32)
        gtb[k, at] = part.astype(BF)
        to = zp if k < 4 or (k == 4 and half == 0) else zm
        sent[k, half] = send(gtb.at[k, at], tr.at[k, at], to)

    for j in (1, 3):
        got[0, 0, j].wait_recv()
        got[0, 1, j].wait_recv()
        second(j)
    text_hop(1)
    got[0, 0, 2].wait_recv()
    got[0, 1, 2].wait_recv()
    second(2)
    third(0)
    text_hop(2)
    text_shared(1, 7)
    scores(0, 3)
    third(1)
    third(3)
    text_shared(2, 6)
    scores(0, 2)
    third(2)
    text_hop(3, (0,))

    some_scores(1, 2)
    text_hop(3, (1,))
    some_scores(3, 2)
    tgot[4, 0].wait_recv()
    tgot[4, 1].wait_recv()
    text_share(4)
    text_shared(3, 5, 0)
    for k in (1, 3, 0):
        scores(k, 1)
    text_shared(4)
    scores(1, 0)
    scores(3, 0)
    logits = scores(0, 0)
    r0 = lax.broadcasted_iota(jnp.int32, (32, 128), 0)
    r1 = lax.broadcasted_iota(jnp.int32, (32, 128), 1)
    for h in (0, 1):
        own = logits[128 * h:128 * h + 32, 128:256]
        prob[128 * h:128 * h + 32, 128:256] = jnp.where(
            r1 == r0 + 32 * h, -gain / (1.0 + jnp.exp(own)), gain / (1.0 + jnp.exp(-own))).astype(BF)

    for j in range(4):
        for h in (0, 1):
            got[4, h, j].wait_recv()
            got[5, h, j].wait_recv()
    some_scores(2, 4)
    q0 = text_block(0)
    image_block(2)
    gib[1] = gi[2].astype(BF)
    pairs = (pl.ds(2, 2), pl.ds(0, 2))
    q4 = [[[send(gib.at[1, h, p, A0], r4.at[h, p, A0], axis2[h][0]),
            send(gib.at[1, h, p, A1], r4.at[h, p, A1], axis2[h][2])] for h in (0, 1)] for p in pairs]
    q1 = text_block(1)
    q0.wait_recv()
    text_on(4, 0)
    text_on(4, 1)
    image_block(1)
    for h in (0, 1):
        gib[0, h, :, A1] = gi[1, h, :, A1].astype(BF)
    q1.wait_recv()
    text_on(3, 1)
    text_on(5, 0)
    image_block(3)
    for h in (0, 1):
        gib[2, h, :, A0] = gi[3, h, :, A0].astype(BF)
    qa = [[], []]

    def image_on(n):
        p = pairs[n]
        for h in (0, 1):
            for cp in q4[n][h]:
                cp.wait_recv()
            gib[0, h, p, A0] = (gi[1, h, p, A0] + r4[h, p, A0].astype(F32)).astype(BF)
            gib[2, h, p, A1] = (gi[3, h, p, A1] + r4[h, p, A1].astype(F32)).astype(BF)
            for i in (0, 1):
                qa[n].append(send(gib.at[2 * i, h, p], ra.at[i, h, p], axis2[h][2 * i]))

    qa2 = []

    def image_first(n):
        for cp in qa[n]:
            cp.wait_recv()
        for j in (2, 3) if n == 0 else (1, 0):
            for h in (0, 1):
                part = gi[0, h, j] + ra[0, h, j].astype(F32) + ra[1, h, j].astype(F32)
                if j == 2:
                    sab[h, 1] = part.astype(BF)
                    q2h.append(send(sab.at[h, 1, A0], r2.at[h, A0], axis1[h][0]))
                    q2h.append(send(sab.at[h, 1, A1], r2.at[h, A1], axis1[h][2]))
                else:
                    sa[h, j] = part

    q2h = []

    def image_last():
        for h in (0, 1):
            for cp in q2h[2 * h:2 * h + 2]:
                cp.wait_recv()
            sab[h, 0, A0] = (sa[h, 1, A0] + r2[h, A0].astype(F32)).astype(BF)
            sab[h, 0, A1] = sa[h, 1, A1].astype(BF)
            sab[h, 2, A0] = sa[h, 3, A0].astype(BF)
            sab[h, 2, A1] = (sa[h, 3, A1] + r2[h, A1].astype(F32)).astype(BF)
            qa2.append(send(sab.at[h, 0], ra2.at[h, 0], axis1[h][0]))
            qa2.append(send(sab.at[h, 2], ra2.at[h, 1], axis1[h][2]))

    image_on(0)
    q2 = text_block(2)
    text_on(3, 0)
    text_on(5, 1)
    image_on(1)
    q3 = text_block(3)
    image_block(0)
    q2.wait_recv()
    text_on(2, 1)
    text_on(6, 0)
    text_on(2, 0)
    text_on(6, 1)
    image_first(0)
    q3.wait_recv()
    text_on(1, 1)
    text_on(7, 0)
    image_first(1)
    image_last()
    text_on(1, 0)
    text_on(7, 1)

    def back(m, dx):
        inner = jnp.sum(unit[m] * dx, axis=1, keepdims=True)
        dz = scal[m][:, 0:1] * (dx - unit[m] * inner)
        for q in range(4):
            zs[m, q] = dz[:, 256 * q:256 * q + 256].astype(BF)
        zr[m, mp] = zs[m, mp]
        return dz[:, 1024:1152], [send(zs.at[m, (mp + k) % 4], zr.at[m, mp], mps[k - 1]) for k in (1, 2, 3)]

    for k in (1, 7):
        for half in (0, 1):
            sent[k, half].wait_recv()
    rest_t, z_in = back(1, text_own(0) + tr[1].astype(F32) + tr[7].astype(F32))
    for cp in qa2:
        cp.wait_recv()
    rest_i, q = back(0, jnp.concatenate(
        [sa[h, 0] + ra2[h, 0].astype(F32) + ra2[h, 1].astype(F32)
         for h in (0, 1)], axis=0))
    z_in += q
    for q in range(4):
        turned = [pltpu.roll(r, (128 - 32 * q + 32 * m) % 128, 1) for m, r in ((0, rest_i), (1, rest_t))]
        zsr[q] = jnp.where(lane == 0, turned[0], turned[1]).astype(BF)
    zrr[mp] = zsr[mp]
    z_in += [send(zsr.at[(mp + k) % 4], zrr.at[mp], mps[k - 1]) for k in (1, 2, 3)]

    wide_t = jnp.transpose(feats[0])
    for k in range(8):
        featst[0, k] = wide_t[144 * k:144 * k + 144]
    p0 = lax.broadcasted_iota(jnp.int32, (144, 1152), 0)
    at_z = p0 + 126 * ((p0 * 3641) >> 16)
    p1 = lax.broadcasted_iota(jnp.int32, (144, 1152), 1)

    def turn(w, _):
        turned = (p1 == at_z + 18 * w).astype(F32).astype(BF)
        featst[1, w] = dot_nt(turned, feats[1]).astype(BF)
        featst[2, w] = dot_nt(turned, feats[0]).astype(BF)
        return 0
    lax.fori_loop(0, 8, turn, 0)


    far_z, far_w = (4, 3, 5, 2, 6, 1, 7), (6, 2, 5, 7, 1, 3, 4)
    def by_z(k):
        return (z + k) % 8

    def by_w(k):
        return ((xl + k // 4) % 2) * 4 + (y + k) % 4

    def rows(ref):
        return jnp.concatenate([ref[q] for q in range(4)], axis=0)

    def regroup(q, own, rc, near, far, ys, yr, base, at):
        for cp in q:
            cp.wait_recv()
        for k in near:
            own = own + rc[k].astype(F32)
        cols = own.shape[1]
        for k in range(8):
            ys[k, :, 0:cols] = own[18 * k:18 * k + 16].astype(BF)
            tail = [own[18 * k + r:18 * k + r + 1, i:i + 128] for r in (16, 17) for i in range(0, cols, 128)]
            tail.append(jnp.zeros((16 - len(tail), 128), F32))
            ys[k, :, cols:cols + 128] = jnp.concatenate(tail, axis=0).astype(BF)
        return [send(ys.at[base(k)], yr.at[k], at[k]) for k in far]

    def last_sum(q, ys, yr, base):
        for cp in q:
            cp.wait_recv()
        out = ys[base(0)].astype(F32)
        for k in range(1, 8):
            out = out + yr[k].astype(F32)
        cols = out.shape[1] - 128
        n = cols // 128
        tail = [jnp.concatenate([out[r * n + i:r * n + i + 1, cols:] for i in range(n)], axis=1) for r in (0, 1)]
        return jnp.concatenate([out[:, 0:cols]] + tail, axis=0)

    for cp in z_in:
        cp.wait_recv()
    main_i, main_t = rows(zr.at[0]), rows(zr.at[1])
    rest = rows(zrr).astype(F32)
    which = lax.broadcasted_iota(jnp.int32, (256, 128), 1) // 32
    rest_i = jnp.where(which == 0, rest, 0.0).astype(BF)
    rest_t = jnp.where(which == 1, rest, 0.0).astype(BF)

    def make_t(k):
        a, b = featst[1, by_w(k)], featst[2, by_w(k)]
        rest = dot(a, rest_t) + dot(b, rest_i)
        return dot(a, main_t), rest[0:72] + pltpu.roll(rest[72:144], 64, 1)

    def make_i(k):
        return dot(featst[0, by_z(k)], main_i)

    H0, H1 = pl.ds(0, 80), pl.ds(80, 64)
    fsi[4] = make_i(4).astype(BF)
    qi4 = [send(fsi.at[4, H0], fri.at[4, H0], zs_at[2]), send(fsi.at[4, H1], fri.at[4, H1], zs_at[6])]
    qi3, qi = [], []

    def to_next(k, q):
        fsi[k] = make_i(k).astype(BF)
        q.append(send(fsi.at[k], fri.at[k], zp if k < 4 else zm))

    to_next(3, qi3)
    to_next(5, qi3)
    qt = []
    for k in far_w:
        part, rest = make_t(k)
        fst[k] = part.astype(BF)
        fsr[k, 0:72] = rest.astype(BF)
        qt.append(send(fst.at[k], frt.at[k], ws_at[k]))
        qt.append(send(fsr.at[k], frr.at[k], ws_at[k]))
    own_t, own_r = make_t(0)


    to_next(1, qi)
    to_next(7, qi)
    own_2, own_6 = make_i(2), make_i(6)
    own_i = make_i(0)
    for k, part, via, half in ((2, own_2, 3, 0), (6, own_6, 5, 1)):
        qi3[half].wait_recv()
        part = part + fri[via].astype(F32)
        qi4[half].wait_recv()
        if half == 0:
            fsi[k, H0] = (part[0:80] + fri[4, H0].astype(F32)).astype(BF)
            fsi[k, H1] = part[80:144].astype(BF)
        else:
            fsi[k, H0] = part[0:80].astype(BF)
            fsi[k, H1] = (part[80:144] + fri[4, H1].astype(F32)).astype(BF)
        qi.append(send(fsi.at[k], fri.at[k], zs_at[k]))
    for cp in qt:
        cp.wait_recv()
    for k in far_w:
        own_r = own_r + frr[k, 0:72].astype(F32)
        own_t = own_t + frt[k].astype(F32)
    own_t = jnp.concatenate([own_t, jnp.concatenate([own_r, pltpu.roll(own_r, 64, 1)], axis=0)], axis=1)
    qt = regroup([], own_t, frt, (), far_z, yst, yrt, by_z, zs_at)
    qi = regroup(qi, own_i, fri, (1, 7, 2, 6), far_w, ysi, yri, by_w, ws_at)
    oi_ref[:, 0:256] = last_sum(qi, ysi, yri, by_w)
    out = last_sum(qt, yst, yrt, by_z)
    ot_ref[:, 0:256] = out[:, 0:256]
    oi_ref[:, 256:288] = out[:, 256:288]
    ot_ref[:, 256:288] = pltpu.roll(out[:, 256:384], 96, 1)[:, 0:32]
    for cp in started:
        cp.wait_send()


COPIES = 256


def local(image_feats, text_feats, image_proj, text_proj, log_temp, bias):
    total = image_feats.shape[0] * lax.axis_size("dp")
    vm = pltpu.VMEM
    out = jax.ShapeDtypeStruct((18, 288), F32)
    res = pl.pallas_call(
        functools.partial(kernel, total),
        out_shape=jax.ShapeDtypeStruct((2, 18, 288), F32),
        in_specs=[pl.BlockSpec(memory_space=pl.ANY)] * 4
        + [pl.BlockSpec(memory_space=pltpu.SMEM)] * 2,
        out_specs=pl.BlockSpec(memory_space=vm),
        scratch_shapes=[
            vm((2, 256, 1152), BF),
            vm((2, 288, 1152), BF),
            vm((3, 8, 144, 256), BF),
            vm((2, 4, 64, 256), BF),
            vm((2, 4, 64, 256), BF),
            vm((4, 64, 128), BF),
            vm((4, 64, 128), BF),
            vm((2, 64, 1152), F32),
            vm((2, 64, 128), F32),
            vm((4, 2, 4, 32, 1152), BF),
            vm((8, 2, 64, 1152), BF),
            vm((1024, 1024), BF),
            vm((4, 2, 4, 32, 1152), F32),
            vm((8, 2, 64, 1152), F32),
            vm((3, 2, 4, 32, 1152), BF),
            vm((2, 2, 4, 32, 1152), BF),
            vm((2, 2, 32, 1152), BF),
            vm((2, 32, 1152), BF),
            vm((2, 4, 32, 1152), BF),
            vm((2, 4, 32, 1152), F32),
            vm((2, 3, 32, 1152), BF),
            vm((4, 2, 64, 1152), BF),
            vm((4, 2, 64, 1152), BF),
            vm((8, 64, 1152), BF),
            vm((8, 64, 1152), BF),
            vm((2, 4, 64, 256), BF),
            vm((2, 4, 64, 256), BF),
            vm((4, 64, 128), BF),
            vm((4, 64, 128), BF),
            vm((8, 144, 256), BF),
            vm((8, 144, 256), BF),
            vm((8, 144, 256), BF),
            vm((8, 144, 256), BF),
            vm((8, 80, 128), BF),
            vm((8, 80, 128), BF),
            vm((8, 16, 384), BF),
            vm((8, 16, 384), BF),
            vm((8, 16, 512), BF),
            vm((8, 16, 512), BF),
            pltpu.SemaphoreType.DMA((4,)),
            pltpu.SemaphoreType.DMA((COPIES,)),
            pltpu.SemaphoreType.DMA((COPIES,)),
        ],
        name="contrastive",
        compiler_params=pltpu.CompilerParams(
            collective_id=0, has_side_effects=True, vmem_limit_bytes=60 * 2**20
        ),
    )(image_feats, text_feats, image_proj.T, text_proj.T, log_temp, bias)
    return res[0], res[1]


def solution(mesh):
    placed = (P("dp", None), P("dp", None), P(None, "mp"), P(None, "mp"), P(), P())
    return jax.shard_map(
        local, mesh=mesh, in_specs=placed, out_specs=(P("dp", "mp"), P("dp", "mp")), check_vma=False
    )
```

```python
import functools

import jax
import jax.numpy as jnp
from jax import lax
from jax.experimental import pallas as pl
from jax.experimental.pallas import tpu as pltpu
from jax.sharding import PartitionSpec as P

MESH = pl.DeviceIdType.MESH
F32, BF = jnp.float32, jnp.bfloat16
PIECE = 64
POS = {4: 0, 0: 1, 3: 2, 5: 3, 2: 4, 6: 5, 1: 6, 7: 7}


def dot(a, b):
    return jnp.dot(a, b, preferred_element_type=F32)


def dot_nt(a, b):
    return lax.dot_general(a, b, (((1,), (1,)), ((), ())), preferred_element_type=F32)


def dot_tn(a, b):
    return lax.dot_general(a, b, (((0,), (0,)), ((), ())), preferred_element_type=F32)


def kernel(total, fi_hbm, ft_hbm, wi_hbm, wt_hbm, lt_ref, bs_ref, o_ref,
           feats, wts, featst, es, er, esr, err, unit, scal, img, txt, prob, gi, gt,
           gib, ra, ra2, r2, r4, sa, sab, gts, sibr, gtb, tr, zs, zr, zsr, zrr,
           fsi, fri, fst, frt, fsr, frr, ysi, yri, yst, yrt,
           lsem, ssem, rsem):
    oi_ref, ot_ref = o_ref.at[0], o_ref.at[1]
    dp, mp = lax.axis_index("dp"), lax.axis_index("mp")
    z, xl, y = dp // 8, (dp // 4) % 2, dp % 4
    c = mp % 2
    x = (mp // 2) * 2 + xl

    def dev(xx, yy, zz, cc):
        return (zz * 8 + (xx % 2) * 4 + yy, (xx // 2) * 2 + cc)

    xp, x2, xm = (dev((x + k) % 4, y, z, c) for k in (1, 2, 3))
    yp, y2, ym = (dev(x, (y + k) % 4, z, c) for k in (1, 2, 3))
    zs_at = [dev(x, y, (z + k) % 8, c) for k in range(8)]
    zp, zm = zs_at[1], zs_at[7]
    ws_at = [(z * 8 + ((xl + k // 4) % 2) * 4 + (y + k) % 4, mp) for k in range(8)]
    sib = (dp, (mp // 2) * 2 + (1 - c))
    mps = [(dp, (mp + k) % 4) for k in (1, 2, 3)]

    barrier = pltpu.get_barrier_semaphore()
    greeted = mps + [xp, xm] + zs_at[1:] + ws_at[1:4] + ws_at[5:]
    for d in greeted:
        pl.semaphore_signal(barrier, inc=1, device_id=d, device_id_type=MESH)

    loads = []
    for k, (s, t) in enumerate(((fi_hbm, feats.at[0, 0:224]), (wi_hbm, wts.at[0]),
                                (ft_hbm, feats.at[1, 0:224]), (wt_hbm, wts.at[1]))):
        cp = pltpu.make_async_copy(s, t, lsem.at[k])
        cp.start()
        loads.append(cp)
    feats[:, 224:256, :] = jnp.zeros((2, 32, 1152), BF)

    started, gone = [], []

    def send(src, dst, to):
        k = len(started)
        cp = pltpu.make_async_remote_copy(src_ref=src, dst_ref=dst, send_sem=ssem.at[k],
                                          recv_sem=rsem.at[k], device_id=to, device_id_type=MESH)
        cp.start()
        started.append(cp)
        return cp

    l0 = lax.broadcasted_iota(jnp.int32, (32, 128), 0)
    l1 = lax.broadcasted_iota(jnp.int32, (32, 128), 1)
    emb_in = []
    rests = []
    for m in (0, 1):
        loads[2 * m].wait()
        loads[2 * m + 1].wait()
        main = dot_nt(feats[m], wts[m, 0:256, :]).astype(BF)
        rest = dot_nt(feats[m], wts[m, 256:288, :]).astype(BF)
        place = (l1 == l0 + 32 * ((mp + 2 * m) % 4)).astype(F32).astype(BF)
        rests.append(dot(rest, place))
        for q in range(4):
            es[m, q] = main[64 * q:64 * q + 64]
        if m == 0:
            pl.semaphore_wait(barrier, len(greeted))
        else:
            rest = (rests[0] + rests[1]).astype(BF)
            for q in range(4):
                esr[q] = rest[64 * q:64 * q + 64]
            emb_in += [send(esr.at[(mp + k) % 4], err.at[mp], mps[k - 1]) for k in (1, 2, 3)]
            err[mp] = esr[mp]
        emb_in += [send(es.at[m, (mp + k) % 4], er.at[m, mp], mps[k - 1]) for k in (1, 2, 3)]
        er[m, mp] = es[m, mp]

    lane = lax.broadcasted_iota(jnp.int32, (64, 128), 1) // 32

    def normalize(m):
        rest = sum(jnp.where(lane == (q + 2 * m) % 4, err[q].astype(F32), 0.0) for q in range(4))
        if m:
            rest = pltpu.roll(rest, 64, 1)
        wide = jnp.concatenate([er[m, q].astype(F32) for q in range(4)] + [rest], axis=1)
        scale = lax.rsqrt(jnp.sum(wide * wide, axis=1, keepdims=True) + 1e-06)
        unit[m] = wide * scale
        scal[m] = jnp.broadcast_to(scale, (64, 128))
        return (wide * scale).astype(BF)

    for cp in emb_in:
        cp.wait_recv()
    A, B, A0, A1 = pl.ds(0, 32), pl.ds(32, 32), pl.ds(0, 16), pl.ds(16, 16)
    axis1 = ((xp, x2, xm), (yp, y2, ym))
    axis2 = ((yp, y2, ym), (xp, x2, xm))
    got = {}
    piece = normalize(0)
    img[0, 0, 0] = piece[0:32]
    img[0, 1, 0] = piece[32:64]
    for j in (1, 3, 2):
        for h in (0, 1):
            got[0, h, 4 - j] = send(img.at[0, h, 0], img.at[0, h, 4 - j], axis1[h][j - 1])

    def second(j):
        for h in (0, 1):
            got[3, h, j] = send(img.at[0, h, j], img.at[3, h, j], axis2[h][0])
            got[1, h, j] = send(img.at[0, h, j], img.at[1, h, j], axis2[h][2])

    def third(j):
        for h in (0, 1):
            got[3, h, j].wait_recv()
            got[4, h, j] = send(img.at[3, h, j, A0], img.at[2, h, j, A0], axis2[h][0])
            got[1, h, j].wait_recv()
            got[5, h, j] = send(img.at[1, h, j, A1], img.at[2, h, j, A1], axis2[h][2])

    second(0)
    txt[POS[0], 0] = normalize(1)
    tgot, sgot = {}, {}
    halves = (A, B)

    def text_send(src, dst, half, to):
        tgot[dst, half] = send(txt.at[POS[src], 0, halves[half]], txt.at[POS[dst], 0, halves[half]], to)

    def text_share(*slots):
        for k in slots:
            sgot[k] = send(txt.at[POS[k], 0], txt.at[POS[k], 1], sib)

    def text_shared(*slots):
        for k in slots:
            sgot[k].wait_recv()

    def text_hop(k, turns=(0, 1)):
        for turn in turns:
            for src, nxt, to, lead in ((8 - k, 7 - k, zp, 0), (k, k + 1, zm, 1)):
                half = (lead + turn) % 2
                tgot[src, half].wait_recv()
                if k < 3 or turn == 0:
                    text_send(src, nxt, half, to)
        if turns[-1]:
            text_share(8 - k, k)

    text_send(0, 7, 0, zp)
    text_send(0, 1, 1, zm)
    text_share(0)
    for cp in (tgot[7, 0], tgot[1, 1]):
        cp.wait_send()
        gone.append(cp)
    text_send(0, 7, 1, zp)
    text_send(0, 1, 0, zm)
    temp = jnp.exp(jnp.full((1, 1), lt_ref[0], F32))
    shift = jnp.full((1, 1), bs_ref[0], F32)
    gain = temp * (1.0 / total)

    def scores(k, n):
        at = pl.ds(2 * n, 2)
        logits = temp * dot_nt(img[k].reshape(256, 1152), txt[at].reshape(256, 1152)) + shift
        cols = pl.ds(pl.multiple_of(256 * n, 256), 256)
        prob[256 * k:256 * k + 256, cols] = (gain / (1.0 + jnp.exp(-logits))).astype(BF)
        return logits

    def some_scores(k, count):
        for i in range(count):
            scores(k, 3 - i)

    sent = {}

    def image_block(k):
        gi[k] = dot(prob[256 * k:256 * k + 256, :],
                    txt[...].reshape(1024, 1152)).reshape(2, 4, 32, 1152)

    def text_block(n):
        gt[2 * n:2 * n + 2] = dot_tn(prob[:, 256 * n:256 * n + 256],
                                     img[...].reshape(1024, 1152)).reshape(2, 2, 64, 1152)
        gts[n] = gt[2 * n:2 * n + 2, 1].astype(BF)
        return send(gts.at[n], sibr.at[n], sib)

    def text_own(k):
        return gt[POS[k], 0] + sibr[POS[k] // 2, POS[k] % 2].astype(F32)

    def text_on(k, half):
        at = halves[half]
        part = gt[POS[k], 0, at] + sibr[POS[k] // 2, POS[k] % 2, at].astype(F32)
        back_k = k + 1 if k < 4 else k - 1
        if k != 4 and (back_k != 4 or half == (0 if k == 3 else 1)):
            sent[back_k, half].wait_recv()
            part = part + tr[back_k, at].astype(F32)
        gtb[k, at] = part.astype(BF)
        to = zp if k < 4 or (k == 4 and half == 0) else zm
        sent[k, half] = send(gtb.at[k, at], tr.at[k, at], to)

    text_hop(1, (0,))
    for j in (1, 3):
        got[0, 0, j].wait_recv()
        got[0, 1, j].wait_recv()
        second(j)
    text_hop(1, (1,))
    got[0, 0, 2].wait_recv()
    got[0, 1, 2].wait_recv()
    second(2)
    text_hop(2, (0,))
    third(0)
    text_hop(2, (1,))
    text_shared(1, 7)
    scores(0, 3)
    third(1)
    third(3)
    text_hop(3, (0,))
    text_shared(2, 6)
    scores(0, 2)
    third(2)

    some_scores(1, 2)
    text_hop(3, (1,))
    some_scores(3, 2)
    text_shared(3, 5, 0)
    scores(1, 1)
    scores(3, 1)
    tgot[4, 0].wait_recv()
    tgot[4, 1].wait_recv()
    text_share(4)
    scores(0, 1)
    for j in range(4):
        for h in (0, 1):
            got[4, h, j].wait_recv()
            got[5, h, j].wait_recv()
    some_scores(2, 3)
    text_shared(4)
    for k in (2, 1, 3):
        scores(k, 0)
    logits = scores(0, 0)
    r0 = lax.broadcasted_iota(jnp.int32, (32, 128), 0)
    r1 = lax.broadcasted_iota(jnp.int32, (32, 128), 1)
    for h in (0, 1):
        own = logits[128 * h:128 * h + 32, 128:256]
        prob[128 * h:128 * h + 32, 128:256] = jnp.where(
            r1 == r0 + 32 * h, -gain / (1.0 + jnp.exp(own)), gain / (1.0 + jnp.exp(-own))).astype(BF)

    q0 = text_block(0)
    image_block(2)
    gib[1] = gi[2].astype(BF)
    pairs = (pl.ds(2, 2), pl.ds(0, 2))
    q4 = [[[send(gib.at[1, h, p, A0], r4.at[h, p, A0], axis2[h][0]),
            send(gib.at[1, h, p, A1], r4.at[h, p, A1], axis2[h][2])] for h in (0, 1)] for p in pairs]
    q1 = text_block(1)
    q0.wait_recv()
    text_on(4, 0)
    text_on(4, 1)
    image_block(1)
    for h in (0, 1):
        gib[0, h, :, A1] = gi[1, h, :, A1].astype(BF)
    q1.wait_recv()
    text_on(3, 1)
    text_on(5, 0)
    image_block(3)
    for h in (0, 1):
        gib[2, h, :, A0] = gi[3, h, :, A0].astype(BF)
    qa = [[], []]

    def image_on(n):
        p = pairs[n]
        for h in (0, 1):
            for cp in q4[n][h]:
                cp.wait_recv()
            gib[0, h, p, A0] = (gi[1, h, p, A0] + r4[h, p, A0].astype(F32)).astype(BF)
            gib[2, h, p, A1] = (gi[3, h, p, A1] + r4[h, p, A1].astype(F32)).astype(BF)
            for i in (0, 1):
                qa[n].append(send(gib.at[2 * i, h, p], ra.at[i, h, p], axis2[h][2 * i]))

    qa2 = []

    def image_first(n):
        for cp in qa[n]:
            cp.wait_recv()
        for j in (2, 3) if n == 0 else (1, 0):
            for h in (0, 1):
                part = gi[0, h, j] + ra[0, h, j].astype(F32) + ra[1, h, j].astype(F32)
                if j == 2:
                    sab[h, 1] = part.astype(BF)
                    q2h.append(send(sab.at[h, 1, A0], r2.at[h, A0], axis1[h][0]))
                    q2h.append(send(sab.at[h, 1, A1], r2.at[h, A1], axis1[h][2]))
                else:
                    sa[h, j] = part

    q2h = []

    def image_last():
        for h in (0, 1):
            for cp in q2h[2 * h:2 * h + 2]:
                cp.wait_recv()
            sab[h, 0, A0] = (sa[h, 1, A0] + r2[h, A0].astype(F32)).astype(BF)
            sab[h, 0, A1] = sa[h, 1, A1].astype(BF)
            sab[h, 2, A0] = sa[h, 3, A0].astype(BF)
            sab[h, 2, A1] = (sa[h, 3, A1] + r2[h, A1].astype(F32)).astype(BF)
            qa2.append(send(sab.at[h, 0], ra2.at[h, 0], axis1[h][0]))
            qa2.append(send(sab.at[h, 2], ra2.at[h, 1], axis1[h][2]))

    image_on(0)
    q2 = text_block(2)
    text_on(3, 0)
    text_on(5, 1)
    image_on(1)
    q3 = text_block(3)
    image_block(0)
    q2.wait_recv()
    text_on(2, 1)
    text_on(6, 0)
    text_on(2, 0)
    text_on(6, 1)
    image_first(0)
    q3.wait_recv()
    text_on(1, 1)
    text_on(7, 0)
    image_first(1)
    text_on(1, 0)
    text_on(7, 1)
    image_last()

    def back(m, dx):
        inner = jnp.sum(unit[m] * dx, axis=1, keepdims=True)
        dz = scal[m][:, 0:1] * (dx - unit[m] * inner)
        for q in range(4):
            zs[m, q] = dz[:, 256 * q:256 * q + 256].astype(BF)
        zr[m, mp] = zs[m, mp]
        return dz[:, 1024:1152], [send(zs.at[m, (mp + k) % 4], zr.at[m, mp], mps[k - 1]) for k in (1, 2, 3)]

    for k in (1, 7):
        for half in (0, 1):
            sent[k, half].wait_recv()
    rest_t, z_in = back(1, text_own(0) + tr[1].astype(F32) + tr[7].astype(F32))
    for cp in qa2:
        cp.wait_recv()
    rest_i, q = back(0, jnp.concatenate(
        [sa[h, 0] + ra2[h, 0].astype(F32) + ra2[h, 1].astype(F32)
         for h in (0, 1)], axis=0))
    z_in += q
    for q in range(4):
        turned = [pltpu.roll(r, (128 - 32 * q + 32 * m) % 128, 1) for m, r in ((0, rest_i), (1, rest_t))]
        zsr[q] = jnp.where(lane == 0, turned[0], turned[1]).astype(BF)
    zrr[mp] = zsr[mp]
    z_in += [send(zsr.at[(mp + k) % 4], zrr.at[mp], mps[k - 1]) for k in (1, 2, 3)]

    wide_t = jnp.transpose(feats[0])
    for k in range(8):
        featst[0, k] = wide_t[144 * k:144 * k + 144]
    p0 = lax.broadcasted_iota(jnp.int32, (144, 1152), 0)
    at_z = p0 + 126 * ((p0 * 3641) >> 16)
    p1 = lax.broadcasted_iota(jnp.int32, (144, 1152), 1)

    def turn(w, _):
        turned = (p1 == at_z + 18 * w).astype(F32).astype(BF)
        featst[1, w] = dot_nt(turned, feats[1]).astype(BF)
        featst[2, w] = dot_nt(turned, feats[0]).astype(BF)
        return 0
    lax.fori_loop(0, 8, turn, 0)


    far_z, far_w = (4, 3, 5, 2, 6, 1, 7), (6, 2, 5, 7, 1, 3, 4)
    def by_z(k):
        return (z + k) % 8

    def by_w(k):
        return ((xl + k // 4) % 2) * 4 + (y + k) % 4

    def rows(ref):
        return jnp.concatenate([ref[q] for q in range(4)], axis=0)

    def regroup(q, own, rc, near, far, ys, yr, base, at):
        for cp in q:
            cp.wait_recv()
        for k in near:
            own = own + rc[k].astype(F32)
        cols = own.shape[1]
        for k in range(8):
            ys[k, :, 0:cols] = own[18 * k:18 * k + 16].astype(BF)
            tail = [own[18 * k + r:18 * k + r + 1, i:i + 128] for r in (16, 17) for i in range(0, cols, 128)]
            tail.append(jnp.zeros((16 - len(tail), 128), F32))
            ys[k, :, cols:cols + 128] = jnp.concatenate(tail, axis=0).astype(BF)
        return [send(ys.at[base(k)], yr.at[k], at[k]) for k in far]

    def last_sum(q, ys, yr, base):
        for cp in q:
            cp.wait_recv()
        out = ys[base(0)].astype(F32)
        for k in range(1, 8):
            out = out + yr[k].astype(F32)
        cols = out.shape[1] - 128
        n = cols // 128
        tail = [jnp.concatenate([out[r * n + i:r * n + i + 1, cols:] for i in range(n)], axis=1) for r in (0, 1)]
        return jnp.concatenate([out[:, 0:cols]] + tail, axis=0)

    for cp in z_in:
        cp.wait_recv()
    main_i, main_t = rows(zr.at[0]), rows(zr.at[1])
    rest = rows(zrr).astype(F32)
    which = lax.broadcasted_iota(jnp.int32, (256, 128), 1) // 32
    rest_i = jnp.where(which == 0, rest, 0.0).astype(BF)
    rest_t = jnp.where(which == 1, rest, 0.0).astype(BF)

    def make_t(k):
        a, b = featst[1, by_w(k)], featst[2, by_w(k)]
        rest = dot(a, rest_t) + dot(b, rest_i)
        return dot(a, main_t), rest[0:72] + pltpu.roll(rest[72:144], 64, 1)

    def make_i(k):
        return dot(featst[0, by_z(k)], main_i)

    H0, H1 = pl.ds(0, 80), pl.ds(80, 64)
    fsi[4] = make_i(4).astype(BF)
    qi4 = [send(fsi.at[4, H0], fri.at[4, H0], zs_at[2]), send(fsi.at[4, H1], fri.at[4, H1], zs_at[6])]
    qi3, qi = [], []

    def to_next(k, q):
        fsi[k] = make_i(k).astype(BF)
        q.append(send(fsi.at[k], fri.at[k], zp if k < 4 else zm))

    to_next(3, qi3)
    to_next(5, qi3)
    qt = []
    for k in far_w:
        part, rest = make_t(k)
        fst[k] = part.astype(BF)
        fsr[k, 0:72] = rest.astype(BF)
        qt.append(send(fst.at[k], frt.at[k], ws_at[k]))
        qt.append(send(fsr.at[k], frr.at[k], ws_at[k]))
    own_t, own_r = make_t(0)


    to_next(1, qi)
    to_next(7, qi)
    own_2, own_6 = make_i(2), make_i(6)
    own_i = make_i(0)
    for k, part, via, half in ((2, own_2, 3, 0), (6, own_6, 5, 1)):
        qi3[half].wait_recv()
        part = part + fri[via].astype(F32)
        qi4[half].wait_recv()
        if half == 0:
            fsi[k, H0] = (part[0:80] + fri[4, H0].astype(F32)).astype(BF)
            fsi[k, H1] = part[80:144].astype(BF)
        else:
            fsi[k, H0] = part[0:80].astype(BF)
            fsi[k, H1] = (part[80:144] + fri[4, H1].astype(F32)).astype(BF)
        qi.append(send(fsi.at[k], fri.at[k], zs_at[k]))
    for cp in qt:
        cp.wait_recv()
    for k in far_w:
        own_r = own_r + frr[k, 0:72].astype(F32)
        own_t = own_t + frt[k].astype(F32)
    own_t = jnp.concatenate([own_t, jnp.concatenate([own_r, pltpu.roll(own_r, 64, 1)], axis=0)], axis=1)
    qt = regroup([], own_t, frt, (), far_z, yst, yrt, by_z, zs_at)
    qi = regroup(qi, own_i, fri, (1, 7, 2, 6), far_w, ysi, yri, by_w, ws_at)
    oi_ref[:, 0:256] = last_sum(qi, ysi, yri, by_w)
    out = last_sum(qt, yst, yrt, by_z)
    ot_ref[:, 0:256] = out[:, 0:256]
    oi_ref[:, 256:288] = out[:, 256:288]
    ot_ref[:, 256:288] = pltpu.roll(out[:, 256:384], 96, 1)[:, 0:32]
    for cp in started:
        if not any(cp is g for g in gone):
            cp.wait_send()


COPIES = 256


def local(image_feats, text_feats, image_proj, text_proj, log_temp, bias):
    total = image_feats.shape[0] * lax.axis_size("dp")
    vm = pltpu.VMEM
    res = pl.pallas_call(
        functools.partial(kernel, total),
        out_shape=jax.ShapeDtypeStruct((2, 18, 288), F32),
        in_specs=[pl.BlockSpec(memory_space=pl.ANY)] * 4
        + [pl.BlockSpec(memory_space=pltpu.SMEM)] * 2,
        out_specs=pl.BlockSpec(memory_space=vm),
        scratch_shapes=[
            vm((2, 256, 1152), BF),
            vm((2, 288, 1152), BF),
            vm((3, 8, 144, 256), BF),
            vm((2, 4, 64, 256), BF),
            vm((2, 4, 64, 256), BF),
            vm((4, 64, 128), BF),
            vm((4, 64, 128), BF),
            vm((2, 64, 1152), F32),
            vm((2, 64, 128), F32),
            vm((4, 2, 4, 32, 1152), BF),
            vm((8, 2, 64, 1152), BF),
            vm((1024, 1024), BF),
            vm((4, 2, 4, 32, 1152), F32),
            vm((8, 2, 64, 1152), F32),
            vm((3, 2, 4, 32, 1152), BF),
            vm((2, 2, 4, 32, 1152), BF),
            vm((2, 2, 32, 1152), BF),
            vm((2, 32, 1152), BF),
            vm((2, 4, 32, 1152), BF),
            vm((2, 4, 32, 1152), F32),
            vm((2, 3, 32, 1152), BF),
            vm((4, 2, 64, 1152), BF),
            vm((4, 2, 64, 1152), BF),
            vm((8, 64, 1152), BF),
            vm((8, 64, 1152), BF),
            vm((2, 4, 64, 256), BF),
            vm((2, 4, 64, 256), BF),
            vm((4, 64, 128), BF),
            vm((4, 64, 128), BF),
            vm((8, 144, 256), BF),
            vm((8, 144, 256), BF),
            vm((8, 144, 256), BF),
            vm((8, 144, 256), BF),
            vm((8, 80, 128), BF),
            vm((8, 80, 128), BF),
            vm((8, 16, 384), BF),
            vm((8, 16, 384), BF),
            vm((8, 16, 512), BF),
            vm((8, 16, 512), BF),
            pltpu.SemaphoreType.DMA((4,)),
            pltpu.SemaphoreType.DMA((COPIES,)),
            pltpu.SemaphoreType.DMA((COPIES,)),
        ],
        name="contrastive",
        compiler_params=pltpu.CompilerParams(
            collective_id=0, has_side_effects=True, vmem_limit_bytes=60 * 2**20
        ),
    )(image_feats, text_feats, image_proj.T, text_proj.T, log_temp, bias)
    return res[0], res[1]


def solution(mesh):
    placed = (P("dp", None), P("dp", None), P(None, "mp"), P(None, "mp"), P(), P())
    return jax.shard_map(
        local, mesh=mesh, in_specs=placed, out_specs=(P("dp", "mp"), P("dp", "mp")), check_vma=False
    )
```

```python
import functools

import jax
import jax.numpy as jnp
from jax import lax
from jax.experimental import pallas as pl
from jax.experimental.pallas import tpu as pltpu
from jax.sharding import PartitionSpec as P

MESH = pl.DeviceIdType.MESH
F32, BF = jnp.float32, jnp.bfloat16
PIECE = 64
POS = {4: 0, 0: 1, 3: 2, 5: 3, 2: 4, 6: 5, 1: 6, 7: 7}


def dot(a, b):
    return jnp.dot(a, b, preferred_element_type=F32)


def dot_nt(a, b):
    return lax.dot_general(a, b, (((1,), (1,)), ((), ())), preferred_element_type=F32)


def dot_tn(a, b):
    return lax.dot_general(a, b, (((0,), (0,)), ((), ())), preferred_element_type=F32)


def kernel(total, fi_hbm, ft_hbm, wi_hbm, wt_hbm, lt_ref, bs_ref, o_ref,
           feats, wts, featst, es, er, esr, err, unit, scal, img, txt, prob, gi, gt,
           gib, ra, ra2, r2, r4, sa, sab, gts, sibr, gtb, tr, zs, zr, zsr, zrr,
           fsi, fri, fst, frt, fsr, frr, ysi, yri, yst, yrt,
           lsem, ssem, rsem):
    oi_ref, ot_ref = o_ref.at[0], o_ref.at[1]
    dp, mp = lax.axis_index("dp"), lax.axis_index("mp")
    z, xl, y = dp // 8, (dp // 4) % 2, dp % 4
    c = mp % 2
    x = (mp // 2) * 2 + xl

    def dev(xx, yy, zz, cc):
        return (zz * 8 + (xx % 2) * 4 + yy, (xx // 2) * 2 + cc)

    xp, x2, xm = (dev((x + k) % 4, y, z, c) for k in (1, 2, 3))
    yp, y2, ym = (dev(x, (y + k) % 4, z, c) for k in (1, 2, 3))
    zs_at = [dev(x, y, (z + k) % 8, c) for k in range(8)]
    zp, zm = zs_at[1], zs_at[7]
    ws_at = [(z * 8 + ((xl + k // 4) % 2) * 4 + (y + k) % 4, mp) for k in range(8)]
    sib = (dp, (mp // 2) * 2 + (1 - c))
    mps = [(dp, (mp + k) % 4) for k in (1, 2, 3)]

    loads = []
    for k, (s, t) in enumerate(((fi_hbm, feats.at[0, 0:224]), (wi_hbm, wts.at[0]),
                                (ft_hbm, feats.at[1, 0:224]), (wt_hbm, wts.at[1]))):
        cp = pltpu.make_async_copy(s, t, lsem.at[k])
        cp.start()
        loads.append(cp)
    barrier = pltpu.get_barrier_semaphore()
    greeted = mps + [xp, xm] + zs_at[1:] + ws_at[1:4] + ws_at[5:]
    for d in greeted:
        pl.semaphore_signal(barrier, inc=1, device_id=d, device_id_type=MESH)

    feats[:, 224:256, :] = jnp.zeros((2, 32, 1152), BF)

    started, gone = [], []

    def send(src, dst, to):
        k = len(started)
        cp = pltpu.make_async_remote_copy(src_ref=src, dst_ref=dst, send_sem=ssem.at[k],
                                          recv_sem=rsem.at[k], device_id=to, device_id_type=MESH)
        cp.start()
        started.append(cp)
        return cp

    l0 = lax.broadcasted_iota(jnp.int32, (32, 128), 0)
    l1 = lax.broadcasted_iota(jnp.int32, (32, 128), 1)
    emb_in = []
    rests = []
    for m in (0, 1):
        loads[2 * m].wait()
        loads[2 * m + 1].wait()
        main = dot_nt(feats[m], wts[m, 0:256, :]).astype(BF)
        rest = dot_nt(feats[m], wts[m, 256:288, :]).astype(BF)
        place = (l1 == l0 + 32 * ((mp + 2 * m) % 4)).astype(F32).astype(BF)
        rests.append(dot(rest, place))
        for q in range(4):
            es[m, q] = main[64 * q:64 * q + 64]
        if m == 0:
            pl.semaphore_wait(barrier, len(greeted))
        else:
            rest = (rests[0] + rests[1]).astype(BF)
            for q in range(4):
                esr[q] = rest[64 * q:64 * q + 64]
            emb_in += [send(esr.at[(mp + k) % 4], err.at[mp], mps[k - 1]) for k in (1, 2, 3)]
            err[mp] = esr[mp]
        emb_in += [send(es.at[m, (mp + k) % 4], er.at[m, mp], mps[k - 1]) for k in (1, 2, 3)]
        er[m, mp] = es[m, mp]

    lane = lax.broadcasted_iota(jnp.int32, (64, 128), 1) // 32

    def normalize(m):
        rest = sum(jnp.where(lane == (q + 2 * m) % 4, err[q].astype(F32), 0.0) for q in range(4))
        if m:
            rest = pltpu.roll(rest, 64, 1)
        wide = jnp.concatenate([er[m, q].astype(F32) for q in range(4)] + [rest], axis=1)
        scale = lax.rsqrt(jnp.sum(wide * wide, axis=1, keepdims=True) + 1e-06)
        unit[m] = wide * scale
        scal[m] = jnp.broadcast_to(scale, (64, 128))
        return (wide * scale).astype(BF)

    for cp in emb_in:
        cp.wait_recv()
    A, B, A0, A1 = pl.ds(0, 32), pl.ds(32, 32), pl.ds(0, 16), pl.ds(16, 16)
    axis1 = ((xp, x2, xm), (yp, y2, ym))
    axis2 = ((yp, y2, ym), (xp, x2, xm))
    got = {}
    piece = normalize(0)
    img[0, 0, 0] = piece[0:32]
    img[0, 1, 0] = piece[32:64]
    for j in (1, 3, 2):
        for h in (0, 1):
            got[0, h, 4 - j] = send(img.at[0, h, 0], img.at[0, h, 4 - j], axis1[h][j - 1])

    def second(j):
        for h in (0, 1):
            got[3, h, j] = send(img.at[0, h, j], img.at[3, h, j], axis2[h][0])
            got[1, h, j] = send(img.at[0, h, j], img.at[1, h, j], axis2[h][2])

    def third(j):
        for h in (0, 1):
            got[3, h, j].wait_recv()
            got[4, h, j] = send(img.at[3, h, j, A0], img.at[2, h, j, A0], axis2[h][0])
            got[1, h, j].wait_recv()
            got[5, h, j] = send(img.at[1, h, j, A1], img.at[2, h, j, A1], axis2[h][2])

    second(0)
    txt[POS[0], 0] = normalize(1)
    tgot, sgot = {}, {}
    halves = (A, B)

    def text_send(src, dst, half, to):
        tgot[dst, half] = send(txt.at[POS[src], 0, halves[half]], txt.at[POS[dst], 0, halves[half]], to)

    def text_share(*slots):
        for k in slots:
            sgot[k] = send(txt.at[POS[k], 0], txt.at[POS[k], 1], sib)

    def text_shared(*slots):
        for k in slots:
            sgot[k].wait_recv()

    def text_hop(k, turns=(0, 1)):
        for turn in turns:
            for src, nxt, to, lead in ((8 - k, 7 - k, zp, 0), (k, k + 1, zm, 1)):
                half = (lead + turn) % 2
                tgot[src, half].wait_recv()
                if k < 3 or turn == 0:
                    text_send(src, nxt, half, to)
        if turns[-1]:
            text_share(8 - k, k)

    text_send(0, 7, 0, zp)
    text_send(0, 1, 1, zm)
    text_share(0)
    for cp in (tgot[7, 0], tgot[1, 1]):
        cp.wait_send()
        gone.append(cp)
    text_send(0, 7, 1, zp)
    text_send(0, 1, 0, zm)
    temp = jnp.exp(jnp.full((1, 1), lt_ref[0], F32))
    shift = jnp.full((1, 1), bs_ref[0], F32)
    gain = temp * (1.0 / total)

    def scores(k, n):
        at = pl.ds(2 * n, 2)
        logits = temp * dot_nt(img[k].reshape(256, 1152), txt[at].reshape(256, 1152)) + shift
        cols = pl.ds(pl.multiple_of(256 * n, 256), 256)
        prob[256 * k:256 * k + 256, cols] = (gain / (1.0 + jnp.exp(-logits))).astype(BF)
        return logits

    def some_scores(k, count):
        for i in range(count):
            scores(k, 3 - i)

    sent = {}

    def image_block(k):
        gi[k] = dot(prob[256 * k:256 * k + 256, :],
                    txt[...].reshape(1024, 1152)).reshape(2, 4, 32, 1152)

    def text_block(n):
        gt[2 * n:2 * n + 2] = dot_tn(prob[:, 256 * n:256 * n + 256],
                                     img[...].reshape(1024, 1152)).reshape(2, 2, 64, 1152)
        gts[n] = gt[2 * n:2 * n + 2, 1].astype(BF)
        return send(gts.at[n], sibr.at[n], sib)

    def text_own(k):
        return gt[POS[k], 0] + sibr[POS[k] // 2, POS[k] % 2].astype(F32)

    def text_on(k, half):
        at = halves[half]
        part = gt[POS[k], 0, at] + sibr[POS[k] // 2, POS[k] % 2, at].astype(F32)
        back_k = k + 1 if k < 4 else k - 1
        if k != 4 and (back_k != 4 or half == (0 if k == 3 else 1)):
            sent[back_k, half].wait_recv()
            part = part + tr[back_k, at].astype(F32)
        gtb[k, at] = part.astype(BF)
        to = zp if k < 4 or (k == 4 and half == 0) else zm
        sent[k, half] = send(gtb.at[k, at], tr.at[k, at], to)

    text_hop(1, (0,))
    for j in (1, 3):
        got[0, 0, j].wait_recv()
        got[0, 1, j].wait_recv()
        second(j)
    text_hop(1, (1,))
    got[0, 0, 2].wait_recv()
    got[0, 1, 2].wait_recv()
    second(2)
    text_hop(2, (0,))
    third(0)
    text_hop(2, (1,))
    text_shared(1, 7)
    scores(0, 3)
    third(1)
    third(3)
    text_hop(3, (0,))
    text_shared(2, 6)
    scores(0, 2)
    third(2)

    some_scores(1, 2)
    text_hop(3, (1,))
    some_scores(3, 2)
    text_shared(3, 5, 0)
    scores(1, 1)
    scores(3, 1)
    tgot[4, 0].wait_recv()
    tgot[4, 1].wait_recv()
    text_share(4)
    scores(0, 1)
    for j in range(4):
        for h in (0, 1):
            got[4, h, j].wait_recv()
            got[5, h, j].wait_recv()
    some_scores(2, 3)
    text_shared(4)
    for k in (2, 1, 3):
        scores(k, 0)
    logits = scores(0, 0)
    r0 = lax.broadcasted_iota(jnp.int32, (32, 128), 0)
    r1 = lax.broadcasted_iota(jnp.int32, (32, 128), 1)
    for h in (0, 1):
        own = logits[128 * h:128 * h + 32, 128:256]
        prob[128 * h:128 * h + 32, 128:256] = jnp.where(
            r1 == r0 + 32 * h, -gain / (1.0 + jnp.exp(own)), gain / (1.0 + jnp.exp(-own))).astype(BF)

    q0 = text_block(0)
    image_block(2)
    gib[1] = gi[2].astype(BF)
    pairs = (pl.ds(2, 2), pl.ds(0, 2))
    def two_away(p):
        return [[send(gib.at[1, h, p, A0], r4.at[h, p, A0], axis2[h][0]),
                 send(gib.at[1, h, p, A1], r4.at[h, p, A1], axis2[h][2])] for h in (0, 1)]

    q4 = [two_away(pairs[0])]
    q1 = text_block(1)
    q4.append(two_away(pairs[1]))
    q0.wait_recv()
    text_on(4, 0)
    text_on(4, 1)
    image_block(1)
    for h in (0, 1):
        gib[0, h, :, A1] = gi[1, h, :, A1].astype(BF)
    q1.wait_recv()
    text_on(3, 1)
    text_on(5, 0)
    image_block(3)
    for h in (0, 1):
        gib[2, h, :, A0] = gi[3, h, :, A0].astype(BF)
    qa = [[], []]

    def image_on(n):
        p = pairs[n]
        for h in (0, 1):
            for cp in q4[n][h]:
                cp.wait_recv()
            gib[0, h, p, A0] = (gi[1, h, p, A0] + r4[h, p, A0].astype(F32)).astype(BF)
            gib[2, h, p, A1] = (gi[3, h, p, A1] + r4[h, p, A1].astype(F32)).astype(BF)
            for i in (0, 1):
                qa[n].append(send(gib.at[2 * i, h, p], ra.at[i, h, p], axis2[h][2 * i]))

    qa2 = []

    def image_first(n):
        for cp in qa[n]:
            cp.wait_recv()
        for j in (2, 3) if n == 0 else (1, 0):
            for h in (0, 1):
                part = gi[0, h, j] + ra[0, h, j].astype(F32) + ra[1, h, j].astype(F32)
                if j == 2:
                    sab[h, 1] = part.astype(BF)
                    q2h.append(send(sab.at[h, 1, A0], r2.at[h, A0], axis1[h][0]))
                    q2h.append(send(sab.at[h, 1, A1], r2.at[h, A1], axis1[h][2]))
                else:
                    sa[h, j] = part

    q2h = []

    def image_last():
        for h in (0, 1):
            for cp in q2h[2 * h:2 * h + 2]:
                cp.wait_recv()
            sab[h, 0, A0] = (sa[h, 1, A0] + r2[h, A0].astype(F32)).astype(BF)
            sab[h, 0, A1] = sa[h, 1, A1].astype(BF)
            sab[h, 2, A0] = sa[h, 3, A0].astype(BF)
            sab[h, 2, A1] = (sa[h, 3, A1] + r2[h, A1].astype(F32)).astype(BF)
            qa2.append(send(sab.at[h, 0], ra2.at[h, 0], axis1[h][0]))
            qa2.append(send(sab.at[h, 2], ra2.at[h, 1], axis1[h][2]))

    image_on(0)
    q2 = text_block(2)
    text_on(3, 0)
    text_on(5, 1)
    image_on(1)
    q3 = text_block(3)
    image_block(0)
    q2.wait_recv()
    text_on(2, 1)
    text_on(6, 0)
    text_on(2, 0)
    text_on(6, 1)
    image_first(0)
    q3.wait_recv()
    text_on(1, 1)
    text_on(7, 0)
    image_first(1)
    text_on(1, 0)
    text_on(7, 1)
    image_last()

    def back(m, dx):
        inner = jnp.sum(unit[m] * dx, axis=1, keepdims=True)
        dz = scal[m][:, 0:1] * (dx - unit[m] * inner)
        for q in range(4):
            zs[m, q] = dz[:, 256 * q:256 * q + 256].astype(BF)
        zr[m, mp] = zs[m, mp]
        return dz[:, 1024:1152], [send(zs.at[m, (mp + k) % 4], zr.at[m, mp], mps[k - 1]) for k in (1, 2, 3)]

    for k in (1, 7):
        for half in (0, 1):
            sent[k, half].wait_recv()
    rest_t, z_in = back(1, text_own(0) + tr[1].astype(F32) + tr[7].astype(F32))
    for cp in qa2:
        cp.wait_recv()
    rest_i, q = back(0, jnp.concatenate(
        [sa[h, 0] + ra2[h, 0].astype(F32) + ra2[h, 1].astype(F32)
         for h in (0, 1)], axis=0))
    z_in += q
    for q in range(4):
        turned = [pltpu.roll(r, (128 - 32 * q + 32 * m) % 128, 1) for m, r in ((0, rest_i), (1, rest_t))]
        zsr[q] = jnp.where(lane == 0, turned[0], turned[1]).astype(BF)
    zrr[mp] = zsr[mp]
    z_in += [send(zsr.at[(mp + k) % 4], zrr.at[mp], mps[k - 1]) for k in (1, 2, 3)]

    wide_t = jnp.transpose(feats[0])
    for k in range(8):
        featst[0, k] = wide_t[144 * k:144 * k + 144]
    p0 = lax.broadcasted_iota(jnp.int32, (144, 1152), 0)
    at_z = p0 + 126 * ((p0 * 3641) >> 16)
    p1 = lax.broadcasted_iota(jnp.int32, (144, 1152), 1)

    def turn(w, _):
        turned = (p1 == at_z + 18 * w).astype(F32).astype(BF)
        featst[1, w] = dot_nt(turned, feats[1]).astype(BF)
        featst[2, w] = dot_nt(turned, feats[0]).astype(BF)
        return 0
    lax.fori_loop(0, 8, turn, 0)


    far_z, far_w = (4, 3, 5, 2, 6, 1, 7), (6, 2, 5, 7, 1, 3, 4)
    def by_z(k):
        return (z + k) % 8

    def by_w(k):
        return ((xl + k // 4) % 2) * 4 + (y + k) % 4

    def rows(ref):
        return jnp.concatenate([ref[q] for q in range(4)], axis=0)

    def regroup(q, own, rc, near, far, ys, yr, base, at):
        for cp in q:
            cp.wait_recv()
        for k in near:
            own = own + rc[k].astype(F32)
        cols = own.shape[1]
        for k in range(8):
            ys[k, :, 0:cols] = own[18 * k:18 * k + 16].astype(BF)
            tail = [own[18 * k + r:18 * k + r + 1, i:i + 128] for r in (16, 17) for i in range(0, cols, 128)]
            tail.append(jnp.zeros((16 - len(tail), 128), F32))
            ys[k, :, cols:cols + 128] = jnp.concatenate(tail, axis=0).astype(BF)
        return [send(ys.at[base(k)], yr.at[k], at[k]) for k in far]

    def last_sum(q, ys, yr, base):
        for cp in q:
            cp.wait_recv()
        out = ys[base(0)].astype(F32)
        for k in range(1, 8):
            out = out + yr[k].astype(F32)
        cols = out.shape[1] - 128
        n = cols // 128
        tail = [jnp.concatenate([out[r * n + i:r * n + i + 1, cols:] for i in range(n)], axis=1) for r in (0, 1)]
        return jnp.concatenate([out[:, 0:cols]] + tail, axis=0)

    for cp in z_in:
        cp.wait_recv()
    main_i, main_t = rows(zr.at[0]), rows(zr.at[1])
    rest = rows(zrr).astype(F32)
    which = lax.broadcasted_iota(jnp.int32, (256, 128), 1) // 32
    rest_i = jnp.where(which == 0, rest, 0.0).astype(BF)
    rest_t = jnp.where(which == 1, rest, 0.0).astype(BF)

    def make_t(k):
        a, b = featst[1, by_w(k)], featst[2, by_w(k)]
        rest = dot(a, rest_t) + dot(b, rest_i)
        return dot(a, main_t), rest[0:72] + pltpu.roll(rest[72:144], 64, 1)

    def make_i(k):
        return dot(featst[0, by_z(k)], main_i)

    H0, H1 = pl.ds(0, 80), pl.ds(80, 64)
    fsi[4] = make_i(4).astype(BF)
    qi4 = [send(fsi.at[4, H0], fri.at[4, H0], zs_at[2]), send(fsi.at[4, H1], fri.at[4, H1], zs_at[6])]
    qi3, qi = [], []

    def to_next(k, q):
        fsi[k] = make_i(k).astype(BF)
        q.append(send(fsi.at[k], fri.at[k], zp if k < 4 else zm))

    to_next(3, qi3)
    to_next(5, qi3)
    qt = []
    for k in far_w:
        part, rest = make_t(k)
        fst[k] = part.astype(BF)
        fsr[k, 0:72] = rest.astype(BF)
        qt.append(send(fst.at[k], frt.at[k], ws_at[k]))
        qt.append(send(fsr.at[k], frr.at[k], ws_at[k]))
    own_t, own_r = make_t(0)


    to_next(1, qi)
    to_next(7, qi)
    own_2, own_6 = make_i(2), make_i(6)
    own_i = make_i(0)
    for k, part, via, half in ((2, own_2, 3, 0), (6, own_6, 5, 1)):
        qi3[half].wait_recv()
        part = part + fri[via].astype(F32)
        qi4[half].wait_recv()
        if half == 0:
            fsi[k, H0] = (part[0:80] + fri[4, H0].astype(F32)).astype(BF)
            fsi[k, H1] = part[80:144].astype(BF)
        else:
            fsi[k, H0] = part[0:80].astype(BF)
            fsi[k, H1] = (part[80:144] + fri[4, H1].astype(F32)).astype(BF)
        qi.append(send(fsi.at[k], fri.at[k], zs_at[k]))
    for cp in qt:
        cp.wait_recv()
    for k in far_w:
        own_r = own_r + frr[k, 0:72].astype(F32)
        own_t = own_t + frt[k].astype(F32)
    own_t = jnp.concatenate([own_t, jnp.concatenate([own_r, pltpu.roll(own_r, 64, 1)], axis=0)], axis=1)
    low = lax.broadcasted_iota(jnp.int32, (16, 128), 1) < 64
    for k in range(8):
        part = own_t[18 * k:18 * k + 18]
        tail = jnp.concatenate([part[r:r + 1, i:i + 128] for r in (16, 17) for i in (0, 128, 256)]
                               + [jnp.zeros((2, 128), F32)], axis=0)
        tail = jnp.concatenate([pltpu.roll(tail, 64, 1), tail[0:2], tail[3:5], jnp.zeros((4, 128), F32)], axis=0)
        yst[k, :, 0:256] = part[0:16, 0:256].astype(BF)
        yst[k, :, 256:384] = jnp.where(low, part[0:16, 256:384], tail).astype(BF)
    qt = [send(yst.at[by_z(k)], yrt.at[k], zs_at[k]) for k in far_z]
    qi = regroup(qi, own_i, fri, (1, 7, 2, 6), far_w, ysi, yri, by_w, ws_at)
    oi_ref[:, 0:256] = last_sum(qi, ysi, yri, by_w)
    for cp in qt:
        cp.wait_recv()
    out = yst[by_z(0)].astype(F32)
    for k in range(1, 8):
        out = out + yrt[k].astype(F32)
    rest = out[:, 256:384]
    turned = pltpu.roll(rest, 64, 1)
    tail = [jnp.concatenate([jnp.where(low[0:1], turned[3 * r + i:3 * r + i + 1], rest[8 + 2 * r + i:9 + 2 * r + i])
                             for i in (0, 1)] + [turned[3 * r + 2:3 * r + 3]], axis=1) for r in (0, 1)]
    out = jnp.concatenate([out] + tail, axis=0)
    ot_ref[:, 0:256] = out[:, 0:256]
    oi_ref[:, 256:288] = out[:, 256:288]
    ot_ref[:, 256:288] = pltpu.roll(out[:, 256:384], 96, 1)[:, 0:32]
    for cp in started:
        if not any(cp is g for g in gone):
            cp.wait_send()


COPIES = 256


def local(image_feats, text_feats, image_proj, text_proj, log_temp, bias):
    total = image_feats.shape[0] * lax.axis_size("dp")
    vm = pltpu.VMEM
    res = pl.pallas_call(
        functools.partial(kernel, total),
        out_shape=jax.ShapeDtypeStruct((2, 18, 288), F32),
        in_specs=[pl.BlockSpec(memory_space=pl.ANY)] * 4
        + [pl.BlockSpec(memory_space=pltpu.SMEM)] * 2,
        out_specs=pl.BlockSpec(memory_space=vm),
        scratch_shapes=[
            vm((2, 256, 1152), BF),
            vm((2, 288, 1152), BF),
            vm((3, 8, 144, 256), BF),
            vm((2, 4, 64, 256), BF),
            vm((2, 4, 64, 256), BF),
            vm((4, 64, 128), BF),
            vm((4, 64, 128), BF),
            vm((2, 64, 1152), F32),
            vm((2, 64, 128), F32),
            vm((4, 2, 4, 32, 1152), BF),
            vm((8, 2, 64, 1152), BF),
            vm((1024, 1024), BF),
            vm((4, 2, 4, 32, 1152), F32),
            vm((8, 2, 64, 1152), F32),
            vm((3, 2, 4, 32, 1152), BF),
            vm((2, 2, 4, 32, 1152), BF),
            vm((2, 2, 32, 1152), BF),
            vm((2, 32, 1152), BF),
            vm((2, 4, 32, 1152), BF),
            vm((2, 4, 32, 1152), F32),
            vm((2, 3, 32, 1152), BF),
            vm((4, 2, 64, 1152), BF),
            vm((4, 2, 64, 1152), BF),
            vm((8, 64, 1152), BF),
            vm((8, 64, 1152), BF),
            vm((2, 4, 64, 256), BF),
            vm((2, 4, 64, 256), BF),
            vm((4, 64, 128), BF),
            vm((4, 64, 128), BF),
            vm((8, 144, 256), BF),
            vm((8, 144, 256), BF),
            vm((8, 144, 256), BF),
            vm((8, 144, 256), BF),
            vm((8, 80, 128), BF),
            vm((8, 80, 128), BF),
            vm((8, 16, 384), BF),
            vm((8, 16, 384), BF),
            vm((8, 16, 384), BF),
            vm((8, 16, 384), BF),
            pltpu.SemaphoreType.DMA((4,)),
            pltpu.SemaphoreType.DMA((COPIES,)),
            pltpu.SemaphoreType.DMA((COPIES,)),
        ],
        name="contrastive",
        compiler_params=pltpu.CompilerParams(
            collective_id=0, has_side_effects=True, vmem_limit_bytes=60 * 2**20
        ),
    )(image_feats, text_feats, image_proj.T, text_proj.T, log_temp, bias)
    return res[0], res[1]


def solution(mesh):
    placed = (P("dp", None), P("dp", None), P(None, "mp"), P(None, "mp"), P(), P())
    return jax.shard_map(
        local, mesh=mesh, in_specs=placed, out_specs=(P("dp", "mp"), P("dp", "mp")), check_vma=False
    )
```

```python
import functools

import jax
import jax.numpy as jnp
from jax import lax
from jax.experimental import pallas as pl
from jax.experimental.pallas import tpu as pltpu
from jax.sharding import PartitionSpec as P

MESH = pl.DeviceIdType.MESH
F32, BF = jnp.float32, jnp.bfloat16
PIECE = 64
POS = {4: 0, 0: 1, 3: 2, 5: 3, 2: 4, 6: 5, 1: 6, 7: 7}


def dot(a, b):
    return jnp.dot(a, b, preferred_element_type=F32)


def dot_nt(a, b):
    return lax.dot_general(a, b, (((1,), (1,)), ((), ())), preferred_element_type=F32)


def dot_tn(a, b):
    return lax.dot_general(a, b, (((0,), (0,)), ((), ())), preferred_element_type=F32)


def kernel(total, fi_hbm, ft_hbm, wi_hbm, wt_hbm, lt_ref, bs_ref, o_ref,
           feats, wts, featst, es, er, esr, err, unit, scal, img, txt, prob, gi, gt,
           gib, ra, ra2, r2, r4, sa, sab, gts, sibr, gtb, tr, zs, zr, zsr, zrr,
           fsi, fri, fst, frt, fsr, frr, ysi, yri, yst, yrt,
           lsem, ssem, rsem):
    oi_ref, ot_ref = o_ref.at[0], o_ref.at[1]
    dp, mp = lax.axis_index("dp"), lax.axis_index("mp")
    z, xl, y = dp // 8, (dp // 4) % 2, dp % 4
    c = mp % 2
    x = (mp // 2) * 2 + xl

    def dev(xx, yy, zz, cc):
        return (zz * 8 + (xx % 2) * 4 + yy, (xx // 2) * 2 + cc)

    xp, x2, xm = (dev((x + k) % 4, y, z, c) for k in (1, 2, 3))
    yp, y2, ym = (dev(x, (y + k) % 4, z, c) for k in (1, 2, 3))
    zs_at = [dev(x, y, (z + k) % 8, c) for k in range(8)]
    zp, zm = zs_at[1], zs_at[7]
    ws_at = [(z * 8 + ((xl + k // 4) % 2) * 4 + (y + k) % 4, mp) for k in range(8)]
    sib = (dp, (mp // 2) * 2 + (1 - c))
    mps = [(dp, (mp + k) % 4) for k in (1, 2, 3)]

    loads = []
    for k, (s, t) in enumerate(((fi_hbm, feats.at[0, 0:224]), (wi_hbm, wts.at[0]),
                                (ft_hbm, feats.at[1, 0:224]), (wt_hbm, wts.at[1]))):
        cp = pltpu.make_async_copy(s, t, lsem.at[k])
        cp.start()
        loads.append(cp)
    barrier = pltpu.get_barrier_semaphore()
    greeted = mps + [xp, xm] + zs_at[1:] + ws_at[1:4] + ws_at[5:]
    for d in greeted:
        pl.semaphore_signal(barrier, inc=1, device_id=d, device_id_type=MESH)

    feats[:, 224:256, :] = jnp.zeros((2, 32, 1152), BF)

    started, gone = [], []

    def send(src, dst, to):
        k = len(started)
        cp = pltpu.make_async_remote_copy(src_ref=src, dst_ref=dst, send_sem=ssem.at[k],
                                          recv_sem=rsem.at[k], device_id=to, device_id_type=MESH)
        cp.start()
        started.append(cp)
        return cp

    l0 = lax.broadcasted_iota(jnp.int32, (32, 128), 0)
    l1 = lax.broadcasted_iota(jnp.int32, (32, 128), 1)
    emb_in = []
    rests = []
    for m in (0, 1):
        loads[2 * m].wait()
        loads[2 * m + 1].wait()
        main = dot_nt(feats[m], wts[m, 0:256, :]).astype(BF)
        rest = dot_nt(feats[m], wts[m, 256:288, :]).astype(BF)
        place = (l1 == l0 + 32 * ((mp + 2 * m) % 4)).astype(F32).astype(BF)
        rests.append(dot(rest, place))
        for q in range(4):
            es[m, q] = main[64 * q:64 * q + 64]
        if m == 0:
            pl.semaphore_wait(barrier, len(greeted))
        else:
            rest = (rests[0] + rests[1]).astype(BF)
            for q in range(4):
                esr[q] = rest[64 * q:64 * q + 64]
            emb_in += [send(esr.at[(mp + k) % 4], err.at[mp], mps[k - 1]) for k in (1, 2, 3)]
            err[mp] = esr[mp]
        emb_in += [send(es.at[m, (mp + k) % 4], er.at[m, mp], mps[k - 1]) for k in (1, 2, 3)]
        er[m, mp] = es[m, mp]

    lane = lax.broadcasted_iota(jnp.int32, (64, 128), 1) // 32

    def normalize(m):
        rest = sum(jnp.where(lane == (q + 2 * m) % 4, err[q].astype(F32), 0.0) for q in range(4))
        if m:
            rest = pltpu.roll(rest, 64, 1)
        wide = jnp.concatenate([er[m, q].astype(F32) for q in range(4)] + [rest], axis=1)
        scale = lax.rsqrt(jnp.sum(wide * wide, axis=1, keepdims=True) + 1e-06)
        unit[m] = wide * scale
        scal[m] = jnp.broadcast_to(scale, (64, 128))
        return (wide * scale).astype(BF)

    for cp in emb_in:
        cp.wait_recv()
    A, B, A0, A1 = pl.ds(0, 32), pl.ds(32, 32), pl.ds(0, 16), pl.ds(16, 16)
    axis1 = ((xp, x2, xm), (yp, y2, ym))
    axis2 = ((yp, y2, ym), (xp, x2, xm))
    got = {}
    piece = normalize(0)
    img[0, 0, 0] = piece[0:32]
    img[0, 1, 0] = piece[32:64]
    for j in (1, 3, 2):
        for h in (0, 1):
            got[0, h, 4 - j] = send(img.at[0, h, 0], img.at[0, h, 4 - j], axis1[h][j - 1])

    def second(j):
        for h in (0, 1):
            got[3, h, j] = send(img.at[0, h, j], img.at[3, h, j], axis2[h][0])
            got[1, h, j] = send(img.at[0, h, j], img.at[1, h, j], axis2[h][2])

    def third(j):
        for h in (0, 1):
            got[3, h, j].wait_recv()
            got[4, h, j] = send(img.at[3, h, j, A0], img.at[2, h, j, A0], axis2[h][0])
            got[1, h, j].wait_recv()
            got[5, h, j] = send(img.at[1, h, j, A1], img.at[2, h, j, A1], axis2[h][2])

    second(0)
    txt[POS[0], 0] = normalize(1)
    tgot, sgot = {}, {}
    halves = (A, B)

    def text_send(src, dst, half, to):
        tgot[dst, half] = send(txt.at[POS[src], 0, halves[half]], txt.at[POS[dst], 0, halves[half]], to)

    def text_share(*slots):
        for k in slots:
            sgot[k] = send(txt.at[POS[k], 0], txt.at[POS[k], 1], sib)

    def text_shared(*slots):
        for k in slots:
            sgot[k].wait_recv()

    def text_hop(k, turns=(0, 1)):
        for turn in turns:
            for src, nxt, to, lead in ((8 - k, 7 - k, zp, 0), (k, k + 1, zm, 1)):
                half = (lead + turn) % 2
                tgot[src, half].wait_recv()
                if k < 3 or turn == 0:
                    text_send(src, nxt, half, to)
        if turns[-1]:
            text_share(8 - k, k)

    text_send(0, 7, 0, zp)
    text_send(0, 1, 1, zm)
    text_share(0)
    for cp in (tgot[7, 0], tgot[1, 1]):
        cp.wait_send()
        gone.append(cp)
    text_send(0, 7, 1, zp)
    text_send(0, 1, 0, zm)
    temp = jnp.exp(jnp.full((1, 1), lt_ref[0], F32))
    shift = jnp.full((1, 1), bs_ref[0], F32)
    gain = temp * (1.0 / total)

    def scores(k, n):
        at = pl.ds(2 * n, 2)
        logits = temp * dot_nt(img[k].reshape(256, 1152), txt[at].reshape(256, 1152)) + shift
        cols = pl.ds(pl.multiple_of(256 * n, 256), 256)
        prob[256 * k:256 * k + 256, cols] = (gain / (1.0 + jnp.exp(-logits))).astype(BF)
        return logits

    def some_scores(k, count):
        for i in range(count):
            scores(k, 3 - i)

    sent = {}

    def image_block(k):
        gi[k] = dot(prob[256 * k:256 * k + 256, :],
                    txt[...].reshape(1024, 1152)).reshape(2, 4, 32, 1152)

    def text_block(n):
        gt[2 * n:2 * n + 2] = dot_tn(prob[:, 256 * n:256 * n + 256],
                                     img[...].reshape(1024, 1152)).reshape(2, 2, 64, 1152)
        gts[n] = gt[2 * n:2 * n + 2, 1].astype(BF)
        return send(gts.at[n], sibr.at[n], sib)

    def text_own(k):
        return gt[POS[k], 0] + sibr[POS[k] // 2, POS[k] % 2].astype(F32)

    def text_on(k, half):
        at = halves[half]
        part = gt[POS[k], 0, at] + sibr[POS[k] // 2, POS[k] % 2, at].astype(F32)
        back_k = k + 1 if k < 4 else k - 1
        if k != 4 and (back_k != 4 or half == (0 if k == 3 else 1)):
            sent[back_k, half].wait_recv()
            part = part + tr[back_k, at].astype(F32)
        gtb[k, at] = part.astype(BF)
        to = zp if k < 4 or (k == 4 and half == 0) else zm
        sent[k, half] = send(gtb.at[k, at], tr.at[k, at], to)

    text_hop(1, (0,))
    for j in (1, 3):
        got[0, 0, j].wait_recv()
        got[0, 1, j].wait_recv()
        second(j)
    text_hop(1, (1,))
    got[0, 0, 2].wait_recv()
    got[0, 1, 2].wait_recv()
    second(2)
    text_hop(2, (0,))
    third(0)
    text_hop(2, (1,))
    text_shared(1, 7)
    scores(0, 3)
    third(1)
    third(3)
    text_hop(3, (0,))
    text_shared(2, 6)
    scores(0, 2)
    third(2)

    some_scores(1, 2)
    text_hop(3, (1,))
    some_scores(3, 2)
    text_shared(3, 5, 0)
    scores(1, 1)
    scores(3, 1)
    tgot[4, 0].wait_recv()
    tgot[4, 1].wait_recv()
    text_share(4)
    scores(0, 1)
    for j in range(4):
        for h in (0, 1):
            got[4, h, j].wait_recv()
            got[5, h, j].wait_recv()
    some_scores(2, 3)
    text_shared(4)
    for k in (2, 1, 3):
        scores(k, 0)
    logits = scores(0, 0)
    r0 = lax.broadcasted_iota(jnp.int32, (32, 128), 0)
    r1 = lax.broadcasted_iota(jnp.int32, (32, 128), 1)
    for h in (0, 1):
        own = logits[128 * h:128 * h + 32, 128:256]
        prob[128 * h:128 * h + 32, 128:256] = jnp.where(
            r1 == r0 + 32 * h, -gain / (1.0 + jnp.exp(own)), gain / (1.0 + jnp.exp(-own))).astype(BF)

    q0 = text_block(0)
    image_block(2)
    gib[1] = gi[2].astype(BF)
    pairs = (pl.ds(2, 2), pl.ds(0, 2))
    def two_away(p):
        return [[send(gib.at[1, h, p, A0], r4.at[h, p, A0], axis2[h][0]),
                 send(gib.at[1, h, p, A1], r4.at[h, p, A1], axis2[h][2])] for h in (0, 1)]

    q4 = [two_away(pairs[0])]
    q1 = text_block(1)
    q4.append(two_away(pairs[1]))
    q0.wait_recv()
    text_on(4, 0)
    text_on(4, 1)
    image_block(1)
    for h in (0, 1):
        gib[0, h, :, A1] = gi[1, h, :, A1].astype(BF)
    q1.wait_recv()
    text_on(3, 1)
    text_on(5, 0)
    image_block(3)
    for h in (0, 1):
        gib[2, h, :, A0] = gi[3, h, :, A0].astype(BF)
    qa = [[], []]

    def image_on(n):
        p = pairs[n]
        for h in (0, 1):
            for cp in q4[n][h]:
                cp.wait_recv()
            gib[0, h, p, A0] = (gi[1, h, p, A0] + r4[h, p, A0].astype(F32)).astype(BF)
            gib[2, h, p, A1] = (gi[3, h, p, A1] + r4[h, p, A1].astype(F32)).astype(BF)
            for i in (0, 1):
                qa[n].append(send(gib.at[2 * i, h, p], ra.at[i, h, p], axis2[h][2 * i]))

    qa2 = []

    def image_first(n):
        for cp in qa[n]:
            cp.wait_recv()
        for j in (2, 3) if n == 0 else (1, 0):
            for h in (0, 1):
                part = gi[0, h, j] + ra[0, h, j].astype(F32) + ra[1, h, j].astype(F32)
                if j == 2:
                    sab[h, 1] = part.astype(BF)
                    q2h.append(send(sab.at[h, 1, A0], r2.at[h, A0], axis1[h][0]))
                    q2h.append(send(sab.at[h, 1, A1], r2.at[h, A1], axis1[h][2]))
                else:
                    sa[h, j] = part

    q2h = []

    def image_last():
        for h in (0, 1):
            for cp in q2h[2 * h:2 * h + 2]:
                cp.wait_recv()
            sab[h, 0, A0] = (sa[h, 1, A0] + r2[h, A0].astype(F32)).astype(BF)
            sab[h, 0, A1] = sa[h, 1, A1].astype(BF)
            sab[h, 2, A0] = sa[h, 3, A0].astype(BF)
            sab[h, 2, A1] = (sa[h, 3, A1] + r2[h, A1].astype(F32)).astype(BF)
            qa2.append(send(sab.at[h, 0], ra2.at[h, 0], axis1[h][0]))
            qa2.append(send(sab.at[h, 2], ra2.at[h, 1], axis1[h][2]))

    image_on(0)
    q2 = text_block(2)
    text_on(3, 0)
    text_on(5, 1)
    image_on(1)
    q3 = text_block(3)
    image_block(0)
    q2.wait_recv()
    text_on(2, 1)
    text_on(6, 0)
    text_on(2, 0)
    text_on(6, 1)
    image_first(0)
    q3.wait_recv()
    text_on(1, 1)
    text_on(7, 0)
    image_first(1)
    text_on(1, 0)
    text_on(7, 1)
    image_last()

    def back(m, dx):
        inner = jnp.sum(unit[m] * dx, axis=1, keepdims=True)
        dz = scal[m][:, 0:1] * (dx - unit[m] * inner)
        for q in range(4):
            zs[m, q] = dz[:, 256 * q:256 * q + 256].astype(BF)
        zr[m, mp] = zs[m, mp]
        return dz[:, 1024:1152], [send(zs.at[m, (mp + k) % 4], zr.at[m, mp], mps[k - 1]) for k in (1, 2, 3)]

    for k in (1, 7):
        for half in (0, 1):
            sent[k, half].wait_recv()
    rest_t, z_in = back(1, text_own(0) + tr[1].astype(F32) + tr[7].astype(F32))
    for cp in qa2:
        cp.wait_recv()
    rest_i, q = back(0, jnp.concatenate(
        [sa[h, 0] + ra2[h, 0].astype(F32) + ra2[h, 1].astype(F32)
         for h in (0, 1)], axis=0))
    z_in += q
    for q in range(4):
        turned = [pltpu.roll(r, (128 - 32 * q + 32 * m) % 128, 1) for m, r in ((0, rest_i), (1, rest_t))]
        zsr[q] = jnp.where(lane == 0, turned[0], turned[1]).astype(BF)
    zrr[mp] = zsr[mp]
    z_in += [send(zsr.at[(mp + k) % 4], zrr.at[mp], mps[k - 1]) for k in (1, 2, 3)]

    wide_t = jnp.transpose(feats[0])
    for k in range(8):
        featst[0, k] = wide_t[144 * k:144 * k + 144]
    p0 = lax.broadcasted_iota(jnp.int32, (144, 1152), 0)
    at_z = p0 + 126 * ((p0 * 3641) >> 16)
    p1 = lax.broadcasted_iota(jnp.int32, (144, 1152), 1)

    def turn(w, _):
        turned = (p1 == at_z + 18 * w).astype(F32).astype(BF)
        featst[1, w] = dot_nt(turned, feats[1]).astype(BF)
        featst[2, w] = dot_nt(turned, feats[0]).astype(BF)
        return 0
    lax.fori_loop(0, 8, turn, 0)


    far_z, far_w = (4, 3, 5, 2, 6, 1, 7), (6, 2, 5, 7, 1, 3, 4)
    def by_z(k):
        return (z + k) % 8

    def by_w(k):
        return ((xl + k // 4) % 2) * 4 + (y + k) % 4

    def rows(ref):
        return jnp.concatenate([ref[q] for q in range(4)], axis=0)

    def regroup(q, own, rc, near, far, ys, yr, base, at):
        for cp in q:
            cp.wait_recv()
        for k in near:
            own = own + rc[k].astype(F32)
        cols = own.shape[1]
        for k in range(8):
            ys[k, :, 0:cols] = own[18 * k:18 * k + 16].astype(BF)
            tail = [own[18 * k + r:18 * k + r + 1, i:i + 128] for r in (16, 17) for i in range(0, cols, 128)]
            tail.append(jnp.zeros((16 - len(tail), 128), F32))
            ys[k, :, cols:cols + 128] = jnp.concatenate(tail, axis=0).astype(BF)
        return [send(ys.at[base(k)], yr.at[k], at[k]) for k in far]

    def last_sum(q, ys, yr, base):
        for cp in q:
            cp.wait_recv()
        out = ys[base(0)].astype(F32)
        for k in range(1, 8):
            out = out + yr[k].astype(F32)
        cols = out.shape[1] - 128
        n = cols // 128
        tail = [jnp.concatenate([out[r * n + i:r * n + i + 1, cols:] for i in range(n)], axis=1) for r in (0, 1)]
        return jnp.concatenate([out[:, 0:cols]] + tail, axis=0)

    for cp in z_in:
        cp.wait_recv()
    main_i, main_t = rows(zr.at[0]), rows(zr.at[1])
    rest = rows(zrr).astype(F32)
    which = lax.broadcasted_iota(jnp.int32, (256, 128), 1) // 32
    rest_i = jnp.where(which == 0, rest, 0.0).astype(BF)
    rest_t = jnp.where(which == 1, rest, 0.0).astype(BF)

    def make_t(k):
        a, b = featst[1, by_w(k)], featst[2, by_w(k)]
        rest = dot(a, rest_t) + dot(b, rest_i)
        return dot(a, main_t), rest[0:72] + pltpu.roll(rest[72:144], 64, 1)

    def make_i(k):
        return dot(featst[0, by_z(k)], main_i)

    H0, H1 = pl.ds(0, 80), pl.ds(80, 64)
    fsi[4] = make_i(4).astype(BF)
    qi4 = [send(fsi.at[4, H0], fri.at[4, H0], zs_at[2]), send(fsi.at[4, H1], fri.at[4, H1], zs_at[6])]
    qi3, qi = [], []

    def to_next(k, q):
        fsi[k] = make_i(k).astype(BF)
        q.append(send(fsi.at[k], fri.at[k], zp if k < 4 else zm))

    to_next(3, qi3)
    to_next(5, qi3)
    qt = []
    for k in far_w:
        part, rest = make_t(k)
        fst[k] = part.astype(BF)
        fsr[k] = jnp.concatenate([rest, jnp.zeros((8, 128), F32)], axis=0).astype(BF)
        qt.append(send(fst.at[k], frt.at[k], ws_at[k]))
        qt.append(send(fsr.at[k], frr.at[k], ws_at[k]))
    own_t, own_r = make_t(0)


    to_next(1, qi)
    to_next(7, qi)
    own_2, own_6 = make_i(2), make_i(6)
    own_i = make_i(0)
    for k, part, via, half in ((2, own_2, 3, 0), (6, own_6, 5, 1)):
        qi3[half].wait_recv()
        part = part + fri[via].astype(F32)
        qi4[half].wait_recv()
        if half == 0:
            fsi[k, H0] = (part[0:80] + fri[4, H0].astype(F32)).astype(BF)
            fsi[k, H1] = part[80:144].astype(BF)
        else:
            fsi[k, H0] = part[0:80].astype(BF)
            fsi[k, H1] = (part[80:144] + fri[4, H1].astype(F32)).astype(BF)
        qi.append(send(fsi.at[k], fri.at[k], zs_at[k]))
    for cp in qt:
        cp.wait_recv()
    for k in far_w:
        own_r = own_r + frr[k].astype(F32)[0:72]
        own_t = own_t + frt[k].astype(F32)
    own_t = jnp.concatenate([own_t, jnp.concatenate([own_r, pltpu.roll(own_r, 64, 1)], axis=0)], axis=1)
    low = lax.broadcasted_iota(jnp.int32, (16, 128), 1) < 64
    for k in range(8):
        part = own_t[18 * k:18 * k + 18]
        tail = jnp.concatenate([part[r:r + 1, i:i + 128] for r in (16, 17) for i in (0, 128, 256)]
                               + [jnp.zeros((2, 128), F32)], axis=0)
        tail = jnp.concatenate([pltpu.roll(tail, 64, 1), tail[0:2], tail[3:5], jnp.zeros((4, 128), F32)], axis=0)
        yst[k, :, 0:256] = part[0:16, 0:256].astype(BF)
        yst[k, :, 256:384] = jnp.where(low, part[0:16, 256:384], tail).astype(BF)
    qt = [send(yst.at[by_z(k)], yrt.at[k], zs_at[k]) for k in far_z]
    qi = regroup(qi, own_i, fri, (1, 7, 2, 6), far_w, ysi, yri, by_w, ws_at)
    oi_ref[:, 0:256] = last_sum(qi, ysi, yri, by_w)
    for cp in qt:
        cp.wait_recv()
    out = yst[by_z(0)].astype(F32)
    for k in range(1, 8):
        out = out + yrt[k].astype(F32)
    rest = out[:, 256:384]
    turned = pltpu.roll(rest, 64, 1)
    tail = [jnp.concatenate([jnp.where(low[0:1], turned[3 * r + i:3 * r + i + 1], rest[8 + 2 * r + i:9 + 2 * r + i])
                             for i in (0, 1)] + [turned[3 * r + 2:3 * r + 3]], axis=1) for r in (0, 1)]
    out = jnp.concatenate([out] + tail, axis=0)
    ot_ref[:, 0:256] = out[:, 0:256]
    oi_ref[:, 256:288] = out[:, 256:288]
    ot_ref[:, 256:288] = pltpu.roll(out[:, 256:384], 96, 1)[:, 0:32]
    for cp in started:
        if not any(cp is g for g in gone):
            cp.wait_send()


COPIES = 256


def local(image_feats, text_feats, image_proj, text_proj, log_temp, bias):
    total = image_feats.shape[0] * lax.axis_size("dp")
    vm = pltpu.VMEM
    res = pl.pallas_call(
        functools.partial(kernel, total),
        out_shape=jax.ShapeDtypeStruct((2, 18, 288), F32),
        in_specs=[pl.BlockSpec(memory_space=pl.ANY)] * 4
        + [pl.BlockSpec(memory_space=pltpu.SMEM)] * 2,
        out_specs=pl.BlockSpec(memory_space=vm),
        scratch_shapes=[
            vm((2, 256, 1152), BF),
            vm((2, 288, 1152), BF),
            vm((3, 8, 144, 256), BF),
            vm((2, 4, 64, 256), BF),
            vm((2, 4, 64, 256), BF),
            vm((4, 64, 128), BF),
            vm((4, 64, 128), BF),
            vm((2, 64, 1152), F32),
            vm((2, 64, 128), F32),
            vm((4, 2, 4, 32, 1152), BF),
            vm((8, 2, 64, 1152), BF),
            vm((1024, 1024), BF),
            vm((4, 2, 4, 32, 1152), F32),
            vm((8, 2, 64, 1152), F32),
            vm((3, 2, 4, 32, 1152), BF),
            vm((2, 2, 4, 32, 1152), BF),
            vm((2, 2, 32, 1152), BF),
            vm((2, 32, 1152), BF),
            vm((2, 4, 32, 1152), BF),
            vm((2, 4, 32, 1152), F32),
            vm((2, 3, 32, 1152), BF),
            vm((4, 2, 64, 1152), BF),
            vm((4, 2, 64, 1152), BF),
            vm((8, 64, 1152), BF),
            vm((8, 64, 1152), BF),
            vm((2, 4, 64, 256), BF),
            vm((2, 4, 64, 256), BF),
            vm((4, 64, 128), BF),
            vm((4, 64, 128), BF),
            vm((8, 144, 256), BF),
            vm((8, 144, 256), BF),
            vm((8, 144, 256), BF),
            vm((8, 144, 256), BF),
            vm((8, 80, 128), BF),
            vm((8, 80, 128), BF),
            vm((8, 16, 384), BF),
            vm((8, 16, 384), BF),
            vm((8, 16, 384), BF),
            vm((8, 16, 384), BF),
            pltpu.SemaphoreType.DMA((4,)),
            pltpu.SemaphoreType.DMA((COPIES,)),
            pltpu.SemaphoreType.DMA((COPIES,)),
        ],
        name="contrastive",
        compiler_params=pltpu.CompilerParams(
            collective_id=0, has_side_effects=True, vmem_limit_bytes=60 * 2**20
        ),
    )(image_feats, text_feats, image_proj.T, text_proj.T, log_temp, bias)
    return res[0], res[1]


def solution(mesh):
    placed = (P("dp", None), P("dp", None), P(None, "mp"), P(None, "mp"), P(), P())
    return jax.shard_map(
        local, mesh=mesh, in_specs=placed, out_specs=(P("dp", "mp"), P("dp", "mp")), check_vma=False
    )
```

```python
import functools

import jax
import jax.numpy as jnp
from jax import lax
from jax.experimental import pallas as pl
from jax.experimental.pallas import tpu as pltpu
from jax.sharding import PartitionSpec as P

MESH = pl.DeviceIdType.MESH
F32, BF = jnp.float32, jnp.bfloat16
PIECE = 64
POS = {4: 0, 0: 1, 3: 2, 5: 3, 2: 4, 6: 5, 1: 6, 7: 7}


def dot(a, b):
    return jnp.dot(a, b, preferred_element_type=F32)


def dot_nt(a, b):
    return lax.dot_general(a, b, (((1,), (1,)), ((), ())), preferred_element_type=F32)


def dot_tn(a, b):
    return lax.dot_general(a, b, (((0,), (0,)), ((), ())), preferred_element_type=F32)


def kernel(total, fi_hbm, ft_hbm, wi_hbm, wt_hbm, lt_ref, bs_ref, o_ref,
           feats, wts, featst, es, er, esr, err, unit, scal, img, txt, prob, gi, gt,
           gib, ra, ra2, r2, r4, sa, sab, gts, sibr, gtb, tr, zs, zr, zsr, zrr,
           fsi, fri, fst, frt, fsr, frr, ysi, yri, yst, yrt,
           lsem, ssem, rsem):
    oi_ref, ot_ref = o_ref.at[0], o_ref.at[1]
    dp, mp = lax.axis_index("dp"), lax.axis_index("mp")
    z, xl, y = dp // 8, (dp // 4) % 2, dp % 4
    c = mp % 2
    x = (mp // 2) * 2 + xl

    def dev(xx, yy, zz, cc):
        return (zz * 8 + (xx % 2) * 4 + yy, (xx // 2) * 2 + cc)

    xp, x2, xm = (dev((x + k) % 4, y, z, c) for k in (1, 2, 3))
    yp, y2, ym = (dev(x, (y + k) % 4, z, c) for k in (1, 2, 3))
    zs_at = [dev(x, y, (z + k) % 8, c) for k in range(8)]
    zp, zm = zs_at[1], zs_at[7]
    ws_at = [(z * 8 + ((xl + k // 4) % 2) * 4 + (y + k) % 4, mp) for k in range(8)]
    sib = (dp, (mp // 2) * 2 + (1 - c))
    mps = [(dp, (mp + k) % 4) for k in (1, 2, 3)]

    loads = []
    for k, (s, t) in enumerate(((fi_hbm, feats.at[0, 0:224]), (wi_hbm, wts.at[0]),
                                (ft_hbm, feats.at[1, 0:224]), (wt_hbm, wts.at[1]))):
        cp = pltpu.make_async_copy(s, t, lsem.at[k])
        cp.start()
        loads.append(cp)
    barrier = pltpu.get_barrier_semaphore()
    greeted = mps + [xp, xm] + zs_at[1:] + ws_at[1:4] + ws_at[5:]
    for d in greeted:
        pl.semaphore_signal(barrier, inc=1, device_id=d, device_id_type=MESH)

    feats[:, 224:256, :] = jnp.zeros((2, 32, 1152), BF)

    started, gone = [], []

    def send(src, dst, to):
        k = len(started)
        cp = pltpu.make_async_remote_copy(src_ref=src, dst_ref=dst, send_sem=ssem.at[k],
                                          recv_sem=rsem.at[k], device_id=to, device_id_type=MESH)
        cp.start()
        started.append(cp)
        return cp

    l0 = lax.broadcasted_iota(jnp.int32, (32, 128), 0)
    l1 = lax.broadcasted_iota(jnp.int32, (32, 128), 1)
    emb_in = []
    rests = []
    for m in (0, 1):
        loads[2 * m].wait()
        loads[2 * m + 1].wait()
        main = dot_nt(feats[m], wts[m, 0:256, :]).astype(BF)
        rest = dot_nt(feats[m], wts[m, 256:288, :]).astype(BF)
        place = (l1 == l0 + 32 * ((mp + 2 * m) % 4)).astype(F32).astype(BF)
        rests.append(dot(rest, place))
        for q in range(4):
            es[m, q] = main[64 * q:64 * q + 64]
        if m == 0:
            pl.semaphore_wait(barrier, len(greeted))
        else:
            rest = (rests[0] + rests[1]).astype(BF)
            for q in range(4):
                esr[q] = rest[64 * q:64 * q + 64]
            emb_in += [send(esr.at[(mp + k) % 4], err.at[mp], mps[k - 1]) for k in (1, 2, 3)]
            err[mp] = esr[mp]
        emb_in += [send(es.at[m, (mp + k) % 4], er.at[m, mp], mps[k - 1]) for k in (1, 2, 3)]
        er[m, mp] = es[m, mp]

    lane = lax.broadcasted_iota(jnp.int32, (64, 128), 1) // 32

    def normalize(m):
        rest = sum(jnp.where(lane == (q + 2 * m) % 4, err[q].astype(F32), 0.0) for q in range(4))
        if m:
            rest = pltpu.roll(rest, 64, 1)
        wide = jnp.concatenate([er[m, q].astype(F32) for q in range(4)] + [rest], axis=1)
        scale = lax.rsqrt(jnp.sum(wide * wide, axis=1, keepdims=True) + 1e-06)
        unit[m] = wide * scale
        scal[m] = jnp.broadcast_to(scale, (64, 128))
        return (wide * scale).astype(BF)

    for cp in emb_in:
        cp.wait_recv()
    A, B, A0, A1 = pl.ds(0, 32), pl.ds(32, 32), pl.ds(0, 16), pl.ds(16, 16)
    axis1 = ((xp, x2, xm), (yp, y2, ym))
    axis2 = ((yp, y2, ym), (xp, x2, xm))
    got = {}
    piece = normalize(0)
    img[0, 0, 0] = piece[0:32]
    img[0, 1, 0] = piece[32:64]
    for j in (1, 3, 2):
        for h in (0, 1):
            got[0, h, 4 - j] = send(img.at[0, h, 0], img.at[0, h, 4 - j], axis1[h][j - 1])

    def second(j):
        for h in (0, 1):
            got[3, h, j] = send(img.at[0, h, j], img.at[3, h, j], axis2[h][0])
            got[1, h, j] = send(img.at[0, h, j], img.at[1, h, j], axis2[h][2])

    def third(j):
        for h in (0, 1):
            got[3, h, j].wait_recv()
            got[4, h, j] = send(img.at[3, h, j, A0], img.at[2, h, j, A0], axis2[h][0])
            got[1, h, j].wait_recv()
            got[5, h, j] = send(img.at[1, h, j, A1], img.at[2, h, j, A1], axis2[h][2])

    second(0)
    txt[POS[0], 0] = normalize(1)
    tgot, sgot = {}, {}
    halves = (A, B)

    def text_send(src, dst, half, to):
        tgot[dst, half] = send(txt.at[POS[src], 0, halves[half]], txt.at[POS[dst], 0, halves[half]], to)

    def text_share(*slots):
        for k in slots:
            sgot[k] = send(txt.at[POS[k], 0], txt.at[POS[k], 1], sib)

    def text_shared(*slots):
        for k in slots:
            sgot[k].wait_recv()

    def text_hop(k, turns=(0, 1)):
        for turn in turns:
            for src, nxt, to, lead in ((8 - k, 7 - k, zp, 0), (k, k + 1, zm, 1)):
                half = (lead + turn) % 2
                tgot[src, half].wait_recv()
                if k < 3 or turn == 0:
                    text_send(src, nxt, half, to)
        if turns[-1]:
            text_share(8 - k, k)

    text_send(0, 7, 0, zp)
    text_send(0, 1, 1, zm)
    text_share(0)
    for cp in (tgot[7, 0], tgot[1, 1]):
        cp.wait_send()
        gone.append(cp)
    text_send(0, 7, 1, zp)
    text_send(0, 1, 0, zm)
    temp = jnp.exp(jnp.full((1, 1), lt_ref[0], F32))
    shift = jnp.full((1, 1), bs_ref[0], F32)
    gain = temp * (1.0 / total)

    def scores(k, n):
        at = pl.ds(2 * n, 2)
        logits = temp * dot_nt(img[k].reshape(256, 1152), txt[at].reshape(256, 1152)) + shift
        cols = pl.ds(pl.multiple_of(256 * n, 256), 256)
        prob[256 * k:256 * k + 256, cols] = (gain / (1.0 + jnp.exp(-logits))).astype(BF)
        return logits

    def some_scores(k, count):
        for i in range(count):
            scores(k, 3 - i)

    sent = {}

    def image_block(k):
        gi[k] = dot(prob[256 * k:256 * k + 256, :],
                    txt[...].reshape(1024, 1152)).reshape(2, 4, 32, 1152)

    def text_block(n):
        gt[2 * n:2 * n + 2] = dot_tn(prob[:, 256 * n:256 * n + 256],
                                     img[...].reshape(1024, 1152)).reshape(2, 2, 64, 1152)
        gts[n] = gt[2 * n:2 * n + 2, 1].astype(BF)
        return send(gts.at[n], sibr.at[n], sib)

    def text_own(k):
        return gt[POS[k], 0] + sibr[POS[k] // 2, POS[k] % 2].astype(F32)

    def text_on(k, half):
        at = halves[half]
        part = gt[POS[k], 0, at] + sibr[POS[k] // 2, POS[k] % 2, at].astype(F32)
        back_k = k + 1 if k < 4 else k - 1
        if k != 4 and (back_k != 4 or half == (0 if k == 3 else 1)):
            sent[back_k, half].wait_recv()
            part = part + tr[back_k, at].astype(F32)
        gtb[k, at] = part.astype(BF)
        to = zp if k < 4 or (k == 4 and half == 0) else zm
        sent[k, half] = send(gtb.at[k, at], tr.at[k, at], to)

    text_hop(1, (0,))
    for j in (1, 3):
        got[0, 0, j].wait_recv()
        got[0, 1, j].wait_recv()
        second(j)
    text_hop(1, (1,))
    got[0, 0, 2].wait_recv()
    got[0, 1, 2].wait_recv()
    second(2)
    text_hop(2, (0,))
    third(0)
    text_hop(2, (1,))
    text_shared(1, 7)
    scores(0, 3)
    third(1)
    third(3)
    text_hop(3, (0,))
    text_shared(2, 6)
    scores(0, 2)
    third(2)

    some_scores(1, 2)
    text_hop(3, (1,))
    some_scores(3, 2)
    text_shared(3, 5, 0)
    scores(1, 1)
    scores(3, 1)
    tgot[4, 0].wait_recv()
    tgot[4, 1].wait_recv()
    text_share(4)
    scores(0, 1)
    for j in range(4):
        for h in (0, 1):
            got[4, h, j].wait_recv()
            got[5, h, j].wait_recv()
    some_scores(2, 3)
    text_shared(4)
    for k in (2, 1, 3):
        scores(k, 0)
    logits = scores(0, 0)
    r0 = lax.broadcasted_iota(jnp.int32, (32, 128), 0)
    r1 = lax.broadcasted_iota(jnp.int32, (32, 128), 1)
    for h in (0, 1):
        own = logits[128 * h:128 * h + 32, 128:256]
        prob[128 * h:128 * h + 32, 128:256] = jnp.where(
            r1 == r0 + 32 * h, -gain / (1.0 + jnp.exp(own)), gain / (1.0 + jnp.exp(-own))).astype(BF)

    q0 = text_block(0)
    image_block(2)
    gib[1] = gi[2].astype(BF)
    pairs = (pl.ds(2, 2), pl.ds(0, 2))
    def two_away(p):
        return [[send(gib.at[1, h, p, A0], r4.at[h, p, A0], axis2[h][0]),
                 send(gib.at[1, h, p, A1], r4.at[h, p, A1], axis2[h][2])] for h in (0, 1)]

    q4 = [two_away(pairs[0])]
    q1 = text_block(1)
    q4.append(two_away(pairs[1]))
    q0.wait_recv()
    text_on(4, 0)
    text_on(4, 1)
    image_block(1)
    for h in (0, 1):
        gib[0, h, :, A1] = gi[1, h, :, A1].astype(BF)
    q1.wait_recv()
    text_on(3, 1)
    text_on(5, 0)
    image_block(3)
    for h in (0, 1):
        gib[2, h, :, A0] = gi[3, h, :, A0].astype(BF)
    qa = [[], []]

    def image_on(n):
        p = pairs[n]
        for h in (0, 1):
            for cp in q4[n][h]:
                cp.wait_recv()
            gib[0, h, p, A0] = (gi[1, h, p, A0] + r4[h, p, A0].astype(F32)).astype(BF)
            gib[2, h, p, A1] = (gi[3, h, p, A1] + r4[h, p, A1].astype(F32)).astype(BF)
            for i in (0, 1):
                qa[n].append(send(gib.at[2 * i, h, p], ra.at[i, h, p], axis2[h][2 * i]))

    qa2 = []

    def image_first(n):
        for cp in qa[n]:
            cp.wait_recv()
        for j in (2, 3) if n == 0 else (1, 0):
            for h in (0, 1):
                part = gi[0, h, j] + ra[0, h, j].astype(F32) + ra[1, h, j].astype(F32)
                if j == 2:
                    sab[h, 1] = part.astype(BF)
                    q2h.append(send(sab.at[h, 1, A0], r2.at[h, A0], axis1[h][0]))
                    q2h.append(send(sab.at[h, 1, A1], r2.at[h, A1], axis1[h][2]))
                else:
                    sa[h, j] = part

    q2h = []

    def image_last():
        for h in (0, 1):
            for cp in q2h[2 * h:2 * h + 2]:
                cp.wait_recv()
            sab[h, 0, A0] = (sa[h, 1, A0] + r2[h, A0].astype(F32)).astype(BF)
            sab[h, 0, A1] = sa[h, 1, A1].astype(BF)
            sab[h, 2, A0] = sa[h, 3, A0].astype(BF)
            sab[h, 2, A1] = (sa[h, 3, A1] + r2[h, A1].astype(F32)).astype(BF)
            qa2.append(send(sab.at[h, 0], ra2.at[h, 0], axis1[h][0]))
            qa2.append(send(sab.at[h, 2], ra2.at[h, 1], axis1[h][2]))

    image_on(0)
    q2 = text_block(2)
    text_on(3, 0)
    text_on(5, 1)
    image_on(1)
    q3 = text_block(3)
    image_block(0)
    q2.wait_recv()
    text_on(2, 1)
    text_on(6, 0)
    text_on(2, 0)
    text_on(6, 1)
    image_first(0)
    q3.wait_recv()
    text_on(1, 1)
    text_on(7, 0)
    image_first(1)
    text_on(1, 0)
    text_on(7, 1)
    image_last()

    def back(m, dx):
        inner = jnp.sum(unit[m] * dx, axis=1, keepdims=True)
        dz = scal[m][:, 0:1] * (dx - unit[m] * inner)
        for q in range(4):
            zs[m, q] = dz[:, 256 * q:256 * q + 256].astype(BF)
        zr[m, mp] = zs[m, mp]
        return dz[:, 1024:1152], [send(zs.at[m, (mp + k) % 4], zr.at[m, mp], mps[k - 1]) for k in (1, 2, 3)]

    for k in (1, 7):
        for half in (0, 1):
            sent[k, half].wait_recv()
    rest_t, z_in = back(1, text_own(0) + tr[1].astype(F32) + tr[7].astype(F32))
    for cp in qa2:
        cp.wait_recv()
    rest_i, q = back(0, jnp.concatenate(
        [sa[h, 0] + ra2[h, 0].astype(F32) + ra2[h, 1].astype(F32)
         for h in (0, 1)], axis=0))
    z_in += q
    for q in range(4):
        turned = [pltpu.roll(r, (128 - 32 * q + 32 * m) % 128, 1) for m, r in ((0, rest_i), (1, rest_t))]
        zsr[q] = jnp.where(lane == 0, turned[0], turned[1]).astype(BF)
    zrr[mp] = zsr[mp]
    z_in += [send(zsr.at[(mp + k) % 4], zrr.at[mp], mps[k - 1]) for k in (1, 2, 3)]

    wide_t = jnp.transpose(feats[0])
    for k in range(8):
        featst[0, k] = wide_t[144 * k:144 * k + 144]
    p0 = lax.broadcasted_iota(jnp.int32, (144, 1152), 0)
    at_z = p0 + 126 * ((p0 * 3641) >> 16)
    p1 = lax.broadcasted_iota(jnp.int32, (144, 1152), 1)

    def turn(w, _):
        turned = (p1 == at_z + 18 * w).astype(F32).astype(BF)
        featst[1, w] = dot_nt(turned, feats[1]).astype(BF)
        featst[2, w] = dot_nt(turned, feats[0]).astype(BF)
        return 0
    lax.fori_loop(0, 8, turn, 0)


    far_z, far_w = (4, 3, 5, 2, 6, 1, 7), (6, 2, 5, 7, 1, 3, 4)
    def by_z(k):
        return (z + k) % 8

    def by_w(k):
        return ((xl + k // 4) % 2) * 4 + (y + k) % 4

    def rows(ref):
        return jnp.concatenate([ref[q] for q in range(4)], axis=0)

    def regroup(q, own, rc, near, far, ys, yr, base, at):
        for cp in q:
            cp.wait_recv()
        for k in near:
            own = own + rc[k].astype(F32)
        cols = own.shape[1]
        for k in range(8):
            ys[k, :, 0:cols] = own[18 * k:18 * k + 16].astype(BF)
            tail = [own[18 * k + r:18 * k + r + 1, i:i + 128] for r in (16, 17) for i in range(0, cols, 128)]
            tail.append(jnp.zeros((16 - len(tail), 128), F32))
            ys[k, :, cols:cols + 128] = jnp.concatenate(tail, axis=0).astype(BF)
        return [send(ys.at[base(k)], yr.at[k], at[k]) for k in far]

    def last_sum(q, ys, yr, base):
        for cp in q:
            cp.wait_recv()
        out = ys[base(0)].astype(F32)
        for k in range(1, 8):
            out = out + yr[k].astype(F32)
        cols = out.shape[1] - 128
        n = cols // 128
        tail = [jnp.concatenate([out[r * n + i:r * n + i + 1, cols:] for i in range(n)], axis=1) for r in (0, 1)]
        return jnp.concatenate([out[:, 0:cols]] + tail, axis=0)

    for cp in z_in:
        cp.wait_recv()
    main_i, main_t = rows(zr.at[0]), rows(zr.at[1])
    rest = rows(zrr).astype(F32)
    which = lax.broadcasted_iota(jnp.int32, (256, 128), 1) // 32
    rest_i = jnp.where(which == 0, rest, 0.0).astype(BF)
    rest_t = jnp.where(which == 1, rest, 0.0).astype(BF)

    def make_t(k):
        return dot(featst[1, by_w(k)], main_t)

    def make_r(k):
        rest = dot(featst[1, by_w(k)], rest_t) + dot(featst[2, by_w(k)], rest_i)
        return rest[0:72] + pltpu.roll(rest[72:144], 64, 1)

    def make_i(k):
        return dot(featst[0, by_z(k)], main_i)

    H0, H1 = pl.ds(0, 80), pl.ds(80, 64)
    fsi[4] = make_i(4).astype(BF)
    qi4 = [send(fsi.at[4, H0], fri.at[4, H0], zs_at[2]), send(fsi.at[4, H1], fri.at[4, H1], zs_at[6])]
    qi3, qi = [], []

    def to_next(k, q):
        fsi[k] = make_i(k).astype(BF)
        q.append(send(fsi.at[k], fri.at[k], zp if k < 4 else zm))

    to_next(3, qi3)
    to_next(5, qi3)
    qt = []
    for k in (6, 5, 7, 4, 2, 1, 3):
        fst[k] = make_t(k).astype(BF)
        qt.append(send(fst.at[k], frt.at[k], ws_at[k]))
    for k in (6, 5, 7, 4, 2, 1, 3):
        fsr[k] = jnp.concatenate([make_r(k), jnp.zeros((8, 128), F32)], axis=0).astype(BF)
        qt.append(send(fsr.at[k], frr.at[k], ws_at[k]))
    own_t, own_r = make_t(0), make_r(0)


    to_next(1, qi)
    to_next(7, qi)
    own_2, own_6 = make_i(2), make_i(6)
    own_i = make_i(0)
    for k, part, via, half in ((2, own_2, 3, 0), (6, own_6, 5, 1)):
        qi3[half].wait_recv()
        part = part + fri[via].astype(F32)
        qi4[half].wait_recv()
        if half == 0:
            fsi[k, H0] = (part[0:80] + fri[4, H0].astype(F32)).astype(BF)
            fsi[k, H1] = part[80:144].astype(BF)
        else:
            fsi[k, H0] = part[0:80].astype(BF)
            fsi[k, H1] = (part[80:144] + fri[4, H1].astype(F32)).astype(BF)
        qi.append(send(fsi.at[k], fri.at[k], zs_at[k]))
    for cp in qt:
        cp.wait_recv()
    for k in far_w:
        own_r = own_r + frr[k].astype(F32)[0:72]
        own_t = own_t + frt[k].astype(F32)
    own_t = jnp.concatenate([own_t, jnp.concatenate([own_r, pltpu.roll(own_r, 64, 1)], axis=0)], axis=1)
    low = lax.broadcasted_iota(jnp.int32, (16, 128), 1) < 64
    for k in range(8):
        part = own_t[18 * k:18 * k + 18]
        tail = jnp.concatenate([part[r:r + 1, i:i + 128] for r in (16, 17) for i in (0, 128, 256)]
                               + [jnp.zeros((2, 128), F32)], axis=0)
        tail = jnp.concatenate([pltpu.roll(tail, 64, 1), tail[0:2], tail[3:5], jnp.zeros((4, 128), F32)], axis=0)
        yst[k, :, 0:256] = part[0:16, 0:256].astype(BF)
        yst[k, :, 256:384] = jnp.where(low, part[0:16, 256:384], tail).astype(BF)
    qt = [send(yst.at[by_z(k)], yrt.at[k], zs_at[k]) for k in far_z]
    qi = regroup(qi, own_i, fri, (1, 7, 2, 6), far_w, ysi, yri, by_w, ws_at)
    oi_ref[:, 0:256] = last_sum(qi, ysi, yri, by_w)
    for cp in qt:
        cp.wait_recv()
    out = yst[by_z(0)].astype(F32)
    for k in range(1, 8):
        out = out + yrt[k].astype(F32)
    rest = out[:, 256:384]
    turned = pltpu.roll(rest, 64, 1)
    tail = [jnp.concatenate([jnp.where(low[0:1], turned[3 * r + i:3 * r + i + 1], rest[8 + 2 * r + i:9 + 2 * r + i])
                             for i in (0, 1)] + [turned[3 * r + 2:3 * r + 3]], axis=1) for r in (0, 1)]
    out = jnp.concatenate([out] + tail, axis=0)
    ot_ref[:, 0:256] = out[:, 0:256]
    oi_ref[:, 256:288] = out[:, 256:288]
    ot_ref[:, 256:288] = pltpu.roll(out[:, 256:384], 96, 1)[:, 0:32]
    for cp in started:
        if not any(cp is g for g in gone):
            cp.wait_send()


COPIES = 256


def local(image_feats, text_feats, image_proj, text_proj, log_temp, bias):
    total = image_feats.shape[0] * lax.axis_size("dp")
    vm = pltpu.VMEM
    res = pl.pallas_call(
        functools.partial(kernel, total),
        out_shape=jax.ShapeDtypeStruct((2, 18, 288), F32),
        in_specs=[pl.BlockSpec(memory_space=pl.ANY)] * 4
        + [pl.BlockSpec(memory_space=pltpu.SMEM)] * 2,
        out_specs=pl.BlockSpec(memory_space=vm),
        scratch_shapes=[
            vm((2, 256, 1152), BF),
            vm((2, 288, 1152), BF),
            vm((3, 8, 144, 256), BF),
            vm((2, 4, 64, 256), BF),
            vm((2, 4, 64, 256), BF),
            vm((4, 64, 128), BF),
            vm((4, 64, 128), BF),
            vm((2, 64, 1152), F32),
            vm((2, 64, 128), F32),
            vm((4, 2, 4, 32, 1152), BF),
            vm((8, 2, 64, 1152), BF),
            vm((1024, 1024), BF),
            vm((4, 2, 4, 32, 1152), F32),
            vm((8, 2, 64, 1152), F32),
            vm((3, 2, 4, 32, 1152), BF),
            vm((2, 2, 4, 32, 1152), BF),
            vm((2, 2, 32, 1152), BF),
            vm((2, 32, 1152), BF),
            vm((2, 4, 32, 1152), BF),
            vm((2, 4, 32, 1152), F32),
            vm((2, 3, 32, 1152), BF),
            vm((4, 2, 64, 1152), BF),
            vm((4, 2, 64, 1152), BF),
            vm((8, 64, 1152), BF),
            vm((8, 64, 1152), BF),
            vm((2, 4, 64, 256), BF),
            vm((2, 4, 64, 256), BF),
            vm((4, 64, 128), BF),
            vm((4, 64, 128), BF),
            vm((8, 144, 256), BF),
            vm((8, 144, 256), BF),
            vm((8, 144, 256), BF),
            vm((8, 144, 256), BF),
            vm((8, 80, 128), BF),
            vm((8, 80, 128), BF),
            vm((8, 16, 384), BF),
            vm((8, 16, 384), BF),
            vm((8, 16, 384), BF),
            vm((8, 16, 384), BF),
            pltpu.SemaphoreType.DMA((4,)),
            pltpu.SemaphoreType.DMA((COPIES,)),
            pltpu.SemaphoreType.DMA((COPIES,)),
        ],
        name="contrastive",
        compiler_params=pltpu.CompilerParams(
            collective_id=0, has_side_effects=True, vmem_limit_bytes=60 * 2**20
        ),
    )(image_feats, text_feats, image_proj.T, text_proj.T, log_temp, bias)
    return res[0], res[1]


def solution(mesh):
    placed = (P("dp", None), P("dp", None), P(None, "mp"), P(None, "mp"), P(), P())
    return jax.shard_map(
        local, mesh=mesh, in_specs=placed, out_specs=(P("dp", "mp"), P("dp", "mp")), check_vma=False
    )
```
